32 devices in a mesh: mol: 2 (over y), pair: 4 (over z), aux: 4 (over x, core).
Axes of the slice: x: 2, y: 2, z: 4, core: 2. Of those that a mesh axis runs over, the one named last changes fastest.
Arguments:
- ints: bfloat16 [16, 6144, 128], P(('mol', 'pair'), 'aux'), parts along dimension 0, may hold values from -1.75 to 1.75
- proj_first: bfloat16 [128, 128, 128], P(('mol', 'pair')), parts along dimension 0, may hold values from -0.5 to 0.5
- proj_second: bfloat16 [128, 128, 128], P(('mol', 'pair')), parts along dimension 0, may hold values from -0.5 to 0.5
- intersections: bfloat16 [128, 4, 128, 128], P(('mol', 'pair')), parts along dimension 0, may hold values from -0.5 to 0.5
- couple: float32 [128, 4], P(('mol', 'pair')), parts along dimension 0, may hold values from -1.2 to 1.2
- virt_energy: float32 [128, 128], P(('mol', 'pair')), parts along dimension 0, may hold values from 0.2 to 3
- occ_energy: float32 [128, 2], P(('mol', 'pair')), parts along dimension 0, may hold values from -1.2 to -0.2
- pno_count: int32 [128], P(('mol', 'pair')), parts along dimension 0, may hold values from 64 to 128, as said below
- pair_orbitals: int32 [128, 2], P(('mol', 'pair')), parts along dimension 0, may hold values from 0 to 7, as said below
- neighbours: int32 [128, 4], P('mol'), parts along dimension 0, may hold values from 0 to 63, as said below
Outputs:
- amps: float32 [128, 128, 128], P(('mol', 'pair')), parts along dimension 0
- density: float32 [16, 128, 128], P(('mol', 'pair')), parts along dimension 0
The draws below stay inside these ranges and needn't reach their ends.
There are 2 independent parts, one for each index of `mol`. The reference program is written for one: setup_inputs(seed, part) draws one part's arguments, and reference() takes and returns one part's arrays. A program takes and returns all parts, laid end to end along the dimension named above; each array names one. Nothing has to cross between parts.
Inputs may be any that keep to these rules, and one draw needn't show every extreme that they name: `pno_count`: used slots are at least half of 128; some pair uses all 128. `pair_orbitals`: orbitals come in blocks of 2, pairs in aligned blocks of 16. The first orbital of a pair in pair block b lies in orbital block b; the second lies in block b - 1, b or b + 1 and differs from the first. In every pair block some second orbital lies in the block below and some in the block above, where those exist. `neighbours`: all coupled pairs listed for the 16 pairs of one aligned block b lie in 3 consecutive aligned blocks of pairs that contain b, centered on b where the ends of the pair list allow. At most 32 of them lie in any one aligned block, and for every block some aligned block supplies exactly 32.
All inputs are finite; a program needn't handle non-finite values.
Results may differ from the reference program's by a relative error of at most 0.0043.
Values may be sent and summed in bfloat16 or wider, within the bound.
No kernel may reach another device: no remote copies, remote signals or barrier semaphores. Data moves between devices by JAX's collectives and lax.ppermute only.
A program may use at most 64 MiB of HBM per device.

```python
import math
import jax
import jax.numpy as jnp
from jax import lax

P_SIZE = 128
AUX = 6144
OCC_DEV = 2
PAIR_DEV = 16
NBR = 4
ITERS = 2
NOCC = 8
NPAIRS = 64
CAP = 32
REACH = 1


def draw_pno_count(key, part):
    key = jax.random.fold_in(key, 11)
    counts = jax.random.randint(key, (NPAIRS,), P_SIZE // 2, P_SIZE + 1)
    return counts.at[0].set(P_SIZE).astype(jnp.int32)


def draw_pair_orbitals(key, part):
    key = jax.random.fold_in(key, 12)
    key_one, key_two, key_three, key_four = jax.random.split(key, 4)
    blocks = NPAIRS // PAIR_DEV
    rows = jnp.arange(NPAIRS)
    block = rows // PAIR_DEV
    inblock = rows % PAIR_DEV
    first_local = jax.random.randint(key_one, (NPAIRS,), 0, OCC_DEV)
    offset = jax.random.randint(key_two, (NPAIRS,), -1, 2)
    offset = jnp.where(inblock == 0, -1, jnp.where(inblock == 1, 1, offset))
    other = jnp.clip(block + offset, 0, blocks - 1)
    second_local = jax.random.randint(key_three, (NPAIRS,), 0, OCC_DEV)
    moved = (first_local + 1 + jax.random.randint(key_four, (NPAIRS,), 0, OCC_DEV - 1)) % OCC_DEV
    second_local = jnp.where(other == block, moved, second_local)
    first = block * OCC_DEV + first_local
    second = other * OCC_DEV + second_local
    return jnp.stack([first, second], axis=1).astype(jnp.int32)


def draw_neighbours(key, part):
    key = jax.random.fold_in(key, 13)
    blocks = NPAIRS // PAIR_DEV
    wanted = PAIR_DEV * NBR
    span = 2 * REACH + 1

    def one_block(block_key, block):
        key_one, key_two, key_three = jax.random.split(block_key, 3)
        order = jax.random.permutation(key_one, CAP * span)
        source = order // CAP
        score = jnp.where(source == source[0], 0, 1).astype(jnp.int32)
        kept = order[jnp.argsort(score, stable=True)][:wanted]
        kept = kept[jax.random.permutation(key_two, wanted)]
        local = jax.random.randint(key_three, (wanted,), 0, PAIR_DEV)
        start = jnp.clip(block - REACH, 0, blocks - span)
        return (start + kept // CAP) * PAIR_DEV + local
    table = jax.vmap(one_block)(jax.random.split(key, blocks), jnp.arange(blocks))
    return table.reshape(NPAIRS, NBR).astype(jnp.int32)


def draw_couple(key, part):
    key = jax.random.fold_in(key, 14)
    key_size, key_sign = jax.random.split(key)
    magnitude = jax.random.uniform(key_size, (NPAIRS, NBR), jnp.float32, 0.4, 1.2)
    polarity = jnp.where(jax.random.bernoulli(key_sign, 0.5, (NPAIRS, NBR)), 1.0, -1.0)
    return (magnitude * polarity).astype(jnp.float32)


def shard_levels(own_key, dims, cuts, least, high):
    loudness, own = 1.0, jax.random.fold_in(own_key, 6)
    for axis_at, blocks in cuts:
        draws = jnp.exp(jax.random.uniform(jax.random.fold_in(own, axis_at), (blocks,), jnp.float32, least / len(cuts), high / len(cuts)))
        loudness = loudness * jnp.repeat(draws, dims[axis_at] // blocks).reshape([-1 if axis == axis_at else 1 for axis in range(len(dims))])
    return loudness


def centred(rng, dims, deviation, reach, shards=(), kind=jnp.bfloat16):
    array = deviation * jax.random.normal(rng, dims, jnp.float32)
    if shards:
        array = array * shard_levels(rng, dims, shards, -0.22, 0.18)
    return jnp.clip(array, -reach, reach).astype(kind)


def setup_inputs(seed: int = 0, part: int = 0) -> dict:
    splits = jax.random.split(jax.random.key(seed), 11)
    part_keys = jax.random.split(jax.random.fold_in(splits[10], part), 11)
    return {
        "ints": centred(part_keys[0], (NOCC, AUX, P_SIZE), (AUX ** -0.25), 1.75, ((0, 4), (1, 4))),
        "proj_first": centred(part_keys[1], (NPAIRS, P_SIZE, P_SIZE), P_SIZE ** -0.5, 0.5, ((0, 4),)),
        "proj_second": centred(part_keys[2], (NPAIRS, P_SIZE, P_SIZE), P_SIZE ** -0.5, 0.5, ((0, 4),)),
        "intersections": centred(part_keys[3], (NPAIRS, NBR, P_SIZE, P_SIZE), P_SIZE ** -0.5, 0.5, ((0, 4),)),
        "couple": draw_couple(jax.random.fold_in(jax.random.fold_in(splits[10], part), 71), part),
        "virt_energy": jnp.clip(jnp.exp(math.log(3.0) - 2.7080502 * jax.random.uniform(part_keys[5], (NPAIRS, P_SIZE), jnp.float32) ** shard_levels(part_keys[5], (NPAIRS, P_SIZE), ((0, 4),), -0.2, 0.2)), 0.2, 3.0),
        "occ_energy": jnp.clip(-1.2 + 1 * jax.random.uniform(part_keys[6], (NPAIRS, 2), jnp.float32) ** shard_levels(part_keys[6], (NPAIRS, 2), ((0, 4),), -0.2, 0.2), -1.2, -0.2),
        "pno_count": draw_pno_count(jax.random.fold_in(jax.random.fold_in(splits[10], part), 71), part),
        "pair_orbitals": draw_pair_orbitals(jax.random.fold_in(jax.random.fold_in(splits[10], part), 71), part),
        "neighbours": draw_neighbours(jax.random.fold_in(jax.random.fold_in(splits[10], part), 71), part),
    }


HIGH = lax.Precision.HIGHEST


def pair_integrals(ints, proj_first, proj_second, pair_orbitals):
    def one(item):
        first, second, left_map, right_map = item
        left = jnp.dot(ints[first], left_map, preferred_element_type=jnp.float32).astype(jnp.bfloat16)
        right = jnp.dot(ints[second], right_map, preferred_element_type=jnp.float32).astype(jnp.bfloat16)
        return jnp.dot(left.T, right, preferred_element_type=jnp.float32)
    return lax.map(one, (pair_orbitals[:, 0], pair_orbitals[:, 1], proj_first, proj_second))


def coupling(amps, intersections, couple, neighbours):
    low = amps.astype(jnp.bfloat16)

    def one(item):
        over, weights, others = item
        taken = low[others].astype(jnp.float32)
        overf = over.astype(jnp.float32)
        half = jnp.einsum("nab,nbc->nac", overf, taken).astype(jnp.bfloat16)
        full = jnp.einsum("nac,ndc->nad", half.astype(jnp.float32), overf)
        return jnp.sum(weights[:, None, None] * full, axis=0)
    return lax.map(one, (intersections, couple, neighbours))


def density_terms(amps, proj_first, proj_second):
    def one(item):
        amp, left_map, right_map = item
        lf = left_map.astype(jnp.float32)
        rf = right_map.astype(jnp.float32)
        outer = jnp.dot(amp, amp.T, precision=HIGH)
        inner = jnp.dot(amp.T, amp, precision=HIGH)
        first = jnp.dot(jnp.dot(lf, outer, precision=HIGH), lf.T, precision=HIGH)
        second = jnp.dot(jnp.dot(rf, inner, precision=HIGH), rf.T, precision=HIGH)
        return first, second
    return lax.map(one, (amps, proj_first, proj_second))


def reference(ints, proj_first, proj_second, intersections, couple, virt_energy, occ_energy, pno_count, pair_orbitals, neighbours):
    exch = pair_integrals(ints, proj_first, proj_second, pair_orbitals)
    valid = jnp.arange(P_SIZE)[None, :] < pno_count[:, None]
    mask = (valid[:, :, None] & valid[:, None, :]).astype(jnp.float32)
    denom = virt_energy[:, :, None] + virt_energy[:, None, :] - occ_energy[:, 0, None, None] - occ_energy[:, 1, None, None]
    amps = (-mask * exch) / denom
    for sweep in range(ITERS):
        coupled = coupling(amps, intersections, couple, neighbours)
        amps = (-mask * (exch - coupled)) / denom
    first, second = density_terms(amps, proj_first, proj_second)
    density = jnp.zeros((NOCC, P_SIZE, P_SIZE), jnp.float32)
    density = density.at[pair_orbitals[:, 0]].add(first).at[pair_orbitals[:, 1]].add(second)
    return amps, density / P_SIZE
```

```python
import functools

import jax
import jax.numpy as jnp
import numpy as np
from jax import lax
from jax.experimental import pallas as pl
from jax.experimental.pallas import tpu as pltpu
from jax.sharding import PartitionSpec as P

ITERS = 2
BF16 = jnp.bfloat16
F32 = jnp.float32
VMEM = pl.BlockSpec(memory_space=pltpu.VMEM)
SMEM = pl.BlockSpec(memory_space=pltpu.SMEM)
ANY = pl.BlockSpec(memory_space=pl.ANY)
PARAMS = pltpu.CompilerParams(vmem_limit_bytes=24 * 2**20)


def dot(left, right, dims):
    return lax.dot_general(left, right, (dims, ((), ())), preferred_element_type=F32)


def split(value):
    high = value.astype(BF16)
    return high, (value - high.astype(F32)).astype(BF16)


def cost(flops, size):
    return pl.CostEstimate(flops=flops, bytes_accessed=size, transcendentals=0)


def product_kernel(with_own, own_ref, up_ref, down_ref, out_ref):
    count, _, width = own_ref.shape
    own = jnp.concatenate([own_ref[i] for i in range(count)], axis=1)
    near = jnp.concatenate([up_ref[0], down_ref[0]], axis=1)
    full = dot(own, near, ((0,), (0,)))
    for i in range(count):
        rows = full[i * width : (i + 1) * width]
        out_ref[i, :width] = rows[:, :width]
        out_ref[i, width : 2 * width] = rows[:, width:]
    if with_own:
        half = width // 2
        inner = dot(own_ref[0], own_ref[1], ((0,), (0,)))
        out_ref[0, 2 * width :] = inner[:half]
        out_ref[1, 2 * width :] = inner[half:]


def products(ints, up, down, with_own):
    count, depth, width = ints.shape
    rows = 2 * width + (width // 2 if with_own else 0)
    return pl.pallas_call(
        functools.partial(product_kernel, with_own),
        out_shape=jax.ShapeDtypeStruct((count, rows, width), F32),
        in_specs=[VMEM] * 3,
        out_specs=VMEM,
        compiler_params=PARAMS,
        cost_estimate=cost(8 * depth * width * width, 8 * depth * width),
        name="products",
    )(ints, up, down)


def exchange_kernel(
    slots_ref, half_ref, *refs
):
    count = slots_ref.shape[0]
    sums = refs[:8]
    first_ref, second_ref, factor_ref, exch_ref, low_ref, table = refs[8:]
    width = first_ref.shape[-1]
    mine = half_ref[0]
    for side in range(2):
        one = sums[4 * side][...] + sums[4 * side + 1][...]
        two = sums[4 * side + 2][...] + sums[4 * side + 3][...]
        i = mine if side == 0 else 1 - mine
        table[i * 6 + 4] = one[:width]
        table[i * 6 + 0] = one[width : 2 * width]
        table[i * 6 + 5] = two[:width]
        table[i * 6 + 1] = two[width : 2 * width]
        table[3, pl.ds(pl.multiple_of(i * (width // 2), width // 2), width // 2)] = one[2 * width :]
    table[6 + 2] = table[3].T
    for p in range(count):
        product = table[slots_ref[p]]
        right = second_ref[p]
        left = first_ref[p]
        high, rest = split(product)
        inner = dot(
            jnp.concatenate([high, rest], axis=1),
            jnp.concatenate([right, right], axis=0),
            ((1,), (0,)),
        )
        high, rest = split(inner)
        exch = dot(
            jnp.concatenate([left, left], axis=0),
            jnp.concatenate([high, rest], axis=0),
            ((0,), (0,)),
        )
        exch_ref[p] = exch
        low_ref[p] = (factor_ref[p] * exch).astype(BF16)


def exchange(slots, half, sums, first, second, factor):
    count, width, _ = first.shape
    return pl.pallas_call(
        exchange_kernel,
        out_shape=(
            jax.ShapeDtypeStruct(first.shape, F32),
            jax.ShapeDtypeStruct(first.shape, BF16),
        ),
        in_specs=[SMEM, SMEM] + [VMEM] * (len(sums) + 3),
        out_specs=(VMEM, VMEM),
        scratch_shapes=[pltpu.VMEM((12, width, width), F32)],
        compiler_params=PARAMS,
        cost_estimate=cost(8 * count * width**3, 20 * count * width * width),
        name="exchange",
    )(slots, half, *sums, first, second, factor)


def sweep_kernel(last, pieces, index_ref, couple_ref, spots_ref, *refs):
    parts = refs[:pieces]
    over_ref, exch_ref, factor_ref, second_ref = refs[pieces : pieces + 4]
    if last:
        amps_ref, terms_ref, table, sems = refs[pieces + 4 :]
    else:
        low_ref, table, sems = refs[pieces + 4 :]
    count = exch_ref.shape[0]
    nbr_count = over_ref.shape[1]
    copies = []
    at = 0
    for i, part in enumerate(parts):
        size = part.shape[0]
        copies.append(pltpu.make_async_copy(part, table.at[pl.ds(at, size)], sems.at[i]))
        at += size
    for copy in copies:
        copy.start()
    for copy in copies:
        copy.wait()
    if last:
        terms_ref[...] = jnp.zeros_like(terms_ref)
    for p in range(count):
        coupled = None
        for n in range(nbr_count):
            over = over_ref[p, n]
            half = dot(over, table[index_ref[p, n]], ((1,), (0,))).astype(BF16)
            full = couple_ref[p, n] * dot(half, over, ((1,), (1,)))
            coupled = full if coupled is None else coupled + full
        amps = factor_ref[p] * (exch_ref[p] - coupled)
        if not last:
            low_ref[p] = amps.astype(BF16)
            continue
        amps_ref[p] = amps
        high, rest = split(amps)
        right = second_ref[p]
        moved = dot(
            jnp.concatenate([right, right], axis=1),
            jnp.concatenate([high, rest], axis=1),
            ((1,), (1,)),
        )
        spot = spots_ref[p]
        terms_ref[spot] = terms_ref[spot] + square(moved)


def square(value):
    high, rest = split(value)
    return dot(
        jnp.concatenate([high, high, rest, rest], axis=1),
        jnp.concatenate([high, rest, high, rest], axis=1),
        ((1,), (1,)),
    )


def sweep(last, index, couple, spots, parts, over, exch, factor, second, occ_dev):
    count, width, _ = exch.shape
    rows = sum(part.shape[0] for part in parts)
    if last:
        out_shape = (
            jax.ShapeDtypeStruct(exch.shape, F32),
            jax.ShapeDtypeStruct((3 * occ_dev, width, width), F32),
        )
        out_specs = (VMEM, VMEM)
    else:
        out_shape = jax.ShapeDtypeStruct(exch.shape, BF16)
        out_specs = VMEM
    return pl.pallas_call(
        functools.partial(sweep_kernel, last, len(parts)),
        out_shape=out_shape,
        in_specs=[SMEM] * 3 + [ANY] * len(parts) + [VMEM] * 4,
        out_specs=out_specs,
        scratch_shapes=[
            pltpu.VMEM((rows, width, width), BF16),
            pltpu.SemaphoreType.DMA((len(parts),)),
        ],
        compiler_params=PARAMS,
        cost_estimate=cost(16 * count * width**3, (rows + 16 * count) * width * width),
        name="last_sweep" if last else "sweep",
    )(index, couple, spots, *parts, over, exch, factor, second)


def first_kernel(spots_ref, amps_ref, first_ref, terms_ref):
    terms_ref[...] = jnp.zeros_like(terms_ref)
    for p in range(amps_ref.shape[0]):
        high, rest = split(amps_ref[p])
        left = first_ref[p]
        moved = dot(
            jnp.concatenate([left, left], axis=1),
            jnp.concatenate([high, rest], axis=0),
            ((1,), (0,)),
        )
        spot = spots_ref[p]
        terms_ref[spot] = terms_ref[spot] + square(moved)


def first_terms(spots, amps, first, occ_dev):
    count, width, _ = amps.shape
    return pl.pallas_call(
        first_kernel,
        out_shape=jax.ShapeDtypeStruct((occ_dev, width, width), F32),
        in_specs=[SMEM, VMEM, VMEM],
        out_specs=VMEM,
        compiler_params=PARAMS,
        cost_estimate=cost(12 * count * width**3, 6 * count * width * width),
        name="first_terms",
    )(spots, amps, first)


def window_rounds(groups):
    reach = groups // 4
    span = 2 * reach + 1
    edges = []
    for block in range(groups):
        start = min(max(block - reach, 0), groups - span)
        edges += [(source, block) for source in range(start, start + span) if source != block]
    edges.sort(key=lambda edge: (abs(edge[0] - edge[1]), edge))
    rounds = []
    for source, block in edges:
        for pairs in rounds:
            if all(source != s and block != d for s, d in pairs):
                pairs.append((source, block))
                break
        else:
            rounds.append([(source, block)])
    return rounds


def same_owner_rank(owners):
    count = owners.shape[-1]
    places = jnp.arange(count)
    earlier = places[:, None] > places[None, :]
    same = owners[..., :, None] == owners[..., None, :]
    return jnp.sum(same & earlier, axis=-1)


def shards(
    ints,
    proj_first,
    proj_second,
    intersections,
    couple,
    virt_energy,
    occ_energy,
    pno_count,
    pair_orbitals,
    neighbours,
):
    groups = lax.axis_size("pair")
    here = lax.axis_index("pair")
    aux_count = lax.axis_size("aux")
    half = lax.axis_index("aux") % 2
    occ_dev, _, width = ints.shape
    pair_dev = proj_first.shape[0]
    nbr_count = couple.shape[1]
    wanted = pair_dev * nbr_count
    cap = 2 * wanted // groups
    count = pair_dev // 2
    up = [(i + 1, i) for i in range(groups - 1)]
    down = [(i, i + 1) for i in range(groups - 1)]

    def swap(value, step=1):
        return lax.ppermute(value, "aux", [(i, i ^ step) for i in range(aux_count)])

    def own(value):
        return lax.dynamic_slice_in_dim(value, half * count, count, 0)

    near = []
    for j in range(occ_dev):
        piece = lax.slice_in_dim(ints, j, j + 1, axis=0)
        near.append((lax.ppermute(piece, "pair", up), lax.ppermute(piece, "pair", down)))

    first = own(proj_first)
    second = own(proj_second)
    over = own(intersections)
    weights = own(couple)
    orbitals = own(pair_orbitals)
    base = (here - 1) * occ_dev
    first_slot = orbitals[:, 0] - base - occ_dev
    second_slot = orbitals[:, 1] - base
    energy = own(virt_energy)
    occupied = own(occ_energy)
    valid = jnp.arange(width)[None, :] < own(pno_count)[:, None]
    mask = (valid[:, :, None] & valid[:, None, :]).astype(F32)
    denom = (
        energy[:, :, None]
        + energy[:, None, :]
        - occupied[:, 0, None, None]
        - occupied[:, 1, None, None]
    )
    factor = -mask / denom

    def reduced(partial):
        kept = lax.dynamic_index_in_dim(partial, half, 0, keepdims=False)
        sent = lax.dynamic_index_in_dim(partial, 1 - half, 0, keepdims=False)
        total = kept + swap(sent)
        step = 2
        while 2 * step < aux_count:
            total = total + swap(total, step)
            step *= 2
        return total, swap(total, step)

    sums = []
    for j in range(occ_dev):
        sums.append(reduced(products(ints, *near[j], j == 0)))
    sums = [value for pair in sums for value in pair]
    sums = sums + [swap(value) for value in sums]
    exch, low = exchange(
        first_slot * 3 * occ_dev + second_slot,
        half.reshape(1),
        sums,
        first,
        second,
        factor,
    )

    if cap < pair_dev:
        requests = neighbours.reshape(groups, wanted)
        owners = requests // pair_dev
        ranks = same_owner_rank(owners)
        at_home = owners == here
        pick = at_home[:, None, :] & (ranks[:, None, :] == jnp.arange(cap)[None, :, None])
        local = requests % pair_dev
        select = jnp.any(
            pick[..., None]
            & (local[:, None, :, None] == jnp.arange(pair_dev)[None, None, None, :]),
            axis=2,
        )
        select = select.astype(BF16).reshape(groups * cap, pair_dev)
        own_requests = lax.dynamic_slice_in_dim(requests, here, 1, 0)[0]
        own_ranks = lax.dynamic_slice_in_dim(ranks, here, 1, 0)[0]
        row_index = own(
            (own_requests // pair_dev * cap + own_ranks).reshape(pair_dev, nbr_count)
        ).reshape(-1)
        index = jnp.arange(count * nbr_count).reshape(count, nbr_count)
    else:
        rounds = window_rounds(groups)
        table = lax.dynamic_slice_in_dim(neighbours, here * pair_dev + half * count, count, 0)
        owners = table // pair_dev
        local = table % pair_dev
        slot = jnp.zeros_like(owners)
        for place, pairs in enumerate(rounds):
            sources = np.full(groups, -1, np.int32)
            for source, block in pairs:
                sources[block] = source
            slot = jnp.where(owners == jnp.asarray(sources)[here], place + 1, slot)
        other = (local // count != half).astype(jnp.int32)
        index = (2 * slot + other) * count + local % count

    def gathered(low):
        if cap < pair_dev:
            others = swap(low)
            flat = jnp.where(
                half == 0, jnp.concatenate([low, others]), jnp.concatenate([others, low])
            ).reshape(pair_dev, width * width)
            outgoing = jnp.dot(select, flat, preferred_element_type=F32).astype(BF16)
            outgoing = outgoing.reshape(groups, cap, width, width)
            received = lax.all_to_all(outgoing, "pair", split_axis=0, concat_axis=0, tiled=True)
            return [received.reshape(groups * cap, width, width)[row_index]]
        pieces = [low] + [lax.ppermute(low, "pair", pairs) for pairs in rounds]
        return [value for piece in pieces for value in (piece, swap(piece))]

    for it in range(ITERS):
        out = sweep(
            it == ITERS - 1,
            index,
            weights,
            second_slot,
            gathered(low),
            over,
            exch,
            factor,
            second,
            occ_dev,
        )
        if it < ITERS - 1:
            low = out
    amps, terms = out

    from_below = lax.ppermute(terms[2 * occ_dev :], "pair", down)
    from_above = lax.ppermute(terms[:occ_dev], "pair", up)
    inner = first_terms(first_slot, amps, first, occ_dev)
    others = swap(amps)
    whole = jnp.where(half == 0, jnp.concatenate([amps, others]), jnp.concatenate([others, amps]))
    density = inner + terms[occ_dev : 2 * occ_dev] + from_below + from_above
    density = (density + swap(density)) / width
    return (whole, density)


def solution(mesh):
    return jax.shard_map(
        shards,
        mesh=mesh,
        in_specs=(
            P(("mol", "pair"), "aux", None),
            P(("mol", "pair"), None, None),
            P(("mol", "pair"), None, None),
            P(("mol", "pair"), None, None, None),
            P(("mol", "pair"), None),
            P(("mol", "pair"), None),
            P(("mol", "pair"), None),
            P(("mol", "pair")),
            P(("mol", "pair"), None),
            P("mol", None),
        ),
        out_specs=(P(("mol", "pair"), None, None), P(("mol", "pair"), None, None)),
        check_vma=False,
    )
```

```python
import functools

import jax
import jax.numpy as jnp
from jax import lax
from jax.experimental import pallas as pl
from jax.experimental.pallas import tpu as pltpu
from jax.sharding import PartitionSpec as P

ITERS = 2
BF16 = jnp.bfloat16
F32 = jnp.float32
VMEM = pl.BlockSpec(memory_space=pltpu.VMEM)
SMEM = pl.BlockSpec(memory_space=pltpu.SMEM)
ANY = pl.BlockSpec(memory_space=pl.ANY)


def params(mib):
    return pltpu.CompilerParams(vmem_limit_bytes=mib * 2**20)


def dot(left, right, dims):
    return lax.dot_general(left, right, (dims, ((), ())), preferred_element_type=F32)


def split(value):
    high = value.astype(BF16)
    return high, (value - high.astype(F32)).astype(BF16)


def square(value):
    high, rest = split(value)
    return dot(
        jnp.concatenate([high, high, rest, rest], axis=1),
        jnp.concatenate([high, rest, high, rest], axis=1),
        ((1,), (1,)),
    )


def cost(flops, size):
    return pl.CostEstimate(flops=flops, bytes_accessed=size, transcendentals=0)


def product_kernel(own_ref, up_ref, down_ref, out_ref):
    count, _, width = own_ref.shape
    own = jnp.concatenate([own_ref[i] for i in range(count)], axis=1)
    at = 0
    for near_ref in (up_ref, down_ref):
        near = jnp.concatenate([near_ref[i] for i in range(count)], axis=1)
        full = dot(own, near, ((0,), (0,)))
        for j in range(count):
            for i in range(count):
                out_ref[i, at : at + width] = full[
                    i * width : (i + 1) * width, j * width : (j + 1) * width
                ]
            at += width
    half = width // 2
    inner = dot(own_ref[0], own_ref[1], ((0,), (0,)))
    out_ref[0, at:] = inner[:half]
    out_ref[1, at:] = inner[half:]


def products(ints, up, down):
    count, depth, width = ints.shape
    rows = 2 * count * width + width // 2
    return pl.pallas_call(
        product_kernel,
        out_shape=jax.ShapeDtypeStruct((count, rows, width), F32),
        in_specs=[VMEM] * 3,
        out_specs=VMEM,
        compiler_params=params(12),
        cost_estimate=cost(18 * depth * width * width, 12 * depth * width),
        name="products",
    )(ints, up, down)


def exchange_kernel(
    here_ref, half_ref, orbitals_ref, total_ref, far_ref, total_other, far_other,
    first_ref, second_ref, factor_ref, exch_ref, low_ref, table,
):
    count, width, _ = exch_ref.shape
    half = half_ref[0]
    base = here_ref[0] * 2 - 2
    for i, total in (
        (half, total_ref[...] + far_ref[...]),
        (1 - half, total_other[...] + far_other[...]),
    ):
        for at, slot in enumerate((4, 5, 0, 1)):
            table[i * 6 + slot] = total[at * width : (at + 1) * width]
        table[3, pl.ds(pl.multiple_of(i * (width // 2), width // 2), width // 2)] = total[4 * width :]
    table[6 + 2] = table[3].T
    for p in range(count):
        row = half * count + p
        slot = (orbitals_ref[0, row] - base - 2) * 6 + orbitals_ref[1, row] - base
        right = second_ref[p]
        left = first_ref[p]
        high, rest = split(table[slot])
        inner = dot(
            jnp.concatenate([high, rest], axis=1),
            jnp.concatenate([right, right], axis=0),
            ((1,), (0,)),
        )
        high, rest = split(inner)
        exch = dot(
            jnp.concatenate([left, left], axis=0),
            jnp.concatenate([high, rest], axis=0),
            ((0,), (0,)),
        )
        exch_ref[p] = exch
        low_ref[p] = (factor_ref[p] * exch).astype(BF16)


def exchange(here, half, orbitals, sums, first, second, factor):
    shape = first.shape
    count, width, _ = shape
    return pl.pallas_call(
        exchange_kernel,
        out_shape=(jax.ShapeDtypeStruct(shape, F32), jax.ShapeDtypeStruct(shape, BF16)),
        in_specs=[SMEM] * 3 + [VMEM] * (len(sums) + 3),
        out_specs=(VMEM, VMEM),
        scratch_shapes=[pltpu.VMEM((12, width, width), F32)],
        compiler_params=params(12),
        cost_estimate=cost(8 * count * width**3, 20 * count * width * width),
        name="exchange",
    )(here, half, orbitals, *sums, first, second, factor)


def sweep_kernel(last, pieces, rounds, here_ref, half_ref, orbitals_ref, near_ref, couple_ref, *refs):
    parts = refs[:pieces]
    over_ref, exch_ref, factor_ref, second_ref = refs[pieces : pieces + 4]
    if last:
        amps_ref, terms_ref, table = refs[pieces + 4 :]
    else:
        low_ref, table = refs[pieces + 4 :]
    count, width, _ = exch_ref.shape
    pair_dev, nbr_count = over_ref.shape[:2]
    here = here_ref[0]
    half = half_ref[0]
    at = 0
    for part in parts:
        table[at : at + part.shape[0]] = part[...]
        at += part.shape[0]
    sources = []
    for pairs in rounds or ():
        source = -1
        for start, end in pairs:
            source = jnp.where(here == end, start, source)
        sources.append(source)

    def place(p, n):
        if rounds is None:
            return p * nbr_count + n
        wanted = near_ref[n, here * pair_dev + half * count + p]
        owner = wanted // pair_dev
        local = wanted - owner * pair_dev
        slot = 0
        for at, source in enumerate(sources):
            slot = jnp.where(owner == source, 2 * at + 2, slot)
        side = local // count
        return (slot + jnp.where(side == half, 0, 1)) * count + local - side * count

    done = []
    for p in range(count):
        row = half * count + p
        halves = []
        for n in range(nbr_count):
            moved = dot(over_ref[row, n], table[place(p, n)], ((1,), (0,)))
            halves.append((couple_ref[n, row] * moved).astype(BF16))
        coupled = dot(
            jnp.concatenate(halves, axis=1),
            jnp.concatenate([over_ref[row, n] for n in range(nbr_count)], axis=1),
            ((1,), (1,)),
        )
        amps = factor_ref[p] * (exch_ref[p] - coupled)
        if last:
            amps_ref[p] = amps
            done.append(amps)
        else:
            low_ref[p] = amps.astype(BF16)
    if last:
        terms = []
        for p in range(count):
            right = second_ref[p]
            high, rest = split(done[p])
            moved = dot(
                jnp.concatenate([right, right], axis=1),
                jnp.concatenate([high, rest], axis=1),
                ((1,), (1,)),
            )
            terms.append(square(moved))
        terms_ref[...] = jnp.zeros_like(terms_ref)
        for p in range(count):
            spot = orbitals_ref[1, half * count + p] - here * 2 + 2
            terms_ref[spot] += terms[p]


def sweep(last, rounds, here, half, orbitals, near, couple, parts, over, exch, factor, second):
    count, width, _ = exch.shape
    rows = sum(part.shape[0] for part in parts)
    if last:
        out_shape = (
            jax.ShapeDtypeStruct(exch.shape, F32),
            jax.ShapeDtypeStruct((6, width, width), F32),
        )
        out_specs = (VMEM, VMEM)
    else:
        out_shape = jax.ShapeDtypeStruct(exch.shape, BF16)
        out_specs = VMEM
    return pl.pallas_call(
        functools.partial(sweep_kernel, last, len(parts), rounds),
        out_shape=out_shape,
        in_specs=[SMEM] * 5 + [VMEM] * (len(parts) + 4),
        out_specs=out_specs,
        scratch_shapes=[pltpu.VMEM((rows, width, width), BF16)],
        compiler_params=params(16),
        cost_estimate=cost(16 * count * width**3, (rows + 16 * count) * width * width),
        name="last_sweep" if last else "sweep",
    )(here, half, orbitals, near, couple, *parts, over, exch, factor, second)


def first_kernel(
    here_ref, half_ref, orbitals_ref, amps_ref, others_ref, first_ref, whole_ref, terms_ref, sems
):
    count = amps_ref.shape[0]
    half = half_ref[0]
    copies = [
        pltpu.make_async_copy(amps_ref, whole_ref.at[pl.ds(half * count, count)], sems.at[0]),
        pltpu.make_async_copy(others_ref, whole_ref.at[pl.ds((1 - half) * count, count)], sems.at[1]),
    ]
    for copy in copies:
        copy.start()
    terms = []
    for p in range(count):
        high, rest = split(amps_ref[p])
        left = first_ref[p]
        moved = dot(
            jnp.concatenate([left, left], axis=1),
            jnp.concatenate([high, rest], axis=0),
            ((1,), (0,)),
        )
        terms.append(square(moved))
    terms_ref[...] = jnp.zeros_like(terms_ref)
    for p in range(count):
        spot = orbitals_ref[0, half * count + p] - here_ref[0] * 2
        terms_ref[spot] += terms[p]
    for copy in copies:
        copy.wait()


def first_terms(here, half, orbitals, amps, others, first):
    count, width, _ = amps.shape
    return pl.pallas_call(
        first_kernel,
        out_shape=(
            jax.ShapeDtypeStruct((2 * count, width, width), F32),
            jax.ShapeDtypeStruct((2, width, width), F32),
        ),
        in_specs=[SMEM] * 3 + [VMEM] * 3,
        out_specs=(ANY, VMEM),
        scratch_shapes=[pltpu.SemaphoreType.DMA((2,))],
        compiler_params=params(12),
        cost_estimate=cost(12 * count * width**3, 16 * count * width * width),
        name="first_terms",
    )(here, half, orbitals, amps, others, first)


def window_rounds(groups):
    reach = groups // 4
    span = 2 * reach + 1
    edges = []
    for block in range(groups):
        start = min(max(block - reach, 0), groups - span)
        edges += [(source, block) for source in range(start, start + span) if source != block]
    edges.sort(key=lambda edge: (abs(edge[0] - edge[1]), edge))
    rounds = []
    for source, block in edges:
        for pairs in rounds:
            if all(source != s and block != d for s, d in pairs):
                pairs.append((source, block))
                break
        else:
            rounds.append([(source, block)])
    return rounds[::-1]


def same_owner_rank(owners):
    count = owners.shape[-1]
    places = jnp.arange(count)
    earlier = places[:, None] > places[None, :]
    same = owners[..., :, None] == owners[..., None, :]
    return jnp.sum(same & earlier, axis=-1)


def shards(
    ints,
    proj_first,
    proj_second,
    intersections,
    couple,
    virt_energy,
    occ_energy,
    pno_count,
    pair_orbitals,
    neighbours,
):
    groups = lax.axis_size("pair")
    here = lax.axis_index("pair")
    aux_count = lax.axis_size("aux")
    half = lax.axis_index("aux") % 2
    occ_dev, _, width = ints.shape
    pair_dev = proj_first.shape[0]
    nbr_count = couple.shape[1]
    wanted = pair_dev * nbr_count
    cap = 2 * wanted // groups
    count = pair_dev // 2
    up = [(i + 1, i) for i in range(groups - 1)]
    down = [(i, i + 1) for i in range(groups - 1)]
    here_s = here.reshape(1)
    half_s = half.reshape(1)
    orbitals = pair_orbitals.T

    def swap(value, step=1):
        return lax.ppermute(value, "aux", [(i, i ^ step) for i in range(aux_count)])

    above = lax.ppermute(ints, "pair", up)
    below = lax.ppermute(ints, "pair", down)

    def own(value):
        return lax.dynamic_slice_in_dim(value, half * count, count, 0)

    first = own(proj_first)
    second = own(proj_second)
    valid = jnp.arange(width)[None, :] < pno_count[:, None]
    mask = (valid[:, :, None] & valid[:, None, :]).astype(F32)
    denom = (
        virt_energy[:, :, None]
        + virt_energy[:, None, :]
        - occ_energy[:, 0, None, None]
        - occ_energy[:, 1, None, None]
    )
    factor = own(-mask / denom)
    above, first, second, factor = lax.optimization_barrier((above, first, second, factor))

    partial = products(ints, above, below)
    kept = lax.dynamic_index_in_dim(partial, half, 0, keepdims=False)
    sent = lax.dynamic_index_in_dim(partial, 1 - half, 0, keepdims=False)
    total = kept + swap(sent)
    step = 2
    while 2 * step < aux_count:
        total = total + swap(total, step)
        step *= 2
    far = swap(total, step)
    exch, low = exchange(
        here_s, half_s, orbitals, (total, far, swap(total), swap(far)), first, second, factor
    )

    if cap < pair_dev:
        rounds = None
        requests = neighbours.reshape(groups, wanted)
        owners = requests // pair_dev
        ranks = same_owner_rank(owners)
        at_home = owners == here
        pick = at_home[:, None, :] & (ranks[:, None, :] == jnp.arange(cap)[None, :, None])
        local = requests % pair_dev
        select = jnp.any(
            pick[..., None]
            & (local[:, None, :, None] == jnp.arange(pair_dev)[None, None, None, :]),
            axis=2,
        )
        select = select.astype(BF16).reshape(groups * cap, pair_dev)
        own_requests = lax.dynamic_slice_in_dim(requests, here, 1, 0)[0]
        own_ranks = lax.dynamic_slice_in_dim(ranks, here, 1, 0)[0]
        row_index = lax.dynamic_slice_in_dim(
            own_requests // pair_dev * cap + own_ranks,
            half * count * nbr_count,
            count * nbr_count,
            0,
        )
    else:
        rounds = window_rounds(groups)

    def gathered(low):
        if rounds is None:
            others = swap(low)
            flat = jnp.where(
                half == 0, jnp.concatenate([low, others]), jnp.concatenate([others, low])
            ).reshape(pair_dev, width * width)
            outgoing = jnp.dot(select, flat, preferred_element_type=F32).astype(BF16)
            outgoing = outgoing.reshape(groups, cap, width, width)
            received = lax.all_to_all(outgoing, "pair", split_axis=0, concat_axis=0, tiled=True)
            return [received.reshape(groups * cap, width, width)[row_index]]
        pieces = [low] + [lax.ppermute(low, "pair", pairs) for pairs in rounds]
        return [value for piece in pieces for value in (piece, swap(piece))]

    for it in range(ITERS):
        out = sweep(
            it == ITERS - 1,
            rounds,
            here_s,
            half_s,
            orbitals,
            neighbours.T,
            couple.T,
            gathered(low),
            intersections,
            exch,
            factor,
            second,
        )
        if it < ITERS - 1:
            low = out
    amps, terms = out

    from_below = lax.ppermute(terms[2 * occ_dev :], "pair", down)
    from_above = lax.ppermute(terms[:occ_dev], "pair", up)
    whole, inner = first_terms(here_s, half_s, orbitals, amps, swap(amps), first)
    density = inner + terms[occ_dev : 2 * occ_dev] + from_below + from_above
    density = (density + swap(density)) / width
    return (whole, density)


def solution(mesh):
    return jax.shard_map(
        shards,
        mesh=mesh,
        in_specs=(
            P(("mol", "pair"), "aux", None),
            P(("mol", "pair"), None, None),
            P(("mol", "pair"), None, None),
            P(("mol", "pair"), None, None, None),
            P(("mol", "pair"), None),
            P(("mol", "pair"), None),
            P(("mol", "pair"), None),
            P(("mol", "pair")),
            P(("mol", "pair"), None),
            P("mol", None),
        ),
        out_specs=(P(("mol", "pair"), None, None), P(("mol", "pair"), None, None)),
        check_vma=False,
    )
```

```python
import functools

import jax
import jax.numpy as jnp
from jax import lax
from jax.experimental import pallas as pl
from jax.experimental.pallas import tpu as pltpu
from jax.sharding import PartitionSpec as P

ITERS = 2
BF16 = jnp.bfloat16
F32 = jnp.float32
VMEM = pl.BlockSpec(memory_space=pltpu.VMEM)
SMEM = pl.BlockSpec(memory_space=pltpu.SMEM)
ANY = pl.BlockSpec(memory_space=pl.ANY)


def params(mib):
    return pltpu.CompilerParams(vmem_limit_bytes=mib * 2**20)


def dot(left, right, dims):
    return lax.dot_general(left, right, (dims, ((), ())), preferred_element_type=F32)


def split(value):
    high = value.astype(BF16)
    return high, (value - high.astype(F32)).astype(BF16)


def square(value):
    high, rest = split(value)
    return dot(
        jnp.concatenate([high, high, rest, rest], axis=1),
        jnp.concatenate([high, rest, high, rest], axis=1),
        ((1,), (1,)),
    )


def cost(flops, size):
    return pl.CostEstimate(flops=flops, bytes_accessed=size, transcendentals=0)


def prepare_kernel(
    aux_ref, occ_ref, used_ref, energy_ref, first_ref, second_ref, ints_ref,
    first_out, second_out, ints_out, factor_ref, sems,
):
    count, width, _ = factor_ref.shape
    half = lax.rem(aux_ref[0], 2)
    rows = pl.ds(half * count, count)
    copies = [
        pltpu.make_async_copy(first_ref.at[rows], first_out, sems.at[0]),
        pltpu.make_async_copy(second_ref.at[rows], second_out, sems.at[1]),
        pltpu.make_async_copy(ints_ref, ints_out, sems.at[2]),
    ]
    for copy in copies:
        copy.start()
    shape = (width, width)
    along = lax.broadcasted_iota(jnp.int32, shape, 1)
    down = lax.broadcasted_iota(jnp.int32, shape, 0)
    for p in range(count):
        row = half * count + p
        energy = jnp.broadcast_to(energy_ref[pl.ds(row, 1)], shape)
        denom = energy.T + energy - occ_ref[0, row] - occ_ref[1, row]
        inside = (along < used_ref[row]) & (down < used_ref[row])
        factor_ref[p] = jnp.where(inside, -1.0 / denom, 0.0)
    for copy in copies:
        copy.wait()


def prepare(aux, occupied, used, energy, first, second, ints):
    pair_dev, width, _ = first.shape
    shape = (pair_dev // 2, width, width)
    return pl.pallas_call(
        prepare_kernel,
        out_shape=(
            jax.ShapeDtypeStruct(shape, BF16),
            jax.ShapeDtypeStruct(shape, BF16),
            jax.ShapeDtypeStruct(ints.shape, BF16),
            jax.ShapeDtypeStruct(shape, F32),
        ),
        in_specs=[SMEM] * 3 + [VMEM] + [ANY] * 3,
        out_specs=(VMEM,) * 4,
        scratch_shapes=[pltpu.SemaphoreType.DMA((3,))],
        compiler_params=params(8),
        cost_estimate=cost(0, 8 * pair_dev * width * width),
        name="prepare",
    )(aux, occupied, used, energy, first, second, ints)


def product_kernel(aux_ref, own_ref, up_ref, down_ref, kept_ref, sent_ref, inner):
    count, _, width = own_ref.shape
    side = lax.rem(aux_ref[0], 2)
    own = jnp.concatenate([own_ref[side], own_ref[1 - side]], axis=1)
    at = 0
    for near_ref in (up_ref, down_ref):
        near = jnp.concatenate([near_ref[i] for i in range(count)], axis=1)
        full = dot(own, near, ((0,), (0,)))
        for j in range(count):
            columns = slice(j * width, (j + 1) * width)
            kept_ref[at : at + width] = full[:width, columns]
            sent_ref[at : at + width] = full[width:, columns]
            at += width
    half = width // 2
    inner[...] = dot(own_ref[0], own_ref[1], ((0,), (0,)))
    kept_ref[at:] = inner[pl.ds(pl.multiple_of(side * half, half), half)]
    sent_ref[at:] = inner[pl.ds(pl.multiple_of((1 - side) * half, half), half)]


def products(aux, ints, up, down):
    count, depth, width = ints.shape
    rows = 2 * count * width + width // 2
    return pl.pallas_call(
        product_kernel,
        out_shape=(jax.ShapeDtypeStruct((rows, width), F32),) * 2,
        in_specs=[SMEM] + [VMEM] * 3,
        out_specs=(VMEM, VMEM),
        scratch_shapes=[pltpu.VMEM((width, width), F32)],
        compiler_params=params(12),
        cost_estimate=cost(18 * depth * width * width, 12 * depth * width),
        name="products",
    )(aux, ints, up, down)


def own_part(aux_ref, low_ref, part_ref):
    count = part_ref.shape[0]
    part_ref[...] = low_ref[pl.ds(lax.rem(aux_ref[0] // 2, 2) * count, count)]


def exchange_kernel(
    here_ref, aux_ref, orbitals_ref, total_ref, far_ref, total_other, far_other,
    first_ref, second_ref, factor_ref, exch_ref, low_ref, part_ref, table,
):
    count, width, _ = exch_ref.shape
    half = lax.rem(aux_ref[0], 2)
    base = here_ref[0] * 2 - 2
    for i, total in (
        (half, total_ref[...].astype(F32) + far_ref[...].astype(F32)),
        (1 - half, total_other[...].astype(F32) + far_other[...].astype(F32)),
    ):
        for at, slot in enumerate((4, 5, 0, 1)):
            table[i * 6 + slot] = total[at * width : (at + 1) * width]
        table[3, pl.ds(pl.multiple_of(i * (width // 2), width // 2), width // 2)] = total[4 * width :]
    table[6 + 2] = table[3].T
    for p in range(count):
        row = half * count + p
        slot = (orbitals_ref[0, row] - base - 2) * 6 + orbitals_ref[1, row] - base
        right = second_ref[p]
        left = first_ref[p]
        high, rest = split(table[slot])
        inner = dot(
            jnp.concatenate([high, rest], axis=1),
            jnp.concatenate([right, right], axis=0),
            ((1,), (0,)),
        )
        high, rest = split(inner)
        exch = dot(
            jnp.concatenate([left, left], axis=0),
            jnp.concatenate([high, rest], axis=0),
            ((0,), (0,)),
        )
        exch_ref[p] = exch
        low_ref[p] = (factor_ref[p] * exch).astype(BF16)
    own_part(aux_ref, low_ref, part_ref)


def exchange(here, aux, orbitals, sums, first, second, factor):
    shape = first.shape
    count, width, _ = shape
    return pl.pallas_call(
        exchange_kernel,
        out_shape=(
            jax.ShapeDtypeStruct(shape, F32),
            jax.ShapeDtypeStruct(shape, BF16),
            jax.ShapeDtypeStruct((count // 2, width, width), BF16),
        ),
        in_specs=[SMEM] * 3 + [VMEM] * (len(sums) + 3),
        out_specs=(VMEM,) * 3,
        scratch_shapes=[pltpu.VMEM((12, width, width), F32)],
        compiler_params=params(12),
        cost_estimate=cost(8 * count * width**3, 20 * count * width * width),
        name="exchange",
    )(here, aux, orbitals, *sums, first, second, factor)


def sweep_kernel(last, pieces, rounds, here_ref, aux_ref, orbitals_ref, near_ref, couple_ref, *refs):
    parts = refs[:pieces]
    over_ref, exch_ref, factor_ref, second_ref = refs[pieces : pieces + 4]
    if last:
        amps_ref, terms_ref, table = refs[pieces + 4 :]
    else:
        low_ref, part_ref, table = refs[pieces + 4 :]
    count, width, _ = exch_ref.shape
    pair_dev, nbr_count = over_ref.shape[:2]
    here = here_ref[0]
    half = lax.rem(aux_ref[0], 2)
    at = 0
    for part in parts:
        table[at : at + part.shape[0]] = part[...]
        at += part.shape[0]
    across = lax.rem(aux_ref[0] // 2, 2)
    near_block = -1
    for start, end in rounds[0] if rounds else ():
        near_block = jnp.where(here == end, start, near_block)

    def place(p, n):
        if not rounds:
            return p * nbr_count + n
        wanted = near_ref[n, here * pair_dev + half * count + p]
        owner = wanted // pair_dev
        local = wanted - owner * pair_dev
        side = local // count
        local = local - side * count
        other = jnp.where(side == half, 0, 1)
        quarter = local // (count // 2)
        halved = (
            4 * count
            + jnp.where(quarter == across, 0, count)
            + other * (count // 2)
            + local
            - quarter * (count // 2)
        )
        spot = other * count + local + jnp.where(owner == here, 0, 2 * count)
        return jnp.where(owner == near_block, halved, spot)

    done = []
    for p in range(count):
        row = half * count + p
        halves = []
        for n in range(nbr_count):
            moved = dot(over_ref[row, n], table[place(p, n)], ((1,), (0,)))
            halves.append((couple_ref[n, row] * moved).astype(BF16))
        coupled = dot(
            jnp.concatenate(halves, axis=1),
            jnp.concatenate([over_ref[row, n] for n in range(nbr_count)], axis=1),
            ((1,), (1,)),
        )
        amps = factor_ref[p] * (exch_ref[p] - coupled)
        if last:
            amps_ref[p] = amps
            done.append(amps)
        else:
            low_ref[p] = amps.astype(BF16)
    if not last:
        own_part(aux_ref, low_ref, part_ref)
    else:
        terms = []
        for p in range(count):
            right = second_ref[p]
            high, rest = split(done[p])
            moved = dot(
                jnp.concatenate([right, right], axis=1),
                jnp.concatenate([high, rest], axis=1),
                ((1,), (1,)),
            )
            terms.append(square(moved))
        terms_ref[...] = jnp.zeros_like(terms_ref)
        for p in range(count):
            spot = orbitals_ref[1, half * count + p] - here * 2 + 2
            terms_ref[spot] += terms[p]


def sweep(last, rounds, here, aux, orbitals, near, couple, parts, over, exch, factor, second):
    count, width, _ = exch.shape
    rows = sum(part.shape[0] for part in parts)
    if last:
        out_shape = (
            jax.ShapeDtypeStruct(exch.shape, F32),
            jax.ShapeDtypeStruct((6, width, width), F32),
        )
        out_specs = (VMEM, VMEM)
    else:
        out_shape = (
            jax.ShapeDtypeStruct(exch.shape, BF16),
            jax.ShapeDtypeStruct((count // 2, width, width), BF16),
        )
        out_specs = (VMEM, VMEM)
    return pl.pallas_call(
        functools.partial(sweep_kernel, last, len(parts), rounds),
        out_shape=out_shape,
        in_specs=[SMEM] * 5 + [VMEM] * (len(parts) + 4),
        out_specs=out_specs,
        scratch_shapes=[pltpu.VMEM((rows, width, width), BF16)],
        compiler_params=params(16),
        cost_estimate=cost(16 * count * width**3, (rows + 16 * count) * width * width),
        name="last_sweep" if last else "sweep",
    )(here, aux, orbitals, near, couple, *parts, over, exch, factor, second)


def token_kernel(piece_ref, out_ref):
    out_ref[...] = piece_ref[0, :16]


def token(piece):
    return pl.pallas_call(
        token_kernel,
        out_shape=jax.ShapeDtypeStruct((16, piece.shape[-1]), BF16),
        in_specs=[VMEM],
        out_specs=VMEM,
        compiler_params=params(4),
        cost_estimate=cost(5 * 10**9, 2**20),
        name="token",
    )(piece)


def join_kernel(left_ref, right_ref, token_ref, out_ref):
    del token_ref
    out_ref[...] = left_ref[...] + right_ref[...]


def joined(left, right, token):
    return pl.pallas_call(
        join_kernel,
        out_shape=jax.ShapeDtypeStruct(left.shape, BF16),
        in_specs=[VMEM] * 3,
        out_specs=VMEM,
        compiler_params=params(4),
        cost_estimate=cost(left.size, 6 * left.size),
        name="joined",
    )(left, right, token)


def first_kernel(
    here_ref, aux_ref, orbitals_ref, amps_ref, others_ref, first_ref, whole_ref, terms_ref, sems
):
    count = amps_ref.shape[0]
    half = lax.rem(aux_ref[0], 2)
    copies = [
        pltpu.make_async_copy(amps_ref, whole_ref.at[pl.ds(half * count, count)], sems.at[0]),
        pltpu.make_async_copy(others_ref, whole_ref.at[pl.ds((1 - half) * count, count)], sems.at[1]),
    ]
    for copy in copies:
        copy.start()
    terms = []
    for p in range(count):
        high, rest = split(amps_ref[p])
        left = first_ref[p]
        moved = dot(
            jnp.concatenate([left, left], axis=1),
            jnp.concatenate([high, rest], axis=0),
            ((1,), (0,)),
        )
        terms.append(square(moved))
    terms_ref[...] = jnp.zeros_like(terms_ref)
    for p in range(count):
        spot = orbitals_ref[0, half * count + p] - here_ref[0] * 2
        terms_ref[spot] += terms[p]
    for copy in copies:
        copy.wait()


def first_terms(here, aux, orbitals, amps, others, first):
    count, width, _ = amps.shape
    return pl.pallas_call(
        first_kernel,
        out_shape=(
            jax.ShapeDtypeStruct((2 * count, width, width), F32),
            jax.ShapeDtypeStruct((2, width, width), F32),
        ),
        in_specs=[SMEM] * 3 + [VMEM] * 3,
        out_specs=(ANY, VMEM),
        scratch_shapes=[pltpu.SemaphoreType.DMA((2,))],
        compiler_params=params(12),
        cost_estimate=cost(12 * count * width**3, 16 * count * width * width),
        name="first_terms",
    )(here, aux, orbitals, amps, others, first)


def window_rounds(groups):
    edges = []
    for block in range(groups):
        start = min(max(block - 1, 0), groups - 3)
        edges += [(source, block) for source in range(start, start + 3) if source != block]
    edges.sort(key=lambda edge: (-abs(edge[0] - edge[1]), edge))
    first = []
    for source, block in edges:
        if all(source != s and block != d for s, d in first):
            first.append((source, block))
    rest = [edge for edge in edges if edge not in first]
    both = [edge for edge in rest if edge[::-1] in rest]
    rounds = [first, both, [edge for edge in rest if edge not in both]]
    assert len(rounds[0]) == groups
    return rounds


def same_owner_rank(owners):
    count = owners.shape[-1]
    places = jnp.arange(count)
    earlier = places[:, None] > places[None, :]
    same = owners[..., :, None] == owners[..., None, :]
    return jnp.sum(same & earlier, axis=-1)


def shards(
    ints,
    proj_first,
    proj_second,
    intersections,
    couple,
    virt_energy,
    occ_energy,
    pno_count,
    pair_orbitals,
    neighbours,
):
    groups = lax.axis_size("pair")
    here = lax.axis_index("pair")
    aux_count = lax.axis_size("aux")
    aux = lax.axis_index("aux")
    half = aux % 2
    occ_dev, _, width = ints.shape
    pair_dev = proj_first.shape[0]
    nbr_count = couple.shape[1]
    wanted = pair_dev * nbr_count
    cap = 2 * wanted // groups
    count = pair_dev // 2
    up = [(i + 1, i) for i in range(groups - 1)]
    down = [(i, i + 1) for i in range(groups - 1)]
    orbitals = pair_orbitals.T

    def swap(value, step=1):
        return lax.ppermute(value, "aux", [(i, i ^ step) for i in range(aux_count)])

    ints, here_s, aux_s = lax.optimization_barrier((ints, here.reshape(1), aux.reshape(1)))

    above = lax.ppermute(ints, "pair", up)
    below = lax.ppermute(ints, "pair", down)
    first, second, ints, factor = prepare(
        aux_s, occ_energy.T, pno_count, virt_energy, proj_first, proj_second, ints
    )
    above, first, second, ints, factor = lax.optimization_barrier(
        (above, first, second, ints, factor)
    )

    kept, sent = products(aux_s, ints, above, below)
    total = kept + swap(sent)
    step = 2
    while 2 * step < aux_count:
        total = total + swap(total, step)
        step *= 2
    total = total.astype(BF16)
    far = swap(total, step)
    exch, low, part = exchange(
        here_s, aux_s, orbitals, (total, far, swap(total), swap(far)), first, second, factor
    )

    if cap < pair_dev or groups // 4 != 1 or aux_count != 4:
        rounds = None
        requests = neighbours.reshape(groups, wanted)
        owners = requests // pair_dev
        ranks = same_owner_rank(owners)
        at_home = owners == here
        pick = at_home[:, None, :] & (ranks[:, None, :] == jnp.arange(cap)[None, :, None])
        local = requests % pair_dev
        select = jnp.any(
            pick[..., None]
            & (local[:, None, :, None] == jnp.arange(pair_dev)[None, None, None, :]),
            axis=2,
        )
        select = select.astype(BF16).reshape(groups * cap, pair_dev)
        own_requests = lax.dynamic_slice_in_dim(requests, here, 1, 0)[0]
        own_ranks = lax.dynamic_slice_in_dim(ranks, here, 1, 0)[0]
        row_index = lax.dynamic_slice_in_dim(
            own_requests // pair_dev * cap + own_ranks,
            half * count * nbr_count,
            count * nbr_count,
            0,
        )
    else:
        rounds = window_rounds(groups)

    def gathered(low, part):
        if rounds is None:
            others = swap(low)
            flat = jnp.where(
                half == 0, jnp.concatenate([low, others]), jnp.concatenate([others, low])
            ).reshape(pair_dev, width * width)
            outgoing = jnp.dot(select, flat, preferred_element_type=F32).astype(BF16)
            outgoing = outgoing.reshape(groups, cap, width, width)
            received = lax.all_to_all(outgoing, "pair", split_axis=0, concat_axis=0, tiled=True)
            return [received.reshape(groups * cap, width, width)[row_index]]
        one = lax.ppermute(part, "pair", rounds[0])
        cross = swap(one, 2)
        others = swap(low)
        two = joined(*(lax.ppermute(low, "pair", pairs) for pairs in rounds[1:]), token(one))
        return [low, others, two, swap(two), one, swap(one), cross, swap(cross)]

    for it in range(ITERS):
        out = sweep(
            it == ITERS - 1,
            rounds,
            here_s,
            aux_s,
            orbitals,
            neighbours.T,
            couple.T,
            gathered(low, part),
            intersections,
            exch,
            factor,
            second,
        )
        if it < ITERS - 1:
            low, part = out
    amps, terms = out

    from_below = lax.ppermute(terms[2 * occ_dev :], "pair", down)
    from_above = lax.ppermute(terms[:occ_dev], "pair", up)
    whole, inner = first_terms(here_s, aux_s, orbitals, amps, swap(amps), first)
    density = inner + terms[occ_dev : 2 * occ_dev] + from_below + from_above
    density = (density + swap(density)) / width
    return (whole, density)


def solution(mesh):
    return jax.shard_map(
        shards,
        mesh=mesh,
        in_specs=(
            P(("mol", "pair"), "aux", None),
            P(("mol", "pair"), None, None),
            P(("mol", "pair"), None, None),
            P(("mol", "pair"), None, None, None),
            P(("mol", "pair"), None),
            P(("mol", "pair"), None),
            P(("mol", "pair"), None),
            P(("mol", "pair")),
            P(("mol", "pair"), None),
            P("mol", None),
        ),
        out_specs=(P(("mol", "pair"), None, None), P(("mol", "pair"), None, None)),
        check_vma=False,
    )
```

```python
import functools

import jax
import jax.numpy as jnp
from jax import lax
from jax.experimental import pallas as pl
from jax.experimental.pallas import tpu as pltpu
from jax.sharding import PartitionSpec as P

ITERS = 2
BF16 = jnp.bfloat16
F32 = jnp.float32
VMEM = pl.BlockSpec(memory_space=pltpu.VMEM)
SMEM = pl.BlockSpec(memory_space=pltpu.SMEM)
ANY = pl.BlockSpec(memory_space=pl.ANY)


def params(mib):
    return pltpu.CompilerParams(vmem_limit_bytes=mib * 2**20)


def dot(left, right, dims):
    return lax.dot_general(left, right, (dims, ((), ())), preferred_element_type=F32)


def split(value):
    high = value.astype(BF16)
    return high, (value - high.astype(F32)).astype(BF16)


def square(value):
    high, rest = split(value)
    return dot(
        jnp.concatenate([high, high, rest, rest], axis=1),
        jnp.concatenate([high, rest, high, rest], axis=1),
        ((1,), (1,)),
    )


def cost(flops, size):
    return pl.CostEstimate(flops=flops, bytes_accessed=size, transcendentals=0)


def prepare_kernel(
    aux_ref, occ_ref, used_ref, energy_ref, first_ref, second_ref, ints_ref,
    first_out, second_out, ints_out, factor_ref, sems,
):
    count, width, _ = factor_ref.shape
    half = lax.rem(aux_ref[0], 2)
    rows = pl.ds(half * count, count)
    copies = [
        pltpu.make_async_copy(first_ref.at[rows], first_out, sems.at[0]),
        pltpu.make_async_copy(second_ref.at[rows], second_out, sems.at[1]),
        pltpu.make_async_copy(ints_ref, ints_out, sems.at[2]),
    ]
    for copy in copies:
        copy.start()
    shape = (width, width)
    along = lax.broadcasted_iota(jnp.int32, shape, 1)
    down = lax.broadcasted_iota(jnp.int32, shape, 0)
    for p in range(count):
        row = half * count + p
        energy = jnp.broadcast_to(energy_ref[pl.ds(row, 1)], shape)
        denom = energy.T + energy - occ_ref[0, row] - occ_ref[1, row]
        inside = (along < used_ref[row]) & (down < used_ref[row])
        factor_ref[p] = jnp.where(inside, -1.0 / denom, 0.0)
    for copy in copies:
        copy.wait()


def prepare(aux, occupied, used, energy, first, second, ints):
    pair_dev, width, _ = first.shape
    shape = (pair_dev // 2, width, width)
    return pl.pallas_call(
        prepare_kernel,
        out_shape=(
            jax.ShapeDtypeStruct(shape, BF16),
            jax.ShapeDtypeStruct(shape, BF16),
            jax.ShapeDtypeStruct(ints.shape, BF16),
            jax.ShapeDtypeStruct(shape, F32),
        ),
        in_specs=[SMEM] * 3 + [VMEM] + [ANY] * 3,
        out_specs=(VMEM,) * 4,
        scratch_shapes=[pltpu.SemaphoreType.DMA((3,))],
        compiler_params=params(8),
        cost_estimate=cost(0, 8 * pair_dev * width * width),
        name="prepare",
    )(aux, occupied, used, energy, first, second, ints)


def product_kernel(aux_ref, own_ref, one_ref, two_ref, kept_ref, sent_ref, inner):
    count, _, width = own_ref.shape
    side = lax.rem(aux_ref[0], 2)
    own = jnp.concatenate([own_ref[side], own_ref[1 - side]], axis=1)
    at = 0
    for near_ref in (one_ref, two_ref):
        near = jnp.concatenate([near_ref[i] for i in range(count)], axis=1)
        full = dot(own, near, ((0,), (0,)))
        for j in range(count):
            columns = slice(j * width, (j + 1) * width)
            kept_ref[at : at + width] = full[:width, columns]
            sent_ref[at : at + width] = full[width:, columns]
            at += width
    half = width // 2
    inner[...] = dot(own_ref[0], own_ref[1], ((0,), (0,)))
    kept_ref[at:] = inner[pl.ds(pl.multiple_of(side * half, half), half)]
    sent_ref[at:] = inner[pl.ds(pl.multiple_of((1 - side) * half, half), half)]


def products(aux, ints, one, two):
    count, depth, width = ints.shape
    rows = 2 * count * width + width // 2
    return pl.pallas_call(
        product_kernel,
        out_shape=(jax.ShapeDtypeStruct((rows, width), F32),) * 2,
        in_specs=[SMEM] + [VMEM] * 3,
        out_specs=(VMEM, VMEM),
        scratch_shapes=[pltpu.VMEM((width, width), F32)],
        compiler_params=params(12),
        cost_estimate=cost(18 * depth * width * width, 12 * depth * width),
        name="products",
    )(aux, ints, one, two)


def own_part(aux_ref, low_ref, part_ref):
    count = part_ref.shape[0]
    part_ref[...] = low_ref[pl.ds(lax.rem(aux_ref[0] // 2, 2) * count, count)]


def exchange_kernel(
    here_ref, aux_ref, orbitals_ref, total_ref, far_ref, total_other, far_other,
    first_ref, second_ref, factor_ref, exch_ref, low_ref, part_ref, table,
):
    count, width, _ = exch_ref.shape
    half = lax.rem(aux_ref[0], 2)
    base = here_ref[0] * 2 - 2
    for i, total in (
        (half, total_ref[...].astype(F32) + far_ref[...].astype(F32)),
        (1 - half, total_other[...].astype(F32) + far_other[...].astype(F32)),
    ):
        for at in range(4):
            above = at // 2 == lax.rem(here_ref[0], 2)
            slot = at % 2 + jnp.where(above, 4, 0)
            table[i * 6 + slot] = total[at * width : (at + 1) * width]
        table[3, pl.ds(pl.multiple_of(i * (width // 2), width // 2), width // 2)] = total[4 * width :]
    table[6 + 2] = table[3].T
    for p in range(count):
        row = half * count + p
        slot = (orbitals_ref[0, row] - base - 2) * 6 + orbitals_ref[1, row] - base
        right = second_ref[p]
        left = first_ref[p]
        high, rest = split(table[slot])
        inner = dot(
            jnp.concatenate([high, rest], axis=1),
            jnp.concatenate([right, right], axis=0),
            ((1,), (0,)),
        )
        high, rest = split(inner)
        exch = dot(
            jnp.concatenate([left, left], axis=0),
            jnp.concatenate([high, rest], axis=0),
            ((0,), (0,)),
        )
        exch_ref[p] = exch
        low_ref[p] = (factor_ref[p] * exch).astype(BF16)
    own_part(aux_ref, low_ref, part_ref)


def exchange(here, aux, orbitals, sums, first, second, factor):
    shape = first.shape
    count, width, _ = shape
    return pl.pallas_call(
        exchange_kernel,
        out_shape=(
            jax.ShapeDtypeStruct(shape, F32),
            jax.ShapeDtypeStruct(shape, BF16),
            jax.ShapeDtypeStruct((count // 2, width, width), BF16),
        ),
        in_specs=[SMEM] * 3 + [VMEM] * (len(sums) + 3),
        out_specs=(VMEM,) * 3,
        scratch_shapes=[pltpu.VMEM((12, width, width), F32)],
        compiler_params=params(12),
        cost_estimate=cost(8 * count * width**3, 20 * count * width * width),
        name="exchange",
    )(here, aux, orbitals, *sums, first, second, factor)


def sweep_kernel(last, pieces, rounds, here_ref, aux_ref, orbitals_ref, near_ref, couple_ref, *refs):
    parts = refs[:pieces]
    over_ref, exch_ref, factor_ref, second_ref = refs[pieces : pieces + 4]
    if last:
        amps_ref, terms_ref, one_ref, two_ref, all_terms, table = refs[pieces + 4 :]
    else:
        low_ref, part_ref, table = refs[pieces + 4 :]
    count, width, _ = exch_ref.shape
    pair_dev, nbr_count = over_ref.shape[:2]
    here = here_ref[0]
    half = lax.rem(aux_ref[0], 2)
    at = 0
    for part in parts:
        table[at : at + part.shape[0]] = part[...]
        at += part.shape[0]
    across = lax.rem(aux_ref[0] // 2, 2)
    near_block = -1
    for start, end in rounds[0] if rounds else ():
        near_block = jnp.where(here == end, start, near_block)

    def place(p, n):
        if not rounds:
            return p * nbr_count + n
        wanted = near_ref[n, here * pair_dev + half * count + p]
        owner = wanted // pair_dev
        local = wanted - owner * pair_dev
        side = local // count
        local = local - side * count
        other = jnp.where(side == half, 0, 1)
        quarter = local // (count // 2)
        halved = (
            4 * count
            + jnp.where(quarter == across, 0, count)
            + other * (count // 2)
            + local
            - quarter * (count // 2)
        )
        spot = other * count + local + jnp.where(owner == here, 0, 2 * count)
        return jnp.where(owner == near_block, halved, spot)

    done = []
    for p in range(count):
        row = half * count + p
        halves = []
        for n in range(nbr_count):
            moved = dot(over_ref[row, n], table[place(p, n)], ((1,), (0,)))
            halves.append((couple_ref[n, row] * moved).astype(BF16))
        coupled = dot(
            jnp.concatenate(halves, axis=1),
            jnp.concatenate([over_ref[row, n] for n in range(nbr_count)], axis=1),
            ((1,), (1,)),
        )
        amps = factor_ref[p] * (exch_ref[p] - coupled)
        if last:
            amps_ref[p] = amps
            done.append(amps)
        else:
            low_ref[p] = amps.astype(BF16)
    if not last:
        own_part(aux_ref, low_ref, part_ref)
    else:
        terms = []
        for p in range(count):
            right = second_ref[p]
            high, rest = split(done[p])
            moved = dot(
                jnp.concatenate([right, right], axis=1),
                jnp.concatenate([high, rest], axis=1),
                ((1,), (1,)),
            )
            terms.append(square(moved))
        all_terms[...] = jnp.zeros_like(all_terms)
        for p in range(count):
            spot = orbitals_ref[1, half * count + p] - here * 2 + 2
            all_terms[spot] += terms[p]
        terms_ref[...] = all_terms[2:4]
        below = lax.rem(here, 2) * 4
        one_ref[...] = all_terms[pl.ds(4 - below, 2)].astype(BF16)
        two_ref[...] = all_terms[pl.ds(below, 2)].astype(BF16)


def sweep(last, rounds, here, aux, orbitals, near, couple, parts, over, exch, factor, second):
    count, width, _ = exch.shape
    rows = sum(part.shape[0] for part in parts)
    if last:
        out_shape = (
            jax.ShapeDtypeStruct(exch.shape, F32),
            jax.ShapeDtypeStruct((2, width, width), F32),
            jax.ShapeDtypeStruct((2, width, width), BF16),
            jax.ShapeDtypeStruct((2, width, width), BF16),
        )
        out_specs = (VMEM,) * 4
        scratch = [pltpu.VMEM((6, width, width), F32)]
    else:
        out_shape = (
            jax.ShapeDtypeStruct(exch.shape, BF16),
            jax.ShapeDtypeStruct((count // 2, width, width), BF16),
        )
        out_specs = (VMEM, VMEM)
        scratch = []
    return pl.pallas_call(
        functools.partial(sweep_kernel, last, len(parts), rounds),
        out_shape=out_shape,
        in_specs=[SMEM] * 5 + [VMEM] * (len(parts) + 4),
        out_specs=out_specs,
        scratch_shapes=scratch + [pltpu.VMEM((rows, width, width), BF16)],
        compiler_params=params(16),
        cost_estimate=cost(16 * count * width**3, (rows + 16 * count) * width * width),
        name="last_sweep" if last else "sweep",
    )(here, aux, orbitals, near, couple, *parts, over, exch, factor, second)


def token_kernel(piece_ref, out_ref):
    out_ref[...] = piece_ref[0, :16]


def token(piece):
    return pl.pallas_call(
        token_kernel,
        out_shape=jax.ShapeDtypeStruct((16, piece.shape[-1]), BF16),
        in_specs=[VMEM],
        out_specs=VMEM,
        compiler_params=params(4),
        cost_estimate=cost(5 * 10**9, 2**20),
        name="token",
    )(piece)


def join_kernel(left_ref, right_ref, token_ref, piece_ref, out_ref):
    del token_ref, piece_ref
    out_ref[...] = left_ref[...] + right_ref[...]


def joined(left, right, token, piece):
    return pl.pallas_call(
        join_kernel,
        out_shape=jax.ShapeDtypeStruct(left.shape, BF16),
        in_specs=[VMEM] * 3 + [ANY],
        out_specs=VMEM,
        compiler_params=params(4),
        cost_estimate=cost(left.size, 6 * left.size),
        name="joined",
    )(left, right, token, piece)


def first_kernel(
    here_ref, aux_ref, orbitals_ref, amps_ref, others_ref, first_ref, whole_ref, terms_ref, sems
):
    count = amps_ref.shape[0]
    half = lax.rem(aux_ref[0], 2)
    copies = [
        pltpu.make_async_copy(amps_ref, whole_ref.at[pl.ds(half * count, count)], sems.at[0]),
        pltpu.make_async_copy(others_ref, whole_ref.at[pl.ds((1 - half) * count, count)], sems.at[1]),
    ]
    for copy in copies:
        copy.start()
    terms = []
    for p in range(count):
        high, rest = split(amps_ref[p])
        left = first_ref[p]
        moved = dot(
            jnp.concatenate([left, left], axis=1),
            jnp.concatenate([high, rest], axis=0),
            ((1,), (0,)),
        )
        terms.append(square(moved))
    terms_ref[...] = jnp.zeros_like(terms_ref)
    for p in range(count):
        spot = orbitals_ref[0, half * count + p] - here_ref[0] * 2
        terms_ref[spot] += terms[p]
    for copy in copies:
        copy.wait()


def first_terms(here, aux, orbitals, amps, others, first):
    count, width, _ = amps.shape
    return pl.pallas_call(
        first_kernel,
        out_shape=(
            jax.ShapeDtypeStruct((2 * count, width, width), F32),
            jax.ShapeDtypeStruct((2, width, width), F32),
        ),
        in_specs=[SMEM] * 3 + [VMEM] * 3,
        out_specs=(ANY, VMEM),
        scratch_shapes=[pltpu.SemaphoreType.DMA((2,))],
        compiler_params=params(12),
        cost_estimate=cost(12 * count * width**3, 16 * count * width * width),
        name="first_terms",
    )(here, aux, orbitals, amps, others, first)


def window_rounds(groups):
    edges = []
    for block in range(groups):
        start = min(max(block - 1, 0), groups - 3)
        edges += [(source, block) for source in range(start, start + 3) if source != block]
    edges.sort(key=lambda edge: (-abs(edge[0] - edge[1]), edge))
    first = []
    for source, block in edges:
        if all(source != s and block != d for s, d in first):
            first.append((source, block))
    rest = [edge for edge in edges if edge not in first]
    both = [edge for edge in rest if edge[::-1] in rest]
    rounds = [first, both, [edge for edge in rest if edge not in both]]
    assert len(rounds[0]) == groups
    return rounds


def same_owner_rank(owners):
    count = owners.shape[-1]
    places = jnp.arange(count)
    earlier = places[:, None] > places[None, :]
    same = owners[..., :, None] == owners[..., None, :]
    return jnp.sum(same & earlier, axis=-1)


def shards(
    ints,
    proj_first,
    proj_second,
    intersections,
    couple,
    virt_energy,
    occ_energy,
    pno_count,
    pair_orbitals,
    neighbours,
):
    groups = lax.axis_size("pair")
    here = lax.axis_index("pair")
    aux_count = lax.axis_size("aux")
    aux = lax.axis_index("aux")
    half = aux % 2
    occ_dev, _, width = ints.shape
    pair_dev = proj_first.shape[0]
    nbr_count = couple.shape[1]
    wanted = pair_dev * nbr_count
    cap = 2 * wanted // groups
    count = pair_dev // 2
    partners = [
        [(i, j) for i in range(groups) for j in (i + 1 - 2 * ((i + r) % 2),) if 0 <= j < groups]
        for r in range(2)
    ]
    orbitals = pair_orbitals.T

    def swap(value, step=1):
        return lax.ppermute(value, "aux", [(i, i ^ step) for i in range(aux_count)])

    ints, here_s, aux_s = lax.optimization_barrier((ints, here.reshape(1), aux.reshape(1)))

    near_one, near_two = (lax.ppermute(ints, "pair", pairs) for pairs in partners)
    first, second, ints, factor = prepare(
        aux_s, occ_energy.T, pno_count, virt_energy, proj_first, proj_second, ints
    )
    near_one, first, second, ints, factor = lax.optimization_barrier(
        (near_one, first, second, ints, factor)
    )

    kept, sent = products(aux_s, ints, near_one, near_two)
    total = kept + swap(sent)
    step = 2
    while 2 * step < aux_count:
        total = total + swap(total, step)
        step *= 2
    total = total.astype(BF16)
    far = swap(total, step)
    exch, low, part = exchange(
        here_s, aux_s, orbitals, (total, far, swap(total), swap(far)), first, second, factor
    )

    if cap < pair_dev or groups // 4 != 1 or aux_count != 4:
        rounds = None
        requests = neighbours.reshape(groups, wanted)
        owners = requests // pair_dev
        ranks = same_owner_rank(owners)
        at_home = owners == here
        pick = at_home[:, None, :] & (ranks[:, None, :] == jnp.arange(cap)[None, :, None])
        local = requests % pair_dev
        select = jnp.any(
            pick[..., None]
            & (local[:, None, :, None] == jnp.arange(pair_dev)[None, None, None, :]),
            axis=2,
        )
        select = select.astype(BF16).reshape(groups * cap, pair_dev)
        own_requests = lax.dynamic_slice_in_dim(requests, here, 1, 0)[0]
        own_ranks = lax.dynamic_slice_in_dim(ranks, here, 1, 0)[0]
        row_index = lax.dynamic_slice_in_dim(
            own_requests // pair_dev * cap + own_ranks,
            half * count * nbr_count,
            count * nbr_count,
            0,
        )
    else:
        rounds = window_rounds(groups)

    def gathered(low, part):
        if rounds is None:
            others = swap(low)
            flat = jnp.where(
                half == 0, jnp.concatenate([low, others]), jnp.concatenate([others, low])
            ).reshape(pair_dev, width * width)
            outgoing = jnp.dot(select, flat, preferred_element_type=F32).astype(BF16)
            outgoing = outgoing.reshape(groups, cap, width, width)
            received = lax.all_to_all(outgoing, "pair", split_axis=0, concat_axis=0, tiled=True)
            return [received.reshape(groups * cap, width, width)[row_index]]
        one = lax.ppermute(part, "pair", rounds[0])
        one_other = swap(one)
        cross = swap(one, 2)
        two = (lax.ppermute(low, "pair", pairs) for pairs in rounds[1:])
        two = joined(*two, token(one), one_other)
        return [low, swap(low), two, swap(two), one, one_other, cross, swap(cross)]

    for it in range(ITERS):
        out = sweep(
            it == ITERS - 1,
            rounds,
            here_s,
            aux_s,
            orbitals,
            neighbours.T,
            couple.T,
            gathered(low, part),
            intersections,
            exch,
            factor,
            second,
        )
        if it < ITERS - 1:
            low, part = out
    amps, terms, *sent = out

    near_one, near_two = (
        lax.ppermute(value, "pair", pairs) for value, pairs in zip(sent, partners)
    )
    whole, inner = first_terms(here_s, aux_s, orbitals, amps, swap(amps), first)
    density = inner + terms + near_one.astype(F32) + near_two.astype(F32)
    density = (density + swap(density)) / width
    return (whole, density)


def solution(mesh):
    return jax.shard_map(
        shards,
        mesh=mesh,
        in_specs=(
            P(("mol", "pair"), "aux", None),
            P(("mol", "pair"), None, None),
            P(("mol", "pair"), None, None),
            P(("mol", "pair"), None, None, None),
            P(("mol", "pair"), None),
            P(("mol", "pair"), None),
            P(("mol", "pair"), None),
            P(("mol", "pair")),
            P(("mol", "pair"), None),
            P("mol", None),
        ),
        out_specs=(P(("mol", "pair"), None, None), P(("mol", "pair"), None, None)),
        check_vma=False,
    )
```

```python
import functools

import jax
import jax.numpy as jnp
from jax import lax
from jax.experimental import pallas as pl
from jax.experimental.pallas import tpu as pltpu
from jax.sharding import PartitionSpec as P

ITERS = 2
BF16 = jnp.bfloat16
F32 = jnp.float32
VMEM = pl.BlockSpec(memory_space=pltpu.VMEM)
SMEM = pl.BlockSpec(memory_space=pltpu.SMEM)
ANY = pl.BlockSpec(memory_space=pl.ANY)
HBM = pl.BlockSpec(memory_space=pltpu.HBM)


def params(mib):
    return pltpu.CompilerParams(vmem_limit_bytes=mib * 2**20)


def dot(left, right, dims):
    return lax.dot_general(left, right, (dims, ((), ())), preferred_element_type=F32)


def split(value):
    high = value.astype(BF16)
    return high, (value - high.astype(F32)).astype(BF16)


def square(value):
    high, rest = split(value)
    return dot(
        jnp.concatenate([high, high, rest, rest], axis=1),
        jnp.concatenate([high, rest, high, rest], axis=1),
        ((1,), (1,)),
    )


def cost(flops, size):
    return pl.CostEstimate(flops=flops, bytes_accessed=size, transcendentals=0)


def prepare_kernel(
    aux_ref, occ_ref, used_ref, energy_ref, first_ref, second_ref, ints_ref,
    first_out, second_out, ints_out, factor_ref, sems,
):
    count, width, _ = factor_ref.shape
    half = lax.rem(aux_ref[0], 2)
    rows = pl.ds(half * count, count)
    copies = [
        pltpu.make_async_copy(first_ref.at[rows], first_out, sems.at[0]),
        pltpu.make_async_copy(second_ref.at[rows], second_out, sems.at[1]),
        pltpu.make_async_copy(ints_ref, ints_out, sems.at[2]),
    ]
    for copy in copies:
        copy.start()
    shape = (width, width)
    along = lax.broadcasted_iota(jnp.int32, shape, 1)
    down = lax.broadcasted_iota(jnp.int32, shape, 0)
    for p in range(count):
        row = half * count + p
        energy = jnp.broadcast_to(energy_ref[pl.ds(row, 1)], shape)
        denom = energy.T + energy - occ_ref[0, row] - occ_ref[1, row]
        inside = (along < used_ref[row]) & (down < used_ref[row])
        factor_ref[p] = jnp.where(inside, -1.0 / denom, 0.0)
    for copy in copies:
        copy.wait()


def prepare(aux, occupied, used, energy, first, second, ints):
    pair_dev, width, _ = first.shape
    shape = (pair_dev // 2, width, width)
    return pl.pallas_call(
        prepare_kernel,
        out_shape=(
            jax.ShapeDtypeStruct(shape, BF16),
            jax.ShapeDtypeStruct(shape, BF16),
            jax.ShapeDtypeStruct(ints.shape, BF16),
            jax.ShapeDtypeStruct(shape, F32),
        ),
        in_specs=[SMEM] * 3 + [VMEM] + [HBM] * 3,
        out_specs=(VMEM,) * 4,
        scratch_shapes=[pltpu.SemaphoreType.DMA((3,))],
        compiler_params=params(8),
        cost_estimate=cost(0, 8 * pair_dev * width * width),
        name="prepare",
    )(aux, occupied, used, energy, first, second, ints)


def first_is_lower(here_ref, aux_ref):
    return lax.rem(here_ref[0] + aux_ref[0], 2)


def halves_kernel(here_ref, aux_ref, ints_ref, one_ref, two_ref, sems):
    depth = one_ref.shape[1]
    odd = first_is_lower(here_ref, aux_ref)
    copies = [
        pltpu.make_async_copy(ints_ref.at[:, pl.ds((1 - odd) * depth, depth)], one_ref, sems.at[0]),
        pltpu.make_async_copy(ints_ref.at[:, pl.ds(odd * depth, depth)], two_ref, sems.at[1]),
    ]
    for copy in copies:
        copy.start()
    for copy in copies:
        copy.wait()


def halves(here, aux, ints):
    count, depth, width = ints.shape
    return pl.pallas_call(
        halves_kernel,
        out_shape=(jax.ShapeDtypeStruct((count, depth // 2, width), BF16),) * 2,
        in_specs=[SMEM, SMEM, HBM],
        out_specs=(VMEM, VMEM),
        scratch_shapes=[pltpu.SemaphoreType.DMA((2,))],
        compiler_params=params(4),
        cost_estimate=cost(0, 4 * ints.size),
        name="halves",
    )(here, aux, ints)


def product_kernel(
    here_ref, aux_ref, own_ref, one_ref, two_ref, kept_ref, sent_ref, full_ref, inner_ref
):
    count, _, width = own_ref.shape
    depth = one_ref.shape[1]
    odd = first_is_lower(here_ref, aux_ref)
    side = lax.rem(aux_ref[0], 2)
    rows_each = count * width
    for r, near_ref in enumerate((one_ref, two_ref)):
        lower = odd if r == 0 else 1 - odd
        rows = pl.ds(pl.multiple_of(lower * depth, depth), depth)
        own = jnp.concatenate([own_ref[i, rows] for i in range(count)], axis=1)
        near = jnp.concatenate([near_ref[i] for i in range(count)], axis=1)
        full_ref[...] = dot(
            jnp.where(lower == 1, near, own), jnp.where(lower == 1, own, near), ((0,), (0,))
        )
        for j in range(count):
            columns = slice(j * width, (j + 1) * width)
            for out_ref, i in ((kept_ref, side), (sent_ref, 1 - side)):
                at = pl.multiple_of((r ^ side) * rows_each + j * width, width)
                out_ref[pl.ds(at, width)] = full_ref[
                    pl.ds(pl.multiple_of(i * width, width), width), columns
                ]
    at = 2 * rows_each
    half = width // 2
    inner_ref[...] = dot(own_ref[0], own_ref[1], ((0,), (0,)))
    kept_ref[at:] = inner_ref[pl.ds(pl.multiple_of(side * half, half), half)]
    sent_ref[at:] = inner_ref[pl.ds(pl.multiple_of((1 - side) * half, half), half)]


def products(here, aux, ints, one, two):
    count, depth, width = ints.shape
    rows = 2 * count * width + width // 2
    return pl.pallas_call(
        product_kernel,
        out_shape=(jax.ShapeDtypeStruct((rows, width), F32),) * 2,
        in_specs=[SMEM] * 2 + [VMEM] * 3,
        out_specs=(VMEM, VMEM),
        scratch_shapes=[
            pltpu.VMEM((count * width, count * width), F32),
            pltpu.VMEM((width, width), F32),
        ],
        compiler_params=params(12),
        cost_estimate=cost(10 * depth * width * width, 8 * depth * width),
        name="products",
    )(here, aux, ints, one, two)


def pair_kernel(kept_ref, received_ref, total_ref, one_ref, two_ref):
    total = kept_ref[...] + received_ref[...]
    total_ref[...] = total
    rows = one_ref.shape[0]
    one_ref[...] = total[:rows].astype(BF16)
    two_ref[...] = total[rows : 2 * rows].astype(BF16)


def pair_sum(kept, received, rows):
    part = jax.ShapeDtypeStruct((rows, kept.shape[1]), BF16)
    return pl.pallas_call(
        pair_kernel,
        out_shape=(jax.ShapeDtypeStruct(kept.shape, F32), part, part),
        in_specs=[VMEM] * 2,
        out_specs=(VMEM,) * 3,
        compiler_params=params(4),
        cost_estimate=cost(kept.size, 16 * kept.size),
        name="pair_sum",
    )(kept, received)


def partner_kernel(total_ref, one_ref, two_ref, out_ref):
    rows = one_ref.shape[0]
    out_ref[:rows] = (total_ref[:rows] + one_ref[...].astype(F32)).astype(BF16)
    out_ref[rows : 2 * rows] = (
        total_ref[rows : 2 * rows] + two_ref[...].astype(F32)
    ).astype(BF16)
    out_ref[2 * rows :] = total_ref[2 * rows :].astype(BF16)


def partner_sum(total, one, two):
    return pl.pallas_call(
        partner_kernel,
        out_shape=jax.ShapeDtypeStruct(total.shape, BF16),
        in_specs=[VMEM] * 3,
        out_specs=VMEM,
        compiler_params=params(4),
        cost_estimate=cost(total.size, 8 * total.size),
        name="partner_sum",
    )(total, one, two)


def own_part(aux_ref, low_ref, part_ref):
    count = part_ref.shape[0]
    part_ref[...] = low_ref[pl.ds(lax.rem(aux_ref[0] // 2, 2) * count, count)]


def exchange_kernel(
    here_ref, aux_ref, orbitals_ref, total_ref, far_ref, total_other, far_other,
    first_ref, second_ref, factor_ref, exch_ref, low_ref, part_ref, table,
):
    count, width, _ = exch_ref.shape
    half = lax.rem(aux_ref[0], 2)
    base = here_ref[0] * 2 - 2
    odd = lax.rem(here_ref[0], 2) == 1
    for i, total in (
        (half, total_ref[...].astype(F32) + far_ref[...].astype(F32)),
        (1 - half, total_other[...].astype(F32) + far_other[...].astype(F32)),
    ):
        for j in range(2):
            one = total[j * width : (j + 1) * width]
            two = total[(j + 2) * width : (j + 3) * width]
            table[i * 6 + 4 + j] = jnp.where(odd, two, one)
            table[j * 6 + i] = jnp.where(odd, one, two).T
        table[3, pl.ds(pl.multiple_of(i * (width // 2), width // 2), width // 2)] = total[4 * width :]
    table[6 + 2] = table[3].T
    for p in range(count):
        row = half * count + p
        slot = (orbitals_ref[0, row] - base - 2) * 6 + orbitals_ref[1, row] - base
        right = second_ref[p]
        left = first_ref[p]
        high, rest = split(table[slot])
        inner = dot(
            jnp.concatenate([high, rest], axis=1),
            jnp.concatenate([right, right], axis=0),
            ((1,), (0,)),
        )
        high, rest = split(inner)
        exch = dot(
            jnp.concatenate([left, left], axis=0),
            jnp.concatenate([high, rest], axis=0),
            ((0,), (0,)),
        )
        exch_ref[p] = exch
        low_ref[p] = (factor_ref[p] * exch).astype(BF16)
    own_part(aux_ref, low_ref, part_ref)


def exchange(here, aux, orbitals, sums, first, second, factor):
    shape = first.shape
    count, width, _ = shape
    return pl.pallas_call(
        exchange_kernel,
        out_shape=(
            jax.ShapeDtypeStruct(shape, F32),
            jax.ShapeDtypeStruct(shape, BF16),
            jax.ShapeDtypeStruct((count // 2, width, width), BF16),
        ),
        in_specs=[SMEM] * 3 + [VMEM] * (len(sums) + 3),
        out_specs=(VMEM,) * 3,
        scratch_shapes=[pltpu.VMEM((12, width, width), F32)],
        compiler_params=params(12),
        cost_estimate=cost(8 * count * width**3, 20 * count * width * width),
        name="exchange",
    )(here, aux, orbitals, *sums, first, second, factor)


def sweep_kernel(last, pieces, rounds, here_ref, aux_ref, orbitals_ref, near_ref, couple_ref, *refs):
    parts = refs[:pieces]
    over_ref, exch_ref, factor_ref, second_ref = refs[pieces : pieces + 4]
    if last:
        amps_ref, terms_ref, one_ref, two_ref, all_terms, table = refs[pieces + 4 :]
    else:
        low_ref, part_ref, table = refs[pieces + 4 :]
    count, width, _ = exch_ref.shape
    pair_dev, nbr_count = over_ref.shape[:2]
    here = here_ref[0]
    half = lax.rem(aux_ref[0], 2)
    at = 0
    for part in parts:
        table[at : at + part.shape[0]] = part[...]
        at += part.shape[0]
    across = lax.rem(aux_ref[0] // 2, 2)
    near_block = -1
    for start, end in rounds[0] if rounds else ():
        near_block = jnp.where(here == end, start, near_block)

    def place(p, n):
        if not rounds:
            return p * nbr_count + n
        wanted = near_ref[n, here * pair_dev + half * count + p]
        owner = wanted // pair_dev
        local = wanted - owner * pair_dev
        side = local // count
        local = local - side * count
        other = jnp.where(side == half, 0, 1)
        quarter = local // (count // 2)
        halved = (
            4 * count
            + jnp.where(quarter == across, 0, count)
            + other * (count // 2)
            + local
            - quarter * (count // 2)
        )
        spot = other * count + local + jnp.where(owner == here, 0, 2 * count)
        return jnp.where(owner == near_block, halved, spot)

    done = []
    for p in range(count):
        row = half * count + p
        halves = []
        for n in range(nbr_count):
            moved = dot(over_ref[row, n], table[place(p, n)], ((1,), (0,)))
            halves.append((couple_ref[n, row] * moved).astype(BF16))
        coupled = dot(
            jnp.concatenate(halves, axis=1),
            jnp.concatenate([over_ref[row, n] for n in range(nbr_count)], axis=1),
            ((1,), (1,)),
        )
        amps = factor_ref[p] * (exch_ref[p] - coupled)
        if last:
            amps_ref[p] = amps
            done.append(amps)
        else:
            low_ref[p] = amps.astype(BF16)
    if not last:
        own_part(aux_ref, low_ref, part_ref)
    else:
        terms = []
        for p in range(count):
            right = second_ref[p]
            high, rest = split(done[p])
            moved = dot(
                jnp.concatenate([right, right], axis=1),
                jnp.concatenate([high, rest], axis=1),
                ((1,), (1,)),
            )
            terms.append(square(moved))
        all_terms[...] = jnp.zeros_like(all_terms)
        for p in range(count):
            spot = orbitals_ref[1, half * count + p] - here * 2 + 2
            all_terms[spot] += terms[p]
        terms_ref[...] = all_terms[2:4]
        below = lax.rem(here, 2) * 4
        one_ref[...] = all_terms[pl.ds(4 - below, 2)].astype(BF16)
        two_ref[...] = all_terms[pl.ds(below, 2)].astype(BF16)


def sweep(last, rounds, here, aux, orbitals, near, couple, parts, over, exch, factor, second):
    count, width, _ = exch.shape
    rows = sum(part.shape[0] for part in parts)
    if last:
        out_shape = (
            jax.ShapeDtypeStruct(exch.shape, F32),
            jax.ShapeDtypeStruct((2, width, width), F32),
            jax.ShapeDtypeStruct((2, width, width), BF16),
            jax.ShapeDtypeStruct((2, width, width), BF16),
        )
        out_specs = (VMEM,) * 4
        scratch = [pltpu.VMEM((6, width, width), F32)]
    else:
        out_shape = (
            jax.ShapeDtypeStruct(exch.shape, BF16),
            jax.ShapeDtypeStruct((count // 2, width, width), BF16),
        )
        out_specs = (VMEM, VMEM)
        scratch = []
    return pl.pallas_call(
        functools.partial(sweep_kernel, last, len(parts), rounds),
        out_shape=out_shape,
        in_specs=[SMEM] * 5 + [VMEM] * (len(parts) + 4),
        out_specs=out_specs,
        scratch_shapes=scratch + [pltpu.VMEM((rows, width, width), BF16)],
        compiler_params=params(16),
        cost_estimate=cost(16 * count * width**3, (rows + 16 * count) * width * width),
        name="last_sweep" if last else "sweep",
    )(here, aux, orbitals, near, couple, *parts, over, exch, factor, second)


def token_kernel(piece_ref, out_ref):
    out_ref[...] = piece_ref[0, :16]


def token(piece):
    return pl.pallas_call(
        token_kernel,
        out_shape=jax.ShapeDtypeStruct((16, piece.shape[-1]), BF16),
        in_specs=[VMEM],
        out_specs=VMEM,
        compiler_params=params(4),
        cost_estimate=cost(5 * 10**9, 2**20),
        name="token",
    )(piece)


def join_kernel(left_ref, right_ref, token_ref, piece_ref, out_ref):
    del token_ref, piece_ref
    out_ref[...] = left_ref[...] + right_ref[...]


def joined(left, right, token, piece):
    return pl.pallas_call(
        join_kernel,
        out_shape=jax.ShapeDtypeStruct(left.shape, BF16),
        in_specs=[VMEM] * 3 + [ANY],
        out_specs=VMEM,
        compiler_params=params(4),
        cost_estimate=cost(left.size, 6 * left.size),
        name="joined",
    )(left, right, token, piece)


def first_kernel(
    here_ref, aux_ref, orbitals_ref, amps_ref, others_ref, first_ref, whole_ref, terms_ref, sems
):
    count = amps_ref.shape[0]
    half = lax.rem(aux_ref[0], 2)
    copies = [
        pltpu.make_async_copy(amps_ref, whole_ref.at[pl.ds(half * count, count)], sems.at[0]),
        pltpu.make_async_copy(others_ref, whole_ref.at[pl.ds((1 - half) * count, count)], sems.at[1]),
    ]
    for copy in copies:
        copy.start()
    terms = []
    for p in range(count):
        high, rest = split(amps_ref[p])
        left = first_ref[p]
        moved = dot(
            jnp.concatenate([left, left], axis=1),
            jnp.concatenate([high, rest], axis=0),
            ((1,), (0,)),
        )
        terms.append(square(moved))
    terms_ref[...] = jnp.zeros_like(terms_ref)
    for p in range(count):
        spot = orbitals_ref[0, half * count + p] - here_ref[0] * 2
        terms_ref[spot] += terms[p]
    for copy in copies:
        copy.wait()


def first_terms(here, aux, orbitals, amps, others, first):
    count, width, _ = amps.shape
    return pl.pallas_call(
        first_kernel,
        out_shape=(
            jax.ShapeDtypeStruct((2 * count, width, width), F32),
            jax.ShapeDtypeStruct((2, width, width), F32),
        ),
        in_specs=[SMEM] * 3 + [VMEM] * 3,
        out_specs=(ANY, VMEM),
        scratch_shapes=[pltpu.SemaphoreType.DMA((2,))],
        compiler_params=params(12),
        cost_estimate=cost(12 * count * width**3, 16 * count * width * width),
        name="first_terms",
    )(here, aux, orbitals, amps, others, first)


def window_rounds(groups):
    edges = []
    for block in range(groups):
        start = min(max(block - 1, 0), groups - 3)
        edges += [(source, block) for source in range(start, start + 3) if source != block]
    edges.sort(key=lambda edge: (-abs(edge[0] - edge[1]), edge))
    first = []
    for source, block in edges:
        if all(source != s and block != d for s, d in first):
            first.append((source, block))
    rest = [edge for edge in edges if edge not in first]
    both = [edge for edge in rest if edge[::-1] in rest]
    rounds = [first, both, [edge for edge in rest if edge not in both]]
    assert len(rounds[0]) == groups
    return rounds


def same_owner_rank(owners):
    count = owners.shape[-1]
    places = jnp.arange(count)
    earlier = places[:, None] > places[None, :]
    same = owners[..., :, None] == owners[..., None, :]
    return jnp.sum(same & earlier, axis=-1)


def shards(
    ints,
    proj_first,
    proj_second,
    intersections,
    couple,
    virt_energy,
    occ_energy,
    pno_count,
    pair_orbitals,
    neighbours,
):
    groups = lax.axis_size("pair")
    here = lax.axis_index("pair")
    aux_count = lax.axis_size("aux")
    aux = lax.axis_index("aux")
    half = aux % 2
    occ_dev, _, width = ints.shape
    pair_dev = proj_first.shape[0]
    nbr_count = couple.shape[1]
    wanted = pair_dev * nbr_count
    cap = 2 * wanted // groups
    count = pair_dev // 2
    partners = [
        [(i, j) for i in range(groups) for j in (i + 1 - 2 * ((i + r) % 2),) if 0 <= j < groups]
        for r in range(2)
    ]
    orbitals = pair_orbitals.T

    def swap(value, step=1):
        return lax.ppermute(value, "aux", [(i, i ^ step) for i in range(aux_count)])

    ints, here_s, aux_s = lax.optimization_barrier((ints, here.reshape(1), aux.reshape(1)))

    def both(one, two):
        return [lax.ppermute(one, "pair", partners[0]), lax.ppermute(two, "pair", partners[1])]

    def exchanged(one, two, rounds):
        return [
            lax.ppermute(
                value,
                ("pair", "aux"),
                [
                    (i * aux_count + a, j * aux_count + a)
                    for a in range(aux_count)
                    for i, j in rounds[(r + a) % 2]
                ],
            )
            for r, value in enumerate((one, two))
        ]

    near_one, near_two = exchanged(*halves(here_s, aux_s, ints), partners)
    first, second, ints, factor = prepare(
        aux_s, occ_energy.T, pno_count, virt_energy, proj_first, proj_second, ints
    )
    near_one, first, second, ints, factor = lax.optimization_barrier(
        (near_one, first, second, ints, factor)
    )

    kept, sent = products(here_s, aux_s, ints, near_one, near_two)
    total, *sent = pair_sum(kept, swap(sent), occ_dev * width)
    total = partner_sum(total, *both(*sent))
    step = 2
    while 2 * step < aux_count:
        total = (total.astype(F32) + swap(total, step).astype(F32)).astype(BF16)
        step *= 2
    far = swap(total, step)
    exch, low, part = exchange(
        here_s, aux_s, orbitals, (total, far, swap(total), swap(far)), first, second, factor
    )

    if cap < pair_dev or groups // 4 != 1 or aux_count != 4:
        rounds = None
        requests = neighbours.reshape(groups, wanted)
        owners = requests // pair_dev
        ranks = same_owner_rank(owners)
        at_home = owners == here
        pick = at_home[:, None, :] & (ranks[:, None, :] == jnp.arange(cap)[None, :, None])
        local = requests % pair_dev
        select = jnp.any(
            pick[..., None]
            & (local[:, None, :, None] == jnp.arange(pair_dev)[None, None, None, :]),
            axis=2,
        )
        select = select.astype(BF16).reshape(groups * cap, pair_dev)
        own_requests = lax.dynamic_slice_in_dim(requests, here, 1, 0)[0]
        own_ranks = lax.dynamic_slice_in_dim(ranks, here, 1, 0)[0]
        row_index = lax.dynamic_slice_in_dim(
            own_requests // pair_dev * cap + own_ranks,
            half * count * nbr_count,
            count * nbr_count,
            0,
        )
    else:
        rounds = window_rounds(groups)

    def gathered(low, part):
        if rounds is None:
            others = swap(low)
            flat = jnp.where(
                half == 0, jnp.concatenate([low, others]), jnp.concatenate([others, low])
            ).reshape(pair_dev, width * width)
            outgoing = jnp.dot(select, flat, preferred_element_type=F32).astype(BF16)
            outgoing = outgoing.reshape(groups, cap, width, width)
            received = lax.all_to_all(outgoing, "pair", split_axis=0, concat_axis=0, tiled=True)
            return [received.reshape(groups * cap, width, width)[row_index]]
        one = lax.ppermute(part, "pair", rounds[0])
        one_other = swap(one)
        cross = swap(one, 2)
        two = joined(*exchanged(low, low, rounds[1:]), token(one), one_other)
        return [low, swap(low), two, swap(two), one, one_other, cross, swap(cross)]

    for it in range(ITERS):
        out = sweep(
            it == ITERS - 1,
            rounds,
            here_s,
            aux_s,
            orbitals,
            neighbours.T,
            couple.T,
            gathered(low, part),
            intersections,
            exch,
            factor,
            second,
        )
        if it < ITERS - 1:
            low, part = out
    amps, terms, *sent = out

    near_one, near_two = both(*sent)
    whole, inner = first_terms(here_s, aux_s, orbitals, amps, swap(amps), first)
    density = inner + terms + near_one.astype(F32) + near_two.astype(F32)
    density = (density + swap(density)) / width
    return (whole, density)


def solution(mesh):
    return jax.shard_map(
        shards,
        mesh=mesh,
        in_specs=(
            P(("mol", "pair"), "aux", None),
            P(("mol", "pair"), None, None),
            P(("mol", "pair"), None, None),
            P(("mol", "pair"), None, None, None),
            P(("mol", "pair"), None),
            P(("mol", "pair"), None),
            P(("mol", "pair"), None),
            P(("mol", "pair")),
            P(("mol", "pair"), None),
            P("mol", None),
        ),
        out_specs=(P(("mol", "pair"), None, None), P(("mol", "pair"), None, None)),
        check_vma=False,
    )
```

```python
import functools

import jax
import jax.numpy as jnp
from jax import lax
from jax.experimental import pallas as pl
from jax.experimental.pallas import tpu as pltpu
from jax.sharding import PartitionSpec as P

ITERS = 2
BF16 = jnp.bfloat16
F32 = jnp.float32
VMEM = pl.BlockSpec(memory_space=pltpu.VMEM)
SMEM = pl.BlockSpec(memory_space=pltpu.SMEM)
ANY = pl.BlockSpec(memory_space=pl.ANY)
HBM = pl.BlockSpec(memory_space=pltpu.HBM)


def params(mib):
    return pltpu.CompilerParams(vmem_limit_bytes=mib * 2**20)


def dot(left, right, dims):
    return lax.dot_general(left, right, (dims, ((), ())), preferred_element_type=F32)


def split(value):
    high = value.astype(BF16)
    return high, (value - high.astype(F32)).astype(BF16)


def square(value):
    high, rest = split(value)
    return dot(
        jnp.concatenate([high, high, rest, rest], axis=1),
        jnp.concatenate([high, rest, high, rest], axis=1),
        ((1,), (1,)),
    )


def cost(flops, size):
    return pl.CostEstimate(flops=flops, bytes_accessed=size, transcendentals=0)


def prepare_kernel(
    aux_ref, occ_ref, used_ref, energy_ref, first_ref, second_ref,
    first_out, second_out, factor_ref, sems,
):
    count, width, _ = factor_ref.shape
    half = lax.rem(aux_ref[0], 2)
    rows = pl.ds(half * count, count)
    copies = [
        pltpu.make_async_copy(first_ref.at[rows], first_out, sems.at[0]),
        pltpu.make_async_copy(second_ref.at[rows], second_out, sems.at[1]),
    ]
    for copy in copies:
        copy.start()
    shape = (width, width)
    along = lax.broadcasted_iota(jnp.int32, shape, 1)
    down = lax.broadcasted_iota(jnp.int32, shape, 0)
    for p in range(count):
        row = half * count + p
        energy = jnp.broadcast_to(energy_ref[pl.ds(row, 1)], shape)
        denom = energy.T + energy - occ_ref[0, row] - occ_ref[1, row]
        inside = (along < used_ref[row]) & (down < used_ref[row])
        factor_ref[p] = jnp.where(inside, -1.0 / denom, 0.0)
    for copy in copies:
        copy.wait()


def prepare(aux, occupied, used, energy, first, second):
    pair_dev, width, _ = first.shape
    shape = (pair_dev // 2, width, width)
    return pl.pallas_call(
        prepare_kernel,
        out_shape=(
            jax.ShapeDtypeStruct(shape, BF16),
            jax.ShapeDtypeStruct(shape, BF16),
            jax.ShapeDtypeStruct(shape, F32),
        ),
        in_specs=[SMEM] * 3 + [VMEM] + [HBM] * 2,
        out_specs=(VMEM,) * 3,
        scratch_shapes=[pltpu.SemaphoreType.DMA((2,))],
        compiler_params=params(8),
        cost_estimate=cost(0, 8 * pair_dev * width * width),
        name="prepare",
    )(aux, occupied, used, energy, first, second)


def first_is_lower(here_ref, aux_ref):
    return lax.rem(here_ref[0] + aux_ref[0], 2)


def halves_kernel(here_ref, aux_ref, ints_ref, one_ref, two_ref, sems):
    depth = one_ref.shape[1]
    odd = first_is_lower(here_ref, aux_ref)
    copies = [
        pltpu.make_async_copy(ints_ref.at[:, pl.ds((1 - odd) * depth, depth)], one_ref, sems.at[0]),
        pltpu.make_async_copy(ints_ref.at[:, pl.ds(odd * depth, depth)], two_ref, sems.at[1]),
    ]
    for copy in copies:
        copy.start()
    for copy in copies:
        copy.wait()


def halves(here, aux, ints):
    count, depth, width = ints.shape
    return pl.pallas_call(
        halves_kernel,
        out_shape=(jax.ShapeDtypeStruct((count, depth // 2, width), BF16),) * 2,
        in_specs=[SMEM, SMEM, HBM],
        out_specs=(VMEM, VMEM),
        scratch_shapes=[pltpu.SemaphoreType.DMA((2,))],
        compiler_params=params(4),
        cost_estimate=cost(0, 4 * ints.size),
        name="halves",
    )(here, aux, ints)


PRODUCT, FIRST, SECOND = 4, 5, 6


def index_kernel(
    rounds, here_ref, aux_ref, orbitals_ref, near_ref, couple_ref, index_ref, weight_ref
):
    nbr_count, pair_dev = couple_ref.shape
    count = pair_dev // 2
    here = here_ref[0]
    half = lax.rem(aux_ref[0], 2)
    across = lax.rem(aux_ref[0] // 2, 2)
    near_block = -1
    for start, end in rounds[0] if rounds else ():
        near_block = jnp.where(here == end, start, near_block)

    def place(p, n):
        if not rounds:
            return p * nbr_count + n
        wanted = near_ref[n, here * pair_dev + half * count + p]
        owner = wanted // pair_dev
        local = wanted - owner * pair_dev
        side = local // count
        local = local - side * count
        other = jnp.where(side == half, 0, 1)
        quarter = local // (count // 2)
        halved = (
            4 * count
            + jnp.where(quarter == across, 0, count)
            + other * (count // 2)
            + local
            - quarter * (count // 2)
        )
        spot = other * count + local + jnp.where(owner == here, 0, 2 * count)
        return jnp.where(owner == near_block, halved, spot)

    lane = lax.broadcasted_iota(jnp.int32, (1, index_ref.shape[1]), 1)
    for p in range(count):
        row = half * count + p
        first = orbitals_ref[0, row] - here * 2
        second = orbitals_ref[1, row] - here * 2 + 2
        values = {PRODUCT: first * 6 + second, FIRST: first, SECOND: second}
        values.update((n, place(p, n)) for n in range(nbr_count))
        index_ref[p : p + 1] = sum(jnp.where(lane == at, v, 0) for at, v in values.items())
        weight_ref[p : p + 1] = sum(
            jnp.where(lane == n, couple_ref[n, row], 0.0) for n in range(nbr_count)
        )


def indices(rounds, here, aux, orbitals, near, couple):
    nbr_count, pair_dev = couple.shape
    assert nbr_count <= PRODUCT
    return pl.pallas_call(
        functools.partial(index_kernel, rounds),
        out_shape=(
            jax.ShapeDtypeStruct((pair_dev // 2, 128), jnp.int32),
            jax.ShapeDtypeStruct((pair_dev // 2, 128), F32),
        ),
        in_specs=[SMEM] * 5,
        out_specs=(VMEM, VMEM),
        compiler_params=params(4),
        cost_estimate=cost(10**6, 2**16),
        name="indices",
    )(here, aux, orbitals, near, couple)


def product_kernel(
    here_ref, aux_ref, own_one_ref, own_two_ref, one_ref, two_ref, kept_ref, sent_ref, full_ref,
    inner_ref,
):
    count, _, width = one_ref.shape
    odd = first_is_lower(here_ref, aux_ref)
    side = lax.rem(aux_ref[0], 2)
    rows_each = count * width
    for r, (own_ref, near_ref) in enumerate(((own_two_ref, one_ref), (own_one_ref, two_ref))):
        lower = odd if r == 0 else 1 - odd
        own = jnp.concatenate([own_ref[i] for i in range(count)], axis=1)
        near = jnp.concatenate([near_ref[i] for i in range(count)], axis=1)
        full_ref[...] = dot(
            jnp.where(lower == 1, near, own), jnp.where(lower == 1, own, near), ((0,), (0,))
        )
        for j in range(count):
            columns = slice(j * width, (j + 1) * width)
            for out_ref, i in ((kept_ref, side), (sent_ref, 1 - side)):
                at = pl.multiple_of((r ^ side) * rows_each + j * width, width)
                out_ref[pl.ds(at, width)] = full_ref[
                    pl.ds(pl.multiple_of(i * width, width), width), columns
                ]
    at = 2 * rows_each
    half = width // 2
    inner_ref[...] = dot(own_one_ref[0], own_one_ref[1], ((0,), (0,))) + dot(
        own_two_ref[0], own_two_ref[1], ((0,), (0,))
    )
    kept_ref[at:] = inner_ref[pl.ds(pl.multiple_of(side * half, half), half)]
    sent_ref[at:] = inner_ref[pl.ds(pl.multiple_of((1 - side) * half, half), half)]


def products(here, aux, own_one, own_two, one, two):
    count, depth, width = one.shape
    rows = 2 * count * width + width // 2
    return pl.pallas_call(
        product_kernel,
        out_shape=(jax.ShapeDtypeStruct((rows, width), F32),) * 2,
        in_specs=[SMEM] * 2 + [VMEM] * 4,
        out_specs=(VMEM, VMEM),
        scratch_shapes=[
            pltpu.VMEM((count * width, count * width), F32),
            pltpu.VMEM((width, width), F32),
        ],
        compiler_params=params(12),
        cost_estimate=cost(20 * depth * width * width, 16 * depth * width),
        name="products",
    )(here, aux, own_one, own_two, one, two)


def pair_kernel(kept_ref, received_ref, total_ref, one_ref, two_ref):
    total = kept_ref[...] + received_ref[...]
    total_ref[...] = total
    rows = one_ref.shape[0]
    one_ref[...] = total[:rows].astype(BF16)
    two_ref[...] = total[rows : 2 * rows].astype(BF16)


def pair_sum(kept, received, rows):
    part = jax.ShapeDtypeStruct((rows, kept.shape[1]), BF16)
    return pl.pallas_call(
        pair_kernel,
        out_shape=(jax.ShapeDtypeStruct(kept.shape, F32), part, part),
        in_specs=[VMEM] * 2,
        out_specs=(VMEM,) * 3,
        compiler_params=params(4),
        cost_estimate=cost(kept.size, 16 * kept.size),
        name="pair_sum",
    )(kept, received)


def partner_kernel(total_ref, one_ref, two_ref, out_ref):
    rows = one_ref.shape[0]
    out_ref[:rows] = (total_ref[:rows] + one_ref[...].astype(F32)).astype(BF16)
    out_ref[rows : 2 * rows] = (
        total_ref[rows : 2 * rows] + two_ref[...].astype(F32)
    ).astype(BF16)
    out_ref[2 * rows :] = total_ref[2 * rows :].astype(BF16)


def partner_sum(total, one, two):
    return pl.pallas_call(
        partner_kernel,
        out_shape=jax.ShapeDtypeStruct(total.shape, BF16),
        in_specs=[VMEM] * 3,
        out_specs=VMEM,
        compiler_params=params(4),
        cost_estimate=cost(total.size, 8 * total.size),
        name="partner_sum",
    )(total, one, two)


def own_part(aux_ref, low_ref, part_ref):
    count = part_ref.shape[0]
    part_ref[...] = low_ref[pl.ds(lax.rem(aux_ref[0] // 2, 2) * count, count)]


def exchange_kernel(
    here_ref, aux_ref, index_ref, total_ref, far_ref, total_other, far_other,
    first_ref, second_ref, factor_ref, exch_ref, low_ref, part_ref, table,
):
    count, width, _ = exch_ref.shape
    half = lax.rem(aux_ref[0], 2)
    odd = lax.rem(here_ref[0], 2) == 1
    for i, total in (
        (half, total_ref[...].astype(F32) + far_ref[...].astype(F32)),
        (1 - half, total_other[...].astype(F32) + far_other[...].astype(F32)),
    ):
        for j in range(2):
            one = total[j * width : (j + 1) * width]
            two = total[(j + 2) * width : (j + 3) * width]
            table[i * 6 + 4 + j] = jnp.where(odd, two, one)
            table[j * 6 + i] = jnp.where(odd, one, two).T
        table[3, pl.ds(pl.multiple_of(i * (width // 2), width // 2), width // 2)] = total[4 * width :]
    table[6 + 2] = table[3].T
    for p in range(count):
        right = second_ref[p]
        left = first_ref[p]
        high, rest = split(table[index_ref[p, PRODUCT]])
        inner = dot(
            jnp.concatenate([high, rest], axis=1),
            jnp.concatenate([right, right], axis=0),
            ((1,), (0,)),
        )
        high, rest = split(inner)
        exch = dot(
            jnp.concatenate([left, left], axis=0),
            jnp.concatenate([high, rest], axis=0),
            ((0,), (0,)),
        )
        exch_ref[p] = exch
        low_ref[p] = (factor_ref[p] * exch).astype(BF16)
    own_part(aux_ref, low_ref, part_ref)


def exchange(here, aux, index, sums, first, second, factor):
    shape = first.shape
    count, width, _ = shape
    return pl.pallas_call(
        exchange_kernel,
        out_shape=(
            jax.ShapeDtypeStruct(shape, F32),
            jax.ShapeDtypeStruct(shape, BF16),
            jax.ShapeDtypeStruct((count // 2, width, width), BF16),
        ),
        in_specs=[SMEM] * 2 + [VMEM] * (len(sums) + 4),
        out_specs=(VMEM,) * 3,
        scratch_shapes=[pltpu.VMEM((12, width, width), F32)],
        compiler_params=params(12),
        cost_estimate=cost(8 * count * width**3, 20 * count * width * width),
        name="exchange",
    )(here, aux, index, *sums, first, second, factor)


def sweep_kernel(last, pieces, here_ref, aux_ref, index_ref, weight_ref, *refs):
    parts = refs[:pieces]
    over_ref, exch_ref, factor_ref, second_ref = refs[pieces : pieces + 4]
    if last:
        amps_ref, terms_ref, one_ref, two_ref, all_terms, table = refs[pieces + 4 :]
    else:
        low_ref, part_ref, table = refs[pieces + 4 :]
    count, width, _ = exch_ref.shape
    nbr_count = over_ref.shape[1]
    here = here_ref[0]
    half = lax.rem(aux_ref[0], 2)
    at = 0
    for part in parts:
        table[at : at + part.shape[0]] = part[...]
        at += part.shape[0]
    done = []
    for p in range(count):
        row = half * count + p
        halves = []
        for n in range(nbr_count):
            moved = dot(over_ref[row, n], table[index_ref[p, n]], ((1,), (0,)))
            halves.append((weight_ref[p, n] * moved).astype(BF16))
        coupled = dot(
            jnp.concatenate(halves, axis=1),
            jnp.concatenate([over_ref[row, n] for n in range(nbr_count)], axis=1),
            ((1,), (1,)),
        )
        amps = factor_ref[p] * (exch_ref[p] - coupled)
        if last:
            amps_ref[p] = amps
            done.append(amps)
        else:
            low_ref[p] = amps.astype(BF16)
    if not last:
        own_part(aux_ref, low_ref, part_ref)
    else:
        terms = []
        for p in range(count):
            right = second_ref[p]
            high, rest = split(done[p])
            moved = dot(
                jnp.concatenate([right, right], axis=1),
                jnp.concatenate([high, rest], axis=1),
                ((1,), (1,)),
            )
            terms.append(square(moved))
        all_terms[...] = jnp.zeros_like(all_terms)
        for p in range(count):
            spot = index_ref[p, SECOND]
            all_terms[spot] += terms[p]
        terms_ref[...] = all_terms[2:4]
        below = lax.rem(here, 2) * 4
        one_ref[...] = all_terms[pl.ds(4 - below, 2)].astype(BF16)
        two_ref[...] = all_terms[pl.ds(below, 2)].astype(BF16)


def sweep(last, here, aux, index, weight, parts, over, exch, factor, second):
    count, width, _ = exch.shape
    rows = sum(part.shape[0] for part in parts)
    if last:
        out_shape = (
            jax.ShapeDtypeStruct(exch.shape, F32),
            jax.ShapeDtypeStruct((2, width, width), F32),
            jax.ShapeDtypeStruct((2, width, width), BF16),
            jax.ShapeDtypeStruct((2, width, width), BF16),
        )
        out_specs = (VMEM,) * 4
        scratch = [pltpu.VMEM((6, width, width), F32)]
    else:
        out_shape = (
            jax.ShapeDtypeStruct(exch.shape, BF16),
            jax.ShapeDtypeStruct((count // 2, width, width), BF16),
        )
        out_specs = (VMEM, VMEM)
        scratch = []
    return pl.pallas_call(
        functools.partial(sweep_kernel, last, len(parts)),
        out_shape=out_shape,
        in_specs=[SMEM] * 2 + [VMEM] * (len(parts) + 6),
        out_specs=out_specs,
        scratch_shapes=scratch + [pltpu.VMEM((rows, width, width), BF16)],
        compiler_params=params(16),
        cost_estimate=cost(16 * count * width**3, (rows + 16 * count) * width * width),
        name="last_sweep" if last else "sweep",
    )(here, aux, index, weight, *parts, over, exch, factor, second)


def token_kernel(piece_ref, out_ref):
    out_ref[...] = piece_ref[0, :16]


def token(piece):
    return pl.pallas_call(
        token_kernel,
        out_shape=jax.ShapeDtypeStruct((16, piece.shape[-1]), BF16),
        in_specs=[VMEM],
        out_specs=VMEM,
        compiler_params=params(4),
        cost_estimate=cost(5 * 10**9, 2**20),
        name="token",
    )(piece)


def join_kernel(left_ref, right_ref, token_ref, piece_ref, out_ref):
    del token_ref, piece_ref
    out_ref[...] = left_ref[...] + right_ref[...]


def joined(left, right, token, piece):
    return pl.pallas_call(
        join_kernel,
        out_shape=jax.ShapeDtypeStruct(left.shape, BF16),
        in_specs=[VMEM] * 3 + [ANY],
        out_specs=VMEM,
        compiler_params=params(4),
        cost_estimate=cost(left.size, 6 * left.size),
        name="joined",
    )(left, right, token, piece)


def first_kernel(
    aux_ref, index_ref, amps_ref, others_ref, first_ref, whole_ref, terms_ref, sems
):
    count = amps_ref.shape[0]
    half = lax.rem(aux_ref[0], 2)
    copies = [
        pltpu.make_async_copy(amps_ref, whole_ref.at[pl.ds(half * count, count)], sems.at[0]),
        pltpu.make_async_copy(others_ref, whole_ref.at[pl.ds((1 - half) * count, count)], sems.at[1]),
    ]
    for copy in copies:
        copy.start()
    terms = []
    for p in range(count):
        high, rest = split(amps_ref[p])
        left = first_ref[p]
        moved = dot(
            jnp.concatenate([left, left], axis=1),
            jnp.concatenate([high, rest], axis=0),
            ((1,), (0,)),
        )
        terms.append(square(moved))
    terms_ref[...] = jnp.zeros_like(terms_ref)
    for p in range(count):
        spot = index_ref[p, FIRST]
        terms_ref[spot] += terms[p]
    for copy in copies:
        copy.wait()


def first_terms(aux, index, amps, others, first):
    count, width, _ = amps.shape
    return pl.pallas_call(
        first_kernel,
        out_shape=(
            jax.ShapeDtypeStruct((2 * count, width, width), F32),
            jax.ShapeDtypeStruct((2, width, width), F32),
        ),
        in_specs=[SMEM] + [VMEM] * 4,
        out_specs=(ANY, VMEM),
        scratch_shapes=[pltpu.SemaphoreType.DMA((2,))],
        compiler_params=params(12),
        cost_estimate=cost(12 * count * width**3, 16 * count * width * width),
        name="first_terms",
    )(aux, index, amps, others, first)


def window_rounds(groups):
    edges = []
    for block in range(groups):
        start = min(max(block - 1, 0), groups - 3)
        edges += [(source, block) for source in range(start, start + 3) if source != block]
    edges.sort(key=lambda edge: (-abs(edge[0] - edge[1]), edge))
    first = []
    for source, block in edges:
        if all(source != s and block != d for s, d in first):
            first.append((source, block))
    rest = [edge for edge in edges if edge not in first]
    both = [edge for edge in rest if edge[::-1] in rest]
    rounds = [first, both, [edge for edge in rest if edge not in both]]
    assert len(rounds[0]) == groups
    return rounds


def same_owner_rank(owners):
    count = owners.shape[-1]
    places = jnp.arange(count)
    earlier = places[:, None] > places[None, :]
    same = owners[..., :, None] == owners[..., None, :]
    return jnp.sum(same & earlier, axis=-1)


def shards(
    ints,
    proj_first,
    proj_second,
    intersections,
    couple,
    virt_energy,
    occ_energy,
    pno_count,
    pair_orbitals,
    neighbours,
):
    groups = lax.axis_size("pair")
    here = lax.axis_index("pair")
    aux_count = lax.axis_size("aux")
    aux = lax.axis_index("aux")
    half = aux % 2
    occ_dev, _, width = ints.shape
    pair_dev = proj_first.shape[0]
    nbr_count = couple.shape[1]
    wanted = pair_dev * nbr_count
    cap = 2 * wanted // groups
    count = pair_dev // 2
    partners = [
        [(i, j) for i in range(groups) for j in (i + 1 - 2 * ((i + r) % 2),) if 0 <= j < groups]
        for r in range(2)
    ]

    def swap(value, step=1):
        return lax.ppermute(value, "aux", [(i, i ^ step) for i in range(aux_count)])

    ints, here_s, aux_s = lax.optimization_barrier((ints, here.reshape(1), aux.reshape(1)))

    def both(one, two):
        return [lax.ppermute(one, "pair", partners[0]), lax.ppermute(two, "pair", partners[1])]

    def exchanged(one, two, rounds):
        return [
            lax.ppermute(
                value,
                ("pair", "aux"),
                [
                    (i * aux_count + a, j * aux_count + a)
                    for a in range(aux_count)
                    for i, j in rounds[(r + a) % 2]
                ],
            )
            for r, value in enumerate((one, two))
        ]

    own_halves = halves(here_s, aux_s, ints)
    near_one, near_two = exchanged(*own_halves, partners)
    first, second, factor = prepare(
        aux_s, occ_energy.T, pno_count, virt_energy, proj_first, proj_second
    )
    near_one, first, second, factor = lax.optimization_barrier((near_one, first, second, factor))

    if cap < pair_dev or groups // 4 != 1 or aux_count != 4:
        rounds = None
        requests = neighbours.reshape(groups, wanted)
        owners = requests // pair_dev
        ranks = same_owner_rank(owners)
        at_home = owners == here
        pick = at_home[:, None, :] & (ranks[:, None, :] == jnp.arange(cap)[None, :, None])
        local = requests % pair_dev
        select = jnp.any(
            pick[..., None]
            & (local[:, None, :, None] == jnp.arange(pair_dev)[None, None, None, :]),
            axis=2,
        )
        select = select.astype(BF16).reshape(groups * cap, pair_dev)
        own_requests = lax.dynamic_slice_in_dim(requests, here, 1, 0)[0]
        own_ranks = lax.dynamic_slice_in_dim(ranks, here, 1, 0)[0]
        row_index = lax.dynamic_slice_in_dim(
            own_requests // pair_dev * cap + own_ranks,
            half * count * nbr_count,
            count * nbr_count,
            0,
        )
    else:
        rounds = window_rounds(groups)
    index, weight = indices(rounds, here_s, aux_s, pair_orbitals.T, neighbours.T, couple.T)

    kept, sent = products(here_s, aux_s, *own_halves, near_one, near_two)
    total, *sent = pair_sum(kept, swap(sent), occ_dev * width)
    total = partner_sum(total, *both(*sent))
    step = 2
    while 2 * step < aux_count:
        total = (total.astype(F32) + swap(total, step).astype(F32)).astype(BF16)
        step *= 2
    far = swap(total, step)
    exch, low, part = exchange(
        here_s, aux_s, index, (total, far, swap(total), swap(far)), first, second, factor
    )

    def gathered(low, part):
        if rounds is None:
            others = swap(low)
            flat = jnp.where(
                half == 0, jnp.concatenate([low, others]), jnp.concatenate([others, low])
            ).reshape(pair_dev, width * width)
            outgoing = jnp.dot(select, flat, preferred_element_type=F32).astype(BF16)
            outgoing = outgoing.reshape(groups, cap, width, width)
            received = lax.all_to_all(outgoing, "pair", split_axis=0, concat_axis=0, tiled=True)
            return [received.reshape(groups * cap, width, width)[row_index]]
        one = lax.ppermute(part, "pair", rounds[0])
        one_other = swap(one)
        cross = swap(one, 2)
        two = joined(*exchanged(low, low, rounds[1:]), token(one), one_other)
        return [low, swap(low), two, swap(two), one, one_other, cross, swap(cross)]

    for it in range(ITERS):
        out = sweep(
            it == ITERS - 1,
            here_s,
            aux_s,
            index,
            weight,
            gathered(low, part),
            intersections,
            exch,
            factor,
            second,
        )
        if it < ITERS - 1:
            low, part = out
    amps, terms, *sent = out

    near_one, near_two = both(*sent)
    whole, inner = first_terms(aux_s, index, amps, swap(amps), first)
    density = inner + terms + near_one.astype(F32) + near_two.astype(F32)
    density = (density + swap(density)) / width
    return (whole, density)


def solution(mesh):
    return jax.shard_map(
        shards,
        mesh=mesh,
        in_specs=(
            P(("mol", "pair"), "aux", None),
            P(("mol", "pair"), None, None),
            P(("mol", "pair"), None, None),
            P(("mol", "pair"), None, None, None),
            P(("mol", "pair"), None),
            P(("mol", "pair"), None),
            P(("mol", "pair"), None),
            P(("mol", "pair")),
            P(("mol", "pair"), None),
            P("mol", None),
        ),
        out_specs=(P(("mol", "pair"), None, None), P(("mol", "pair"), None, None)),
        check_vma=False,
    )
```

```python
import functools

import jax
import jax.numpy as jnp
from jax import lax
from jax.experimental import pallas as pl
from jax.experimental.pallas import tpu as pltpu
from jax.sharding import PartitionSpec as P

ITERS = 2
BF16 = jnp.bfloat16
F32 = jnp.float32
VMEM = pl.BlockSpec(memory_space=pltpu.VMEM)
SMEM = pl.BlockSpec(memory_space=pltpu.SMEM)
ANY = pl.BlockSpec(memory_space=pl.ANY)
HBM = pl.BlockSpec(memory_space=pltpu.HBM)


def params(mib):
    return pltpu.CompilerParams(vmem_limit_bytes=mib * 2**20)


def dot(left, right, dims):
    return lax.dot_general(left, right, (dims, ((), ())), preferred_element_type=F32)


def split(value):
    high = value.astype(BF16)
    return high, (value - high.astype(F32)).astype(BF16)


def square(value):
    high, rest = split(value)
    return dot(
        jnp.concatenate([high, high, rest, rest], axis=1),
        jnp.concatenate([high, rest, high, rest], axis=1),
        ((1,), (1,)),
    )


def cost(flops, size):
    return pl.CostEstimate(flops=flops, bytes_accessed=size, transcendentals=0)


def prepare_kernel(
    aux_ref, occ_ref, used_ref, energy_ref, first_ref, second_ref, ints_ref,
    first_out, second_out, ints_out, factor_ref, sems,
):
    count, width, _ = factor_ref.shape
    half = lax.rem(aux_ref[0], 2)
    rows = pl.ds(half * count, count)
    copies = [
        pltpu.make_async_copy(first_ref.at[rows], first_out, sems.at[0]),
        pltpu.make_async_copy(second_ref.at[rows], second_out, sems.at[1]),
        pltpu.make_async_copy(ints_ref, ints_out, sems.at[2]),
    ]
    for copy in copies:
        copy.start()
    shape = (width, width)
    along = lax.broadcasted_iota(jnp.int32, shape, 1)
    down = lax.broadcasted_iota(jnp.int32, shape, 0)
    for p in range(count):
        row = half * count + p
        energy = jnp.broadcast_to(energy_ref[pl.ds(row, 1)], shape)
        denom = energy.T + energy - occ_ref[0, row] - occ_ref[1, row]
        inside = (along < used_ref[row]) & (down < used_ref[row])
        factor_ref[p] = jnp.where(inside, -1.0 / denom, 0.0)
    for copy in copies:
        copy.wait()


def prepare(aux, occupied, used, energy, first, second, ints):
    pair_dev, width, _ = first.shape
    shape = (pair_dev // 2, width, width)
    return pl.pallas_call(
        prepare_kernel,
        out_shape=(
            jax.ShapeDtypeStruct(shape, BF16),
            jax.ShapeDtypeStruct(shape, BF16),
            jax.ShapeDtypeStruct(ints.shape, BF16),
            jax.ShapeDtypeStruct(shape, F32),
        ),
        in_specs=[SMEM] * 3 + [VMEM] + [HBM] * 3,
        out_specs=(VMEM,) * 4,
        scratch_shapes=[pltpu.SemaphoreType.DMA((3,))],
        compiler_params=params(8),
        cost_estimate=cost(0, 8 * pair_dev * width * width),
        name="prepare",
    )(aux, occupied, used, energy, first, second, ints)


PRODUCT, FIRST, SECOND = 4, 5, 6


def index_kernel(
    rounds, here_ref, aux_ref, orbitals_ref, near_ref, couple_ref, index_ref, weight_ref
):
    nbr_count, pair_dev = couple_ref.shape
    count = pair_dev // 2
    here = here_ref[0]
    half = lax.rem(aux_ref[0], 2)
    across = lax.rem(aux_ref[0] // 2, 2)
    near_block = -1
    for start, end in rounds[0] if rounds else ():
        near_block = jnp.where(here == end, start, near_block)

    def place(p, n):
        if not rounds:
            return p * nbr_count + n
        wanted = near_ref[n, here * pair_dev + half * count + p]
        owner = wanted // pair_dev
        local = wanted - owner * pair_dev
        side = local // count
        local = local - side * count
        other = jnp.where(side == half, 0, 1)
        quarter = local // (count // 2)
        halved = (
            4 * count
            + jnp.where(quarter == across, 0, count)
            + other * (count // 2)
            + local
            - quarter * (count // 2)
        )
        spot = other * count + local + jnp.where(owner == here, 0, 2 * count)
        return jnp.where(owner == near_block, halved, spot)

    lane = lax.broadcasted_iota(jnp.int32, (1, index_ref.shape[1]), 1)
    for p in range(count):
        row = half * count + p
        first = orbitals_ref[0, row] - here * 2
        second = orbitals_ref[1, row] - here * 2 + 2
        values = {PRODUCT: first * 6 + second, FIRST: first, SECOND: second}
        values.update((n, place(p, n)) for n in range(nbr_count))
        index_ref[p : p + 1] = sum(jnp.where(lane == at, v, 0) for at, v in values.items())
        weight_ref[p : p + 1] = sum(
            jnp.where(lane == n, couple_ref[n, row], 0.0) for n in range(nbr_count)
        )


def indices(rounds, here, aux, orbitals, near, couple):
    nbr_count, pair_dev = couple.shape
    assert nbr_count <= PRODUCT
    return pl.pallas_call(
        functools.partial(index_kernel, rounds),
        out_shape=(
            jax.ShapeDtypeStruct((pair_dev // 2, 128), jnp.int32),
            jax.ShapeDtypeStruct((pair_dev // 2, 128), F32),
        ),
        in_specs=[SMEM] * 5,
        out_specs=(VMEM, VMEM),
        compiler_params=params(4),
        cost_estimate=cost(10**6, 2**16),
        name="indices",
    )(here, aux, orbitals, near, couple)


def product_kernel(aux_ref, own_ref, near_ref, total_ref, sent_ref):
    count, _, width = own_ref.shape
    second = lax.rem(aux_ref[0], 2) == 1
    own = jnp.concatenate([own_ref[i] for i in range(count)], axis=1)
    near = jnp.concatenate([near_ref[i] for i in range(count)], axis=1)
    full = dot(jnp.where(second, near, own), jnp.where(second, own, near), ((0,), (0,)))
    at = 0
    for i in range(count):
        for j in range(count):
            block = full[i * width : (i + 1) * width, j * width : (j + 1) * width]
            total_ref[at : at + width] = block
            sent_ref[at : at + width] = block.astype(BF16)
            at += width
    total_ref[at:] = dot(own_ref[0], own_ref[1], ((0,), (0,)))


def products(aux, ints, near):
    count, depth, width = ints.shape
    rows = count * count * width
    return pl.pallas_call(
        product_kernel,
        out_shape=(
            jax.ShapeDtypeStruct((rows + width, width), F32),
            jax.ShapeDtypeStruct((rows, width), BF16),
        ),
        in_specs=[SMEM] + [VMEM] * 2,
        out_specs=(VMEM, VMEM),
        compiler_params=params(12),
        cost_estimate=cost(10 * depth * width * width, 8 * depth * width),
        name="products",
    )(aux, ints, near)


def partner_kernel(total_ref, received_ref, out_ref):
    rows = received_ref.shape[0]
    out_ref[:rows] = (total_ref[:rows] + received_ref[...].astype(F32)).astype(BF16)
    out_ref[rows:] = total_ref[rows:].astype(BF16)


def partner_sum(total, received):
    return pl.pallas_call(
        partner_kernel,
        out_shape=jax.ShapeDtypeStruct(total.shape, BF16),
        in_specs=[VMEM] * 2,
        out_specs=VMEM,
        compiler_params=params(4),
        cost_estimate=cost(total.size, 8 * total.size),
        name="partner_sum",
    )(total, received)


def own_part(aux_ref, low_ref, part_ref):
    count = part_ref.shape[0]
    part_ref[...] = low_ref[pl.ds(lax.rem(aux_ref[0] // 2, 2) * count, count)]


def exchange_kernel(
    aux_ref, index_ref, total_ref, far_ref, total_other, far_other,
    first_ref, second_ref, factor_ref, exch_ref, low_ref, part_ref, table,
):
    count, width, _ = exch_ref.shape
    second = lax.rem(aux_ref[0], 2) == 1
    mine = total_ref[...].astype(F32) + far_ref[...].astype(F32)
    others = total_other[...].astype(F32) + far_other[...].astype(F32)
    for i in range(2):
        for j in range(2):
            at = (2 * i + j) * width
            one = mine[at : at + width]
            two = others[at : at + width]
            table[i * 6 + 4 + j] = jnp.where(second, two, one)
            table[j * 6 + i] = jnp.where(second, one, two).T
    inner = mine[4 * width :] + others[4 * width :]
    table[3] = inner
    table[6 + 2] = inner.T
    for p in range(count):
        right = second_ref[p]
        left = first_ref[p]
        high, rest = split(table[index_ref[p, PRODUCT]])
        inner = dot(
            jnp.concatenate([high, rest], axis=1),
            jnp.concatenate([right, right], axis=0),
            ((1,), (0,)),
        )
        high, rest = split(inner)
        exch = dot(
            jnp.concatenate([left, left], axis=0),
            jnp.concatenate([high, rest], axis=0),
            ((0,), (0,)),
        )
        exch_ref[p] = exch
        low_ref[p] = (factor_ref[p] * exch).astype(BF16)
    own_part(aux_ref, low_ref, part_ref)


def exchange(aux, index, sums, first, second, factor):
    shape = first.shape
    count, width, _ = shape
    return pl.pallas_call(
        exchange_kernel,
        out_shape=(
            jax.ShapeDtypeStruct(shape, F32),
            jax.ShapeDtypeStruct(shape, BF16),
            jax.ShapeDtypeStruct((count // 2, width, width), BF16),
        ),
        in_specs=[SMEM] + [VMEM] * (len(sums) + 4),
        out_specs=(VMEM,) * 3,
        scratch_shapes=[pltpu.VMEM((12, width, width), F32)],
        compiler_params=params(12),
        cost_estimate=cost(8 * count * width**3, 20 * count * width * width),
        name="exchange",
    )(aux, index, *sums, first, second, factor)


def sweep_kernel(last, pieces, here_ref, aux_ref, index_ref, weight_ref, *refs):
    parts = refs[:pieces]
    over_ref, exch_ref, factor_ref, second_ref = refs[pieces : pieces + 4]
    if last:
        amps_ref, terms_ref, one_ref, two_ref, all_terms, table = refs[pieces + 4 :]
    else:
        low_ref, part_ref, table = refs[pieces + 4 :]
    count, width, _ = exch_ref.shape
    nbr_count = over_ref.shape[1]
    here = here_ref[0]
    half = lax.rem(aux_ref[0], 2)
    at = 0
    for part in parts:
        table[at : at + part.shape[0]] = part[...]
        at += part.shape[0]
    done = []
    for p in range(count):
        row = half * count + p
        halves = []
        for n in range(nbr_count):
            moved = dot(over_ref[row, n], table[index_ref[p, n]], ((1,), (0,)))
            halves.append((weight_ref[p, n] * moved).astype(BF16))
        coupled = dot(
            jnp.concatenate(halves, axis=1),
            jnp.concatenate([over_ref[row, n] for n in range(nbr_count)], axis=1),
            ((1,), (1,)),
        )
        amps = factor_ref[p] * (exch_ref[p] - coupled)
        if last:
            amps_ref[p] = amps
            done.append(amps)
        else:
            low_ref[p] = amps.astype(BF16)
    if not last:
        own_part(aux_ref, low_ref, part_ref)
    else:
        terms = []
        for p in range(count):
            right = second_ref[p]
            high, rest = split(done[p])
            moved = dot(
                jnp.concatenate([right, right], axis=1),
                jnp.concatenate([high, rest], axis=1),
                ((1,), (1,)),
            )
            terms.append(square(moved))
        all_terms[...] = jnp.zeros_like(all_terms)
        for p in range(count):
            spot = index_ref[p, SECOND]
            all_terms[spot] += terms[p]
        terms_ref[...] = all_terms[2:4]
        below = lax.rem(here, 2) * 4
        one_ref[...] = all_terms[pl.ds(4 - below, 2)].astype(BF16)
        two_ref[...] = all_terms[pl.ds(below, 2)].astype(BF16)


def sweep(last, here, aux, index, weight, parts, over, exch, factor, second):
    count, width, _ = exch.shape
    rows = sum(part.shape[0] for part in parts)
    if last:
        out_shape = (
            jax.ShapeDtypeStruct(exch.shape, F32),
            jax.ShapeDtypeStruct((2, width, width), F32),
            jax.ShapeDtypeStruct((2, width, width), BF16),
            jax.ShapeDtypeStruct((2, width, width), BF16),
        )
        out_specs = (VMEM,) * 4
        scratch = [pltpu.VMEM((6, width, width), F32)]
    else:
        out_shape = (
            jax.ShapeDtypeStruct(exch.shape, BF16),
            jax.ShapeDtypeStruct((count // 2, width, width), BF16),
        )
        out_specs = (VMEM, VMEM)
        scratch = []
    return pl.pallas_call(
        functools.partial(sweep_kernel, last, len(parts)),
        out_shape=out_shape,
        in_specs=[SMEM] * 2 + [VMEM] * (len(parts) + 6),
        out_specs=out_specs,
        scratch_shapes=scratch + [pltpu.VMEM((rows, width, width), BF16)],
        compiler_params=params(16),
        cost_estimate=cost(16 * count * width**3, (rows + 16 * count) * width * width),
        name="last_sweep" if last else "sweep",
    )(here, aux, index, weight, *parts, over, exch, factor, second)


def token_kernel(piece_ref, out_ref):
    out_ref[...] = piece_ref[0, :16]


def token(piece):
    return pl.pallas_call(
        token_kernel,
        out_shape=jax.ShapeDtypeStruct((16, piece.shape[-1]), BF16),
        in_specs=[VMEM],
        out_specs=VMEM,
        compiler_params=params(4),
        cost_estimate=cost(5 * 10**9, 2**20),
        name="token",
    )(piece)


def join_kernel(left_ref, right_ref, token_ref, piece_ref, out_ref):
    del token_ref, piece_ref
    out_ref[...] = left_ref[...] + right_ref[...]


def joined(left, right, token, piece):
    return pl.pallas_call(
        join_kernel,
        out_shape=jax.ShapeDtypeStruct(left.shape, BF16),
        in_specs=[VMEM] * 3 + [ANY],
        out_specs=VMEM,
        compiler_params=params(4),
        cost_estimate=cost(left.size, 6 * left.size),
        name="joined",
    )(left, right, token, piece)


def first_kernel(
    aux_ref, index_ref, amps_ref, others_ref, first_ref, whole_ref, terms_ref, sems
):
    count = amps_ref.shape[0]
    half = lax.rem(aux_ref[0], 2)
    copies = [
        pltpu.make_async_copy(amps_ref, whole_ref.at[pl.ds(half * count, count)], sems.at[0]),
        pltpu.make_async_copy(others_ref, whole_ref.at[pl.ds((1 - half) * count, count)], sems.at[1]),
    ]
    for copy in copies:
        copy.start()
    terms = []
    for p in range(count):
        high, rest = split(amps_ref[p])
        left = first_ref[p]
        moved = dot(
            jnp.concatenate([left, left], axis=1),
            jnp.concatenate([high, rest], axis=0),
            ((1,), (0,)),
        )
        terms.append(square(moved))
    terms_ref[...] = jnp.zeros_like(terms_ref)
    for p in range(count):
        spot = index_ref[p, FIRST]
        terms_ref[spot] += terms[p]
    for copy in copies:
        copy.wait()


def first_terms(aux, index, amps, others, first):
    count, width, _ = amps.shape
    return pl.pallas_call(
        first_kernel,
        out_shape=(
            jax.ShapeDtypeStruct((2 * count, width, width), F32),
            jax.ShapeDtypeStruct((2, width, width), F32),
        ),
        in_specs=[SMEM] + [VMEM] * 4,
        out_specs=(ANY, VMEM),
        scratch_shapes=[pltpu.SemaphoreType.DMA((2,))],
        compiler_params=params(12),
        cost_estimate=cost(12 * count * width**3, 16 * count * width * width),
        name="first_terms",
    )(aux, index, amps, others, first)


def window_rounds(groups):
    edges = []
    for block in range(groups):
        start = min(max(block - 1, 0), groups - 3)
        edges += [(source, block) for source in range(start, start + 3) if source != block]
    edges.sort(key=lambda edge: (-abs(edge[0] - edge[1]), edge))
    first = []
    for source, block in edges:
        if all(source != s and block != d for s, d in first):
            first.append((source, block))
    rest = [edge for edge in edges if edge not in first]
    both = [edge for edge in rest if edge[::-1] in rest]
    rounds = [first, both, [edge for edge in rest if edge not in both]]
    assert len(rounds[0]) == groups
    return rounds


def same_owner_rank(owners):
    count = owners.shape[-1]
    places = jnp.arange(count)
    earlier = places[:, None] > places[None, :]
    same = owners[..., :, None] == owners[..., None, :]
    return jnp.sum(same & earlier, axis=-1)


def shards(
    ints,
    proj_first,
    proj_second,
    intersections,
    couple,
    virt_energy,
    occ_energy,
    pno_count,
    pair_orbitals,
    neighbours,
):
    groups = lax.axis_size("pair")
    here = lax.axis_index("pair")
    aux_count = lax.axis_size("aux")
    aux = lax.axis_index("aux")
    half = aux % 2
    occ_dev, _, width = ints.shape
    pair_dev = proj_first.shape[0]
    nbr_count = couple.shape[1]
    wanted = pair_dev * nbr_count
    cap = 2 * wanted // groups
    count = pair_dev // 2
    partners = [
        [(i, j) for i in range(groups) for j in (i + 1 - 2 * ((i + r) % 2),) if 0 <= j < groups]
        for r in range(2)
    ]

    def swap(value, step=1):
        return lax.ppermute(value, "aux", [(i, i ^ step) for i in range(aux_count)])

    ints, here_s, aux_s = lax.optimization_barrier((ints, here.reshape(1), aux.reshape(1)))

    def both(one, two):
        return [lax.ppermute(one, "pair", partners[0]), lax.ppermute(two, "pair", partners[1])]

    def exchanged(one, two, rounds):
        return [
            lax.ppermute(
                value,
                ("pair", "aux"),
                [
                    (i * aux_count + a, j * aux_count + a)
                    for a in range(aux_count)
                    for i, j in rounds[(r + a) % 2]
                ],
            )
            for r, value in enumerate((one, two))
        ]

    def joint(rounds):
        return [
            (i * aux_count + a, j * aux_count + (a ^ turn))
            for a in range(aux_count)
            for i, j, turn in rounds[a % 2]
        ]

    near = lax.ppermute(
        ints,
        ("pair", "aux"),
        joint(
            [
                [(i + 1, i, 0) for i in range(groups - 1)],
                [(i, i + 1, 0) for i in range(groups - 1)],
            ]
        ),
    )
    first, second, ints, factor = prepare(
        aux_s, occ_energy.T, pno_count, virt_energy, proj_first, proj_second, ints
    )
    near, first, second, ints, factor = lax.optimization_barrier(
        (near, first, second, ints, factor)
    )

    if cap < pair_dev or groups // 4 != 1 or aux_count != 4:
        rounds = None
        requests = neighbours.reshape(groups, wanted)
        owners = requests // pair_dev
        ranks = same_owner_rank(owners)
        at_home = owners == here
        pick = at_home[:, None, :] & (ranks[:, None, :] == jnp.arange(cap)[None, :, None])
        local = requests % pair_dev
        select = jnp.any(
            pick[..., None]
            & (local[:, None, :, None] == jnp.arange(pair_dev)[None, None, None, :]),
            axis=2,
        )
        select = select.astype(BF16).reshape(groups * cap, pair_dev)
        own_requests = lax.dynamic_slice_in_dim(requests, here, 1, 0)[0]
        own_ranks = lax.dynamic_slice_in_dim(ranks, here, 1, 0)[0]
        row_index = lax.dynamic_slice_in_dim(
            own_requests // pair_dev * cap + own_ranks,
            half * count * nbr_count,
            count * nbr_count,
            0,
        )
    else:
        rounds = window_rounds(groups)
    index, weight = indices(rounds, here_s, aux_s, pair_orbitals.T, neighbours.T, couple.T)

    total, sent = products(aux_s, ints, near)
    received = lax.ppermute(
        sent,
        ("pair", "aux"),
        joint(
            [
                [(i, i + 1, 1) for i in range(groups - 1)],
                [(i + 1, i, 1) for i in range(groups - 1)],
            ]
        ),
    )
    total = partner_sum(total, received)
    step = 2
    while 2 * step < aux_count:
        total = (total.astype(F32) + swap(total, step).astype(F32)).astype(BF16)
        step *= 2
    far = swap(total, step)
    exch, low, part = exchange(
        aux_s, index, (total, far, swap(total), swap(far)), first, second, factor
    )

    def gathered(low, part):
        if rounds is None:
            others = swap(low)
            flat = jnp.where(
                half == 0, jnp.concatenate([low, others]), jnp.concatenate([others, low])
            ).reshape(pair_dev, width * width)
            outgoing = jnp.dot(select, flat, preferred_element_type=F32).astype(BF16)
            outgoing = outgoing.reshape(groups, cap, width, width)
            received = lax.all_to_all(outgoing, "pair", split_axis=0, concat_axis=0, tiled=True)
            return [received.reshape(groups * cap, width, width)[row_index]]
        one = lax.ppermute(part, "pair", rounds[0])
        one_other = swap(one)
        cross = swap(one, 2)
        two = joined(*exchanged(low, low, rounds[1:]), token(one), one_other)
        return [low, swap(low), two, swap(two), one, one_other, cross, swap(cross)]

    for it in range(ITERS):
        out = sweep(
            it == ITERS - 1,
            here_s,
            aux_s,
            index,
            weight,
            gathered(low, part),
            intersections,
            exch,
            factor,
            second,
        )
        if it < ITERS - 1:
            low, part = out
    amps, terms, *sent = out

    near_one, near_two = both(*sent)
    whole, inner = first_terms(aux_s, index, amps, swap(amps), first)
    density = inner + terms + near_one.astype(F32) + near_two.astype(F32)
    density = (density + swap(density)) / width
    return (whole, density)


def solution(mesh):
    return jax.shard_map(
        shards,
        mesh=mesh,
        in_specs=(
            P(("mol", "pair"), "aux", None),
            P(("mol", "pair"), None, None),
            P(("mol", "pair"), None, None),
            P(("mol", "pair"), None, None, None),
            P(("mol", "pair"), None),
            P(("mol", "pair"), None),
            P(("mol", "pair"), None),
            P(("mol", "pair")),
            P(("mol", "pair"), None),
            P("mol", None),
        ),
        out_specs=(P(("mol", "pair"), None, None), P(("mol", "pair"), None, None)),
        check_vma=False,
    )
```

```python
import functools

import jax
import jax.numpy as jnp
from jax import lax
from jax.experimental import pallas as pl
from jax.experimental.pallas import tpu as pltpu
from jax.sharding import PartitionSpec as P

ITERS = 2
BF16 = jnp.bfloat16
F32 = jnp.float32
VMEM = pl.BlockSpec(memory_space=pltpu.VMEM)
SMEM = pl.BlockSpec(memory_space=pltpu.SMEM)
ANY = pl.BlockSpec(memory_space=pl.ANY)
HBM = pl.BlockSpec(memory_space=pltpu.HBM)


def params(mib):
    return pltpu.CompilerParams(vmem_limit_bytes=mib * 2**20)


def dot(left, right, dims):
    return lax.dot_general(left, right, (dims, ((), ())), preferred_element_type=F32)


def split(value):
    high = value.astype(BF16)
    return high, (value - high.astype(F32)).astype(BF16)


def square(value):
    high, rest = split(value)
    return dot(
        jnp.concatenate([high, high, rest, rest], axis=1),
        jnp.concatenate([high, rest, high, rest], axis=1),
        ((1,), (1,)),
    )


def cost(flops, size):
    return pl.CostEstimate(flops=flops, bytes_accessed=size, transcendentals=0)


def prepare_kernel(
    aux_ref, occ_ref, used_ref, energy_ref, first_ref, second_ref, ints_ref,
    first_out, second_out, ints_out, factor_ref, sems,
):
    count, width, _ = factor_ref.shape
    half = lax.rem(aux_ref[0], 2)
    rows = pl.ds(half * count, count)
    copies = [
        pltpu.make_async_copy(first_ref.at[rows], first_out, sems.at[0]),
        pltpu.make_async_copy(second_ref.at[rows], second_out, sems.at[1]),
        pltpu.make_async_copy(ints_ref, ints_out, sems.at[2]),
    ]
    for copy in copies:
        copy.start()
    shape = (width, width)
    along = lax.broadcasted_iota(jnp.int32, shape, 1)
    down = lax.broadcasted_iota(jnp.int32, shape, 0)
    for p in range(count):
        row = half * count + p
        energy = jnp.broadcast_to(energy_ref[pl.ds(row, 1)], shape)
        denom = energy.T + energy - occ_ref[0, row] - occ_ref[1, row]
        inside = (along < used_ref[row]) & (down < used_ref[row])
        factor_ref[p] = jnp.where(inside, -1.0 / denom, 0.0)
    for copy in copies:
        copy.wait()


def prepare(aux, occupied, used, energy, first, second, ints):
    pair_dev, width, _ = first.shape
    shape = (pair_dev // 2, width, width)
    return pl.pallas_call(
        prepare_kernel,
        out_shape=(
            jax.ShapeDtypeStruct(shape, BF16),
            jax.ShapeDtypeStruct(shape, BF16),
            jax.ShapeDtypeStruct(ints.shape, BF16),
            jax.ShapeDtypeStruct(shape, F32),
        ),
        in_specs=[SMEM] * 3 + [VMEM] + [HBM] * 3,
        out_specs=(VMEM,) * 4,
        scratch_shapes=[pltpu.SemaphoreType.DMA((3,))],
        compiler_params=params(8),
        cost_estimate=cost(0, 8 * pair_dev * width * width),
        name="prepare",
    )(aux, occupied, used, energy, first, second, ints)


PRODUCT, FIRST, SECOND = 4, 5, 6


def index_kernel(
    rounds, here_ref, aux_ref, orbitals_ref, near_ref, couple_ref, index_ref, weight_ref
):
    nbr_count, pair_dev = couple_ref.shape
    count = pair_dev // 2
    here = here_ref[0]
    half = lax.rem(aux_ref[0], 2)
    across = lax.rem(aux_ref[0] // 2, 2)
    near_block = -1
    for start, end in rounds[0] if rounds else ():
        near_block = jnp.where(here == end, start, near_block)

    def place(p, n):
        if not rounds:
            return p * nbr_count + n
        wanted = near_ref[n, here * pair_dev + half * count + p]
        owner = wanted // pair_dev
        local = wanted - owner * pair_dev
        side = local // count
        local = local - side * count
        other = jnp.where(side == half, 0, 1)
        quarter = local // (count // 2)
        halved = (
            4 * count
            + jnp.where(quarter == across, 0, count)
            + other * (count // 2)
            + local
            - quarter * (count // 2)
        )
        spot = other * count + local + jnp.where(owner == here, 0, 2 * count)
        return jnp.where(owner == near_block, halved, spot)

    lane = lax.broadcasted_iota(jnp.int32, (1, index_ref.shape[1]), 1)
    for p in range(count):
        row = half * count + p
        first = orbitals_ref[0, row] - here * 2
        second = orbitals_ref[1, row] - here * 2 + 2
        values = {PRODUCT: first * 6 + second, FIRST: first, SECOND: second}
        values.update((n, place(p, n)) for n in range(nbr_count))
        index_ref[p : p + 1] = sum(jnp.where(lane == at, v, 0) for at, v in values.items())
        weight_ref[p : p + 1] = sum(
            jnp.where(lane == n, couple_ref[n, row], 0.0) for n in range(nbr_count)
        )


def indices(rounds, here, aux, orbitals, near, couple):
    nbr_count, pair_dev = couple.shape
    assert nbr_count <= PRODUCT
    return pl.pallas_call(
        functools.partial(index_kernel, rounds),
        out_shape=(
            jax.ShapeDtypeStruct((pair_dev // 2, 128), jnp.int32),
            jax.ShapeDtypeStruct((pair_dev // 2, 128), F32),
        ),
        in_specs=[SMEM] * 5,
        out_specs=(VMEM, VMEM),
        compiler_params=params(4),
        cost_estimate=cost(10**6, 2**16),
        name="indices",
    )(here, aux, orbitals, near, couple)


def product_kernel(aux_ref, own_ref, near_ref, all_ref, sent_ref):
    count, _, width = own_ref.shape
    second = lax.rem(aux_ref[0], 2) == 1
    own = jnp.concatenate([own_ref[i] for i in range(count)], axis=1)
    near = jnp.concatenate([near_ref[i] for i in range(count)], axis=1)
    full = dot(jnp.where(second, near, own), jnp.where(second, own, near), ((0,), (0,)))
    at = 0
    for i in range(count):
        for j in range(count):
            block = full[i * width : (i + 1) * width, j * width : (j + 1) * width].astype(BF16)
            all_ref[at : at + width] = block
            sent_ref[at : at + width] = block
            at += width
    all_ref[at:] = dot(own_ref[0], own_ref[1], ((0,), (0,))).astype(BF16)


def products(aux, ints, near):
    count, depth, width = ints.shape
    rows = count * count * width
    return pl.pallas_call(
        product_kernel,
        out_shape=(
            jax.ShapeDtypeStruct((rows + width, width), BF16),
            jax.ShapeDtypeStruct((rows, width), BF16),
        ),
        in_specs=[SMEM] + [VMEM] * 2,
        out_specs=(VMEM, VMEM),
        compiler_params=params(12),
        cost_estimate=cost(10 * depth * width * width, 8 * depth * width),
        name="products",
    )(aux, ints, near)


def own_part(aux_ref, low_ref, part_ref):
    count = part_ref.shape[0]
    part_ref[...] = low_ref[pl.ds(lax.rem(aux_ref[0] // 2, 2) * count, count)]


def exchange_kernel(aux_ref, index_ref, *refs):
    mine_refs, other_refs, refs = refs[:4], refs[4:8], refs[8:]
    first_ref, second_ref, factor_ref, exch_ref, low_ref, part_ref, table = refs
    count, width, _ = exch_ref.shape
    second = lax.rem(aux_ref[0], 2) == 1
    rows = 4 * width

    def summed(refs):
        whole, cross, near, near_cross = (ref[...].astype(F32) for ref in refs)
        both = whole + cross
        return both[:rows] + (near + near_cross), both[rows:]

    mine, inner = summed(mine_refs)
    others, inner_other = summed(other_refs)
    for i in range(2):
        for j in range(2):
            at = (2 * i + j) * width
            one = mine[at : at + width]
            two = others[at : at + width]
            table[i * 6 + 4 + j] = jnp.where(second, two, one)
            table[j * 6 + i] = jnp.where(second, one, two).T
    inner = inner + inner_other
    table[3] = inner
    table[6 + 2] = inner.T
    for p in range(count):
        right = second_ref[p]
        left = first_ref[p]
        high, rest = split(table[index_ref[p, PRODUCT]])
        inner = dot(
            jnp.concatenate([high, rest], axis=1),
            jnp.concatenate([right, right], axis=0),
            ((1,), (0,)),
        )
        high, rest = split(inner)
        exch = dot(
            jnp.concatenate([left, left], axis=0),
            jnp.concatenate([high, rest], axis=0),
            ((0,), (0,)),
        )
        exch_ref[p] = exch
        low_ref[p] = (factor_ref[p] * exch).astype(BF16)
    own_part(aux_ref, low_ref, part_ref)


def exchange(aux, index, sums, first, second, factor):
    shape = first.shape
    count, width, _ = shape
    return pl.pallas_call(
        exchange_kernel,
        out_shape=(
            jax.ShapeDtypeStruct(shape, F32),
            jax.ShapeDtypeStruct(shape, BF16),
            jax.ShapeDtypeStruct((count // 2, width, width), BF16),
        ),
        in_specs=[SMEM] + [VMEM] * (len(sums) + 4),
        out_specs=(VMEM,) * 3,
        scratch_shapes=[pltpu.VMEM((12, width, width), F32)],
        compiler_params=params(12),
        cost_estimate=cost(8 * count * width**3, 20 * count * width * width),
        name="exchange",
    )(aux, index, *sums, first, second, factor)


def sweep_kernel(last, pieces, here_ref, aux_ref, index_ref, weight_ref, *refs):
    parts = refs[:pieces]
    over_ref, exch_ref, factor_ref, second_ref = refs[pieces : pieces + 4]
    if last:
        amps_ref, terms_ref, one_ref, two_ref, all_terms, table = refs[pieces + 4 :]
    else:
        low_ref, part_ref, table = refs[pieces + 4 :]
    count, width, _ = exch_ref.shape
    nbr_count = over_ref.shape[1]
    here = here_ref[0]
    half = lax.rem(aux_ref[0], 2)
    at = 0
    for part in parts:
        table[at : at + part.shape[0]] = part[...]
        at += part.shape[0]
    done = []
    for p in range(count):
        row = half * count + p
        halves = []
        for n in range(nbr_count):
            moved = dot(over_ref[row, n], table[index_ref[p, n]], ((1,), (0,)))
            halves.append((weight_ref[p, n] * moved).astype(BF16))
        coupled = dot(
            jnp.concatenate(halves, axis=1),
            jnp.concatenate([over_ref[row, n] for n in range(nbr_count)], axis=1),
            ((1,), (1,)),
        )
        amps = factor_ref[p] * (exch_ref[p] - coupled)
        if last:
            amps_ref[p] = amps
            done.append(amps)
        else:
            low_ref[p] = amps.astype(BF16)
    if not last:
        own_part(aux_ref, low_ref, part_ref)
    else:
        terms = []
        for p in range(count):
            right = second_ref[p]
            high, rest = split(done[p])
            moved = dot(
                jnp.concatenate([right, right], axis=1),
                jnp.concatenate([high, rest], axis=1),
                ((1,), (1,)),
            )
            terms.append(square(moved))
        all_terms[...] = jnp.zeros_like(all_terms)
        for p in range(count):
            spot = index_ref[p, SECOND]
            all_terms[spot] += terms[p]
        terms_ref[...] = all_terms[2:4]
        below = lax.rem(here, 2) * 4
        one_ref[...] = all_terms[pl.ds(4 - below, 2)].astype(BF16)
        two_ref[...] = all_terms[pl.ds(below, 2)].astype(BF16)


def sweep(last, here, aux, index, weight, parts, over, exch, factor, second):
    count, width, _ = exch.shape
    rows = sum(part.shape[0] for part in parts)
    if last:
        out_shape = (
            jax.ShapeDtypeStruct(exch.shape, F32),
            jax.ShapeDtypeStruct((2, width, width), F32),
            jax.ShapeDtypeStruct((2, width, width), BF16),
            jax.ShapeDtypeStruct((2, width, width), BF16),
        )
        out_specs = (VMEM,) * 4
        scratch = [pltpu.VMEM((6, width, width), F32)]
    else:
        out_shape = (
            jax.ShapeDtypeStruct(exch.shape, BF16),
            jax.ShapeDtypeStruct((count // 2, width, width), BF16),
        )
        out_specs = (VMEM, VMEM)
        scratch = []
    return pl.pallas_call(
        functools.partial(sweep_kernel, last, len(parts)),
        out_shape=out_shape,
        in_specs=[SMEM] * 2 + [VMEM] * (len(parts) + 6),
        out_specs=out_specs,
        scratch_shapes=scratch + [pltpu.VMEM((rows, width, width), BF16)],
        compiler_params=params(16),
        cost_estimate=cost(16 * count * width**3, (rows + 16 * count) * width * width),
        name="last_sweep" if last else "sweep",
    )(here, aux, index, weight, *parts, over, exch, factor, second)


def token_kernel(piece_ref, out_ref):
    out_ref[...] = piece_ref[0, :16]


def token(piece):
    return pl.pallas_call(
        token_kernel,
        out_shape=jax.ShapeDtypeStruct((16, piece.shape[-1]), BF16),
        in_specs=[VMEM],
        out_specs=VMEM,
        compiler_params=params(4),
        cost_estimate=cost(5 * 10**9, 2**20),
        name="token",
    )(piece)


def join_kernel(left_ref, right_ref, token_ref, piece_ref, out_ref):
    del token_ref, piece_ref
    out_ref[...] = left_ref[...] + right_ref[...]


def joined(left, right, token, piece):
    return pl.pallas_call(
        join_kernel,
        out_shape=jax.ShapeDtypeStruct(left.shape, BF16),
        in_specs=[VMEM] * 3 + [ANY],
        out_specs=VMEM,
        compiler_params=params(4),
        cost_estimate=cost(left.size, 6 * left.size),
        name="joined",
    )(left, right, token, piece)


def first_kernel(
    aux_ref, index_ref, amps_ref, others_ref, first_ref, whole_ref, terms_ref, sems
):
    count = amps_ref.shape[0]
    half = lax.rem(aux_ref[0], 2)
    copies = [
        pltpu.make_async_copy(amps_ref, whole_ref.at[pl.ds(half * count, count)], sems.at[0]),
        pltpu.make_async_copy(others_ref, whole_ref.at[pl.ds((1 - half) * count, count)], sems.at[1]),
    ]
    for copy in copies:
        copy.start()
    terms = []
    for p in range(count):
        high, rest = split(amps_ref[p])
        left = first_ref[p]
        moved = dot(
            jnp.concatenate([left, left], axis=1),
            jnp.concatenate([high, rest], axis=0),
            ((1,), (0,)),
        )
        terms.append(square(moved))
    terms_ref[...] = jnp.zeros_like(terms_ref)
    for p in range(count):
        spot = index_ref[p, FIRST]
        terms_ref[spot] += terms[p]
    for copy in copies:
        copy.wait()


def first_terms(aux, index, amps, others, first):
    count, width, _ = amps.shape
    return pl.pallas_call(
        first_kernel,
        out_shape=(
            jax.ShapeDtypeStruct((2 * count, width, width), F32),
            jax.ShapeDtypeStruct((2, width, width), F32),
        ),
        in_specs=[SMEM] + [VMEM] * 4,
        out_specs=(ANY, VMEM),
        scratch_shapes=[pltpu.SemaphoreType.DMA((2,))],
        compiler_params=params(12),
        cost_estimate=cost(12 * count * width**3, 16 * count * width * width),
        name="first_terms",
    )(aux, index, amps, others, first)


def window_rounds(groups):
    edges = []
    for block in range(groups):
        start = min(max(block - 1, 0), groups - 3)
        edges += [(source, block) for source in range(start, start + 3) if source != block]
    edges.sort(key=lambda edge: (-abs(edge[0] - edge[1]), edge))
    first = []
    for source, block in edges:
        if all(source != s and block != d for s, d in first):
            first.append((source, block))
    rest = [edge for edge in edges if edge not in first]
    both = [edge for edge in rest if edge[::-1] in rest]
    rounds = [first, both, [edge for edge in rest if edge not in both]]
    assert len(rounds[0]) == groups
    return rounds


def same_owner_rank(owners):
    count = owners.shape[-1]
    places = jnp.arange(count)
    earlier = places[:, None] > places[None, :]
    same = owners[..., :, None] == owners[..., None, :]
    return jnp.sum(same & earlier, axis=-1)


def shards(
    ints,
    proj_first,
    proj_second,
    intersections,
    couple,
    virt_energy,
    occ_energy,
    pno_count,
    pair_orbitals,
    neighbours,
):
    groups = lax.axis_size("pair")
    here = lax.axis_index("pair")
    aux_count = lax.axis_size("aux")
    aux = lax.axis_index("aux")
    half = aux % 2
    occ_dev, _, width = ints.shape
    pair_dev = proj_first.shape[0]
    nbr_count = couple.shape[1]
    wanted = pair_dev * nbr_count
    cap = 2 * wanted // groups
    count = pair_dev // 2
    partners = [
        [(i, j) for i in range(groups) for j in (i + 1 - 2 * ((i + r) % 2),) if 0 <= j < groups]
        for r in range(2)
    ]

    def swap(value, step=1):
        return lax.ppermute(value, "aux", [(i, i ^ step) for i in range(aux_count)])

    ints, here_s, aux_s = lax.optimization_barrier((ints, here.reshape(1), aux.reshape(1)))

    def both(one, two):
        return [lax.ppermute(one, "pair", partners[0]), lax.ppermute(two, "pair", partners[1])]

    def exchanged(one, two, rounds):
        return [
            lax.ppermute(
                value,
                ("pair", "aux"),
                [
                    (i * aux_count + a, j * aux_count + a)
                    for a in range(aux_count)
                    for i, j in rounds[(r + a) % 2]
                ],
            )
            for r, value in enumerate((one, two))
        ]

    def joint(rounds):
        return [
            (i * aux_count + a, j * aux_count + (a ^ turn))
            for a in range(aux_count)
            for i, j, turn in rounds[a % 2]
        ]

    near = lax.ppermute(
        ints,
        ("pair", "aux"),
        joint(
            [
                [(i + 1, i, 0) for i in range(groups - 1)],
                [(i, i + 1, 0) for i in range(groups - 1)],
            ]
        ),
    )
    first, second, ints, factor = prepare(
        aux_s, occ_energy.T, pno_count, virt_energy, proj_first, proj_second, ints
    )
    near, first, second, ints, factor = lax.optimization_barrier(
        (near, first, second, ints, factor)
    )

    assert aux_count == 4
    if cap < pair_dev or groups // 4 != 1:
        rounds = None
        requests = neighbours.reshape(groups, wanted)
        owners = requests // pair_dev
        ranks = same_owner_rank(owners)
        at_home = owners == here
        pick = at_home[:, None, :] & (ranks[:, None, :] == jnp.arange(cap)[None, :, None])
        local = requests % pair_dev
        select = jnp.any(
            pick[..., None]
            & (local[:, None, :, None] == jnp.arange(pair_dev)[None, None, None, :]),
            axis=2,
        )
        select = select.astype(BF16).reshape(groups * cap, pair_dev)
        own_requests = lax.dynamic_slice_in_dim(requests, here, 1, 0)[0]
        own_ranks = lax.dynamic_slice_in_dim(ranks, here, 1, 0)[0]
        row_index = lax.dynamic_slice_in_dim(
            own_requests // pair_dev * cap + own_ranks,
            half * count * nbr_count,
            count * nbr_count,
            0,
        )
    else:
        rounds = window_rounds(groups)
    index, weight = indices(rounds, here_s, aux_s, pair_orbitals.T, neighbours.T, couple.T)

    everything, sent = products(aux_s, ints, near)

    def over_z(turn):
        return lax.ppermute(
            sent,
            ("pair", "aux"),
            joint(
                [
                    [(i, i + 1, turn) for i in range(groups - 1)],
                    [(i + 1, i, turn) for i in range(groups - 1)],
                ]
            ),
        )

    sums = [everything, swap(everything, 2), over_z(1), over_z(3)]
    exch, low, part = exchange(
        aux_s, index, sums + [swap(value) for value in sums], first, second, factor
    )

    def gathered(low, part):
        if rounds is None:
            others = swap(low)
            flat = jnp.where(
                half == 0, jnp.concatenate([low, others]), jnp.concatenate([others, low])
            ).reshape(pair_dev, width * width)
            outgoing = jnp.dot(select, flat, preferred_element_type=F32).astype(BF16)
            outgoing = outgoing.reshape(groups, cap, width, width)
            received = lax.all_to_all(outgoing, "pair", split_axis=0, concat_axis=0, tiled=True)
            return [received.reshape(groups * cap, width, width)[row_index]]
        one = lax.ppermute(part, "pair", rounds[0])
        one_other = swap(one)
        cross = swap(one, 2)
        two = joined(*exchanged(low, low, rounds[1:]), token(one), one_other)
        return [low, swap(low), two, swap(two), one, one_other, cross, swap(cross)]

    for it in range(ITERS):
        out = sweep(
            it == ITERS - 1,
            here_s,
            aux_s,
            index,
            weight,
            gathered(low, part),
            intersections,
            exch,
            factor,
            second,
        )
        if it < ITERS - 1:
            low, part = out
    amps, terms, *sent = out

    near_one, near_two = both(*sent)
    whole, inner = first_terms(aux_s, index, amps, swap(amps), first)
    density = inner + terms + near_one.astype(F32) + near_two.astype(F32)
    density = (density + swap(density)) / width
    return (whole, density)


def solution(mesh):
    return jax.shard_map(
        shards,
        mesh=mesh,
        in_specs=(
            P(("mol", "pair"), "aux", None),
            P(("mol", "pair"), None, None),
            P(("mol", "pair"), None, None),
            P(("mol", "pair"), None, None, None),
            P(("mol", "pair"), None),
            P(("mol", "pair"), None),
            P(("mol", "pair"), None),
            P(("mol", "pair")),
            P(("mol", "pair"), None),
            P("mol", None),
        ),
        out_specs=(P(("mol", "pair"), None, None), P(("mol", "pair"), None, None)),
        check_vma=False,
    )
```

```python
import functools

import jax
import jax.numpy as jnp
from jax import lax
from jax.experimental import pallas as pl
from jax.experimental.pallas import tpu as pltpu
from jax.sharding import PartitionSpec as P

ITERS = 2
BF16 = jnp.bfloat16
F32 = jnp.float32
VMEM = pl.BlockSpec(memory_space=pltpu.VMEM)
SMEM = pl.BlockSpec(memory_space=pltpu.SMEM)
ANY = pl.BlockSpec(memory_space=pl.ANY)
HBM = pl.BlockSpec(memory_space=pltpu.HBM)


def params(mib):
    return pltpu.CompilerParams(vmem_limit_bytes=mib * 2**20)


def dot(left, right, dims):
    return lax.dot_general(left, right, (dims, ((), ())), preferred_element_type=F32)


def split(value):
    high = value.astype(BF16)
    return high, (value - high.astype(F32)).astype(BF16)


def square(value):
    high, rest = split(value)
    return dot(
        jnp.concatenate([high, high, rest, rest], axis=1),
        jnp.concatenate([high, rest, high, rest], axis=1),
        ((1,), (1,)),
    )


def cost(flops, size):
    return pl.CostEstimate(flops=flops, bytes_accessed=size, transcendentals=0)


def prepare_kernel(
    aux_ref, occ_ref, used_ref, energy_ref, first_ref, second_ref, ints_ref,
    first_out, second_out, ints_out, factor_ref, sems,
):
    count, width, _ = factor_ref.shape
    half = lax.rem(aux_ref[0], 2)
    rows = pl.ds(half * count, count)
    copies = [
        pltpu.make_async_copy(first_ref.at[rows], first_out, sems.at[0]),
        pltpu.make_async_copy(second_ref.at[rows], second_out, sems.at[1]),
        pltpu.make_async_copy(ints_ref, ints_out, sems.at[2]),
    ]
    for copy in copies:
        copy.start()
    shape = (width, width)
    along = lax.broadcasted_iota(jnp.int32, shape, 1)
    down = lax.broadcasted_iota(jnp.int32, shape, 0)
    for p in range(count):
        row = half * count + p
        energy = jnp.broadcast_to(energy_ref[pl.ds(row, 1)], shape)
        denom = energy.T + energy - occ_ref[0, row] - occ_ref[1, row]
        inside = (along < used_ref[row]) & (down < used_ref[row])
        factor_ref[p] = jnp.where(inside, -1.0 / denom, 0.0)
    for copy in copies:
        copy.wait()


def prepare(aux, occupied, used, energy, first, second, ints):
    pair_dev, width, _ = first.shape
    shape = (pair_dev // 2, width, width)
    return pl.pallas_call(
        prepare_kernel,
        out_shape=(
            jax.ShapeDtypeStruct(shape, BF16),
            jax.ShapeDtypeStruct(shape, BF16),
            jax.ShapeDtypeStruct(ints.shape, BF16),
            jax.ShapeDtypeStruct(shape, F32),
        ),
        in_specs=[SMEM] * 3 + [VMEM] + [HBM] * 3,
        out_specs=(VMEM,) * 4,
        scratch_shapes=[pltpu.SemaphoreType.DMA((3,))],
        compiler_params=params(8),
        cost_estimate=cost(0, 8 * pair_dev * width * width),
        name="prepare",
    )(aux, occupied, used, energy, first, second, ints)


PRODUCT, FIRST, SECOND = 4, 5, 6


def index_kernel(
    rounds, here_ref, aux_ref, orbitals_ref, near_ref, couple_ref, index_ref, weight_ref
):
    nbr_count, pair_dev = couple_ref.shape
    count = pair_dev // 2
    here = here_ref[0]
    half = lax.rem(aux_ref[0], 2)
    across = lax.rem(aux_ref[0] // 2, 2)
    near_block = -1
    for start, end in rounds[0] if rounds else ():
        near_block = jnp.where(here == end, start, near_block)

    def place(p, n):
        if not rounds:
            return p * nbr_count + n
        wanted = near_ref[n, here * pair_dev + half * count + p]
        owner = wanted // pair_dev
        local = wanted - owner * pair_dev
        side = local // count
        local = local - side * count
        other = jnp.where(side == half, 0, 1)
        quarter = local // (count // 2)
        halved = (
            4 * count
            + jnp.where(quarter == across, 0, count)
            + other * (count // 2)
            + local
            - quarter * (count // 2)
        )
        spot = other * count + local + jnp.where(owner == here, 0, 2 * count)
        return jnp.where(owner == near_block, halved, spot)

    lane = lax.broadcasted_iota(jnp.int32, (1, index_ref.shape[1]), 1)
    for p in range(count):
        row = half * count + p
        first = orbitals_ref[0, row] - here * 2
        second = orbitals_ref[1, row] - here * 2 + 2
        values = {PRODUCT: first * 6 + second, FIRST: first, SECOND: second}
        values.update((n, place(p, n)) for n in range(nbr_count))
        index_ref[p : p + 1] = sum(jnp.where(lane == at, v, 0) for at, v in values.items())
        weight_ref[p : p + 1] = sum(
            jnp.where(lane == n, couple_ref[n, row], 0.0) for n in range(nbr_count)
        )


def indices(rounds, here, aux, orbitals, near, couple):
    nbr_count, pair_dev = couple.shape
    assert nbr_count <= PRODUCT
    return pl.pallas_call(
        functools.partial(index_kernel, rounds),
        out_shape=(
            jax.ShapeDtypeStruct((pair_dev // 2, 128), jnp.int32),
            jax.ShapeDtypeStruct((pair_dev // 2, 128), F32),
        ),
        in_specs=[SMEM] * 5,
        out_specs=(VMEM, VMEM),
        compiler_params=params(4),
        cost_estimate=cost(10**6, 2**16),
        name="indices",
    )(here, aux, orbitals, near, couple)


def product_kernel(aux_ref, own_ref, near_ref, all_ref, sent_ref):
    count, _, width = own_ref.shape
    second = lax.rem(aux_ref[0], 2) == 1
    own = jnp.concatenate([own_ref[i] for i in range(count)], axis=1)
    near = jnp.concatenate([near_ref[i] for i in range(count)], axis=1)
    full = dot(jnp.where(second, near, own), jnp.where(second, own, near), ((0,), (0,)))
    at = 0
    for i in range(count):
        for j in range(count):
            block = full[i * width : (i + 1) * width, j * width : (j + 1) * width].astype(BF16)
            all_ref[at : at + width] = block
            sent_ref[at : at + width] = block
            at += width
    all_ref[at:] = dot(own_ref[0], own_ref[1], ((0,), (0,))).astype(BF16)


def products(aux, ints, near):
    count, depth, width = ints.shape
    rows = count * count * width
    return pl.pallas_call(
        product_kernel,
        out_shape=(
            jax.ShapeDtypeStruct((rows + width, width), BF16),
            jax.ShapeDtypeStruct((rows, width), BF16),
        ),
        in_specs=[SMEM] + [VMEM] * 2,
        out_specs=(VMEM, VMEM),
        compiler_params=params(12),
        cost_estimate=cost(10 * depth * width * width, 8 * depth * width),
        name="products",
    )(aux, ints, near)


def own_part(aux_ref, low_ref, part_ref):
    count = part_ref.shape[0]
    part_ref[...] = low_ref[pl.ds(lax.rem(aux_ref[0] // 2, 2) * count, count)]


def exchange_kernel(aux_ref, index_ref, *refs):
    mine_refs, other_refs, refs = refs[:4], refs[4:8], refs[8:]
    first_ref, second_ref, factor_ref, exch_ref, low_ref, part_ref, table = refs
    count, width, _ = exch_ref.shape
    second = lax.rem(aux_ref[0], 2) == 1
    rows = 4 * width

    def summed(refs):
        whole, cross, near, near_cross = (ref[...].astype(F32) for ref in refs)
        both = whole + cross
        return both[:rows] + (near + near_cross), both[rows:]

    mine, inner = summed(mine_refs)
    others, inner_other = summed(other_refs)
    for i in range(2):
        for j in range(2):
            at = (2 * i + j) * width
            one = mine[at : at + width]
            two = others[at : at + width]
            table[i * 6 + 4 + j] = jnp.where(second, two, one)
            table[j * 6 + i] = jnp.where(second, one, two).T
    inner = inner + inner_other
    table[3] = inner
    table[6 + 2] = inner.T
    for p in range(count):
        right = second_ref[p]
        left = first_ref[p]
        high, rest = split(table[index_ref[p, PRODUCT]])
        inner = dot(
            jnp.concatenate([high, rest], axis=1),
            jnp.concatenate([right, right], axis=0),
            ((1,), (0,)),
        )
        high, rest = split(inner)
        exch = dot(
            jnp.concatenate([left, left], axis=0),
            jnp.concatenate([high, rest], axis=0),
            ((0,), (0,)),
        )
        exch_ref[p] = exch
        low_ref[p] = (factor_ref[p] * exch).astype(BF16)
    own_part(aux_ref, low_ref, part_ref)


def exchange(aux, index, sums, first, second, factor):
    shape = first.shape
    count, width, _ = shape
    return pl.pallas_call(
        exchange_kernel,
        out_shape=(
            jax.ShapeDtypeStruct(shape, F32),
            jax.ShapeDtypeStruct(shape, BF16),
            jax.ShapeDtypeStruct((count // 2, width, width), BF16),
        ),
        in_specs=[SMEM] + [VMEM] * (len(sums) + 4),
        out_specs=(VMEM,) * 3,
        scratch_shapes=[pltpu.VMEM((12, width, width), F32)],
        compiler_params=params(12),
        cost_estimate=cost(8 * count * width**3, 20 * count * width * width),
        name="exchange",
    )(aux, index, *sums, first, second, factor)


def sweep_kernel(step, pieces, here_ref, aux_ref, index_ref, weight_ref, *refs):
    parts = refs[:pieces]
    over_ref, exch_ref, factor_ref, second_ref = refs[pieces : pieces + 4]
    last = step == "last"
    refs = refs[pieces + 4 :]
    count, width, _ = exch_ref.shape
    nbr_count = over_ref.shape[1]
    here = here_ref[0]
    half = lax.rem(aux_ref[0], 2)
    across = lax.rem(aux_ref[0] // 2, 2) * (count // 2)
    if step == "rest":
        table, part_ref = parts
        (low_ref,) = refs
        low_ref[pl.ds(across, count // 2)] = part_ref[...]
        pairs = [count // 2 - across + k for k in range(count // 2)]
    else:
        table = refs[-1]
        at = 0
        for part in parts:
            table[at : at + part.shape[0]] = part[...]
            at += part.shape[0]
        pairs = [across + k for k in range(count // 2)]
    if last:
        amps_ref, terms_ref, one_ref, two_ref, all_terms, table = refs
        pairs = range(count)
    done = []
    for k, p in enumerate(pairs):
        row = half * count + p
        halves = []
        for n in range(nbr_count):
            moved = dot(over_ref[row, n], table[index_ref[p, n]], ((1,), (0,)))
            halves.append((weight_ref[p, n] * moved).astype(BF16))
        coupled = dot(
            jnp.concatenate(halves, axis=1),
            jnp.concatenate([over_ref[row, n] for n in range(nbr_count)], axis=1),
            ((1,), (1,)),
        )
        amps = factor_ref[p] * (exch_ref[p] - coupled)
        if last:
            amps_ref[p] = amps
            done.append(amps)
        elif step == "part":
            refs[0][k] = amps.astype(BF16)
        else:
            low_ref[p] = amps.astype(BF16)
    if last:
        terms = []
        for p in range(count):
            right = second_ref[p]
            high, rest = split(done[p])
            moved = dot(
                jnp.concatenate([right, right], axis=1),
                jnp.concatenate([high, rest], axis=1),
                ((1,), (1,)),
            )
            terms.append(square(moved))
        all_terms[...] = jnp.zeros_like(all_terms)
        for p in range(count):
            spot = index_ref[p, SECOND]
            all_terms[spot] += terms[p]
        terms_ref[...] = all_terms[2:4]
        below = lax.rem(here, 2) * 4
        one_ref[...] = all_terms[pl.ds(4 - below, 2)].astype(BF16)
        two_ref[...] = all_terms[pl.ds(below, 2)].astype(BF16)


def sweep(last, here, aux, index, weight, parts, over, exch, factor, second):
    count, width, _ = exch.shape
    table = (sum(part.shape[0] for part in parts), width, width)

    def call(step, parts, out_shape, scratch):
        return pl.pallas_call(
            functools.partial(sweep_kernel, step, len(parts)),
            out_shape=out_shape,
            in_specs=[SMEM] * 2 + [VMEM] * (len(parts) + 6),
            out_specs=(VMEM,) * len(out_shape),
            scratch_shapes=scratch,
            compiler_params=params(16),
            cost_estimate=cost(16 * count * width**3, (table[0] + 16 * count) * width * width),
            name="sweep_" + step,
        )(here, aux, index, weight, *parts, over, exch, factor, second)

    if last:
        return call(
            "last",
            parts,
            (
                jax.ShapeDtypeStruct(exch.shape, F32),
                jax.ShapeDtypeStruct((2, width, width), F32),
                jax.ShapeDtypeStruct((2, width, width), BF16),
                jax.ShapeDtypeStruct((2, width, width), BF16),
            ),
            [pltpu.VMEM((6, width, width), F32), pltpu.VMEM(table, BF16)],
        )
    part, whole = call(
        "part",
        parts,
        (
            jax.ShapeDtypeStruct((count // 2, width, width), BF16),
            jax.ShapeDtypeStruct(table, BF16),
        ),
        [],
    )
    (low,) = call("rest", (whole, part), (jax.ShapeDtypeStruct(exch.shape, BF16),), [])
    return low, part


def token_kernel(piece_ref, out_ref):
    out_ref[...] = piece_ref[0, :16]


def token(piece):
    return pl.pallas_call(
        token_kernel,
        out_shape=jax.ShapeDtypeStruct((16, piece.shape[-1]), BF16),
        in_specs=[VMEM],
        out_specs=VMEM,
        compiler_params=params(4),
        cost_estimate=cost(5 * 10**9, 2**20),
        name="token",
    )(piece)


def join_kernel(left_ref, right_ref, token_ref, piece_ref, out_ref):
    del token_ref, piece_ref
    out_ref[...] = left_ref[...] + right_ref[...]


def joined(left, right, token, piece):
    return pl.pallas_call(
        join_kernel,
        out_shape=jax.ShapeDtypeStruct(left.shape, BF16),
        in_specs=[VMEM] * 3 + [ANY],
        out_specs=VMEM,
        compiler_params=params(4),
        cost_estimate=cost(left.size, 6 * left.size),
        name="joined",
    )(left, right, token, piece)


def first_kernel(
    aux_ref, index_ref, amps_ref, others_ref, first_ref, whole_ref, terms_ref, sems
):
    count = amps_ref.shape[0]
    half = lax.rem(aux_ref[0], 2)
    copies = [
        pltpu.make_async_copy(amps_ref, whole_ref.at[pl.ds(half * count, count)], sems.at[0]),
        pltpu.make_async_copy(others_ref, whole_ref.at[pl.ds((1 - half) * count, count)], sems.at[1]),
    ]
    for copy in copies:
        copy.start()
    terms = []
    for p in range(count):
        high, rest = split(amps_ref[p])
        left = first_ref[p]
        moved = dot(
            jnp.concatenate([left, left], axis=1),
            jnp.concatenate([high, rest], axis=0),
            ((1,), (0,)),
        )
        terms.append(square(moved))
    terms_ref[...] = jnp.zeros_like(terms_ref)
    for p in range(count):
        spot = index_ref[p, FIRST]
        terms_ref[spot] += terms[p]
    for copy in copies:
        copy.wait()


def first_terms(aux, index, amps, others, first):
    count, width, _ = amps.shape
    return pl.pallas_call(
        first_kernel,
        out_shape=(
            jax.ShapeDtypeStruct((2 * count, width, width), F32),
            jax.ShapeDtypeStruct((2, width, width), F32),
        ),
        in_specs=[SMEM] + [VMEM] * 4,
        out_specs=(ANY, VMEM),
        scratch_shapes=[pltpu.SemaphoreType.DMA((2,))],
        compiler_params=params(12),
        cost_estimate=cost(12 * count * width**3, 16 * count * width * width),
        name="first_terms",
    )(aux, index, amps, others, first)


def window_rounds(groups):
    edges = []
    for block in range(groups):
        start = min(max(block - 1, 0), groups - 3)
        edges += [(source, block) for source in range(start, start + 3) if source != block]
    edges.sort(key=lambda edge: (-abs(edge[0] - edge[1]), edge))
    first = []
    for source, block in edges:
        if all(source != s and block != d for s, d in first):
            first.append((source, block))
    rest = [edge for edge in edges if edge not in first]
    both = [edge for edge in rest if edge[::-1] in rest]
    rounds = [first, both, [edge for edge in rest if edge not in both]]
    assert len(rounds[0]) == groups
    return rounds


def same_owner_rank(owners):
    count = owners.shape[-1]
    places = jnp.arange(count)
    earlier = places[:, None] > places[None, :]
    same = owners[..., :, None] == owners[..., None, :]
    return jnp.sum(same & earlier, axis=-1)


def shards(
    ints,
    proj_first,
    proj_second,
    intersections,
    couple,
    virt_energy,
    occ_energy,
    pno_count,
    pair_orbitals,
    neighbours,
):
    groups = lax.axis_size("pair")
    here = lax.axis_index("pair")
    aux_count = lax.axis_size("aux")
    aux = lax.axis_index("aux")
    half = aux % 2
    occ_dev, _, width = ints.shape
    pair_dev = proj_first.shape[0]
    nbr_count = couple.shape[1]
    wanted = pair_dev * nbr_count
    cap = 2 * wanted // groups
    count = pair_dev // 2
    partners = [
        [(i, j) for i in range(groups) for j in (i + 1 - 2 * ((i + r) % 2),) if 0 <= j < groups]
        for r in range(2)
    ]

    def swap(value, step=1):
        return lax.ppermute(value, "aux", [(i, i ^ step) for i in range(aux_count)])

    ints, here_s, aux_s = lax.optimization_barrier((ints, here.reshape(1), aux.reshape(1)))

    def both(one, two):
        return [lax.ppermute(one, "pair", partners[0]), lax.ppermute(two, "pair", partners[1])]

    def exchanged(one, two, rounds):
        return [
            lax.ppermute(
                value,
                ("pair", "aux"),
                [
                    (i * aux_count + a, j * aux_count + a)
                    for a in range(aux_count)
                    for i, j in rounds[(r + a) % 2]
                ],
            )
            for r, value in enumerate((one, two))
        ]

    def joint(rounds):
        return [
            (i * aux_count + a, j * aux_count + (a ^ turn))
            for a in range(aux_count)
            for i, j, turn in rounds[a % 2]
        ]

    near = lax.ppermute(
        ints,
        ("pair", "aux"),
        joint(
            [
                [(i + 1, i, 0) for i in range(groups - 1)],
                [(i, i + 1, 0) for i in range(groups - 1)],
            ]
        ),
    )
    first, second, ints, factor = prepare(
        aux_s, occ_energy.T, pno_count, virt_energy, proj_first, proj_second, ints
    )
    near, first, second, ints, factor = lax.optimization_barrier(
        (near, first, second, ints, factor)
    )

    assert aux_count == 4
    if cap < pair_dev or groups // 4 != 1:
        rounds = None
        requests = neighbours.reshape(groups, wanted)
        owners = requests // pair_dev
        ranks = same_owner_rank(owners)
        at_home = owners == here
        pick = at_home[:, None, :] & (ranks[:, None, :] == jnp.arange(cap)[None, :, None])
        local = requests % pair_dev
        select = jnp.any(
            pick[..., None]
            & (local[:, None, :, None] == jnp.arange(pair_dev)[None, None, None, :]),
            axis=2,
        )
        select = select.astype(BF16).reshape(groups * cap, pair_dev)
        own_requests = lax.dynamic_slice_in_dim(requests, here, 1, 0)[0]
        own_ranks = lax.dynamic_slice_in_dim(ranks, here, 1, 0)[0]
        row_index = lax.dynamic_slice_in_dim(
            own_requests // pair_dev * cap + own_ranks,
            half * count * nbr_count,
            count * nbr_count,
            0,
        )
    else:
        rounds = window_rounds(groups)
    index, weight = indices(rounds, here_s, aux_s, pair_orbitals.T, neighbours.T, couple.T)

    everything, sent = products(aux_s, ints, near)

    def over_z(turn):
        return lax.ppermute(
            sent,
            ("pair", "aux"),
            joint(
                [
                    [(i, i + 1, turn) for i in range(groups - 1)],
                    [(i + 1, i, turn) for i in range(groups - 1)],
                ]
            ),
        )

    sums = [everything, swap(everything, 2), over_z(1), over_z(3)]
    exch, low, part = exchange(
        aux_s, index, sums + [swap(value) for value in sums], first, second, factor
    )

    def gathered(low, part):
        if rounds is None:
            others = swap(low)
            flat = jnp.where(
                half == 0, jnp.concatenate([low, others]), jnp.concatenate([others, low])
            ).reshape(pair_dev, width * width)
            outgoing = jnp.dot(select, flat, preferred_element_type=F32).astype(BF16)
            outgoing = outgoing.reshape(groups, cap, width, width)
            received = lax.all_to_all(outgoing, "pair", split_axis=0, concat_axis=0, tiled=True)
            return [received.reshape(groups * cap, width, width)[row_index]]
        one = lax.ppermute(part, "pair", rounds[0])
        one_other = swap(one)
        cross = swap(one, 2)
        two = joined(*exchanged(low, low, rounds[1:]), token(one), one_other)
        return [low, swap(low), two, swap(two), one, one_other, cross, swap(cross)]

    for it in range(ITERS):
        out = sweep(
            it == ITERS - 1,
            here_s,
            aux_s,
            index,
            weight,
            gathered(low, part),
            intersections,
            exch,
            factor,
            second,
        )
        if it < ITERS - 1:
            low, part = out
    amps, terms, *sent = out

    near_one, near_two = both(*sent)
    whole, inner = first_terms(aux_s, index, amps, swap(amps), first)
    density = inner + terms + near_one.astype(F32) + near_two.astype(F32)
    density = (density + swap(density)) / width
    return (whole, density)


def solution(mesh):
    return jax.shard_map(
        shards,
        mesh=mesh,
        in_specs=(
            P(("mol", "pair"), "aux", None),
            P(("mol", "pair"), None, None),
            P(("mol", "pair"), None, None),
            P(("mol", "pair"), None, None, None),
            P(("mol", "pair"), None),
            P(("mol", "pair"), None),
            P(("mol", "pair"), None),
            P(("mol", "pair")),
            P(("mol", "pair"), None),
            P("mol", None),
        ),
        out_specs=(P(("mol", "pair"), None, None), P(("mol", "pair"), None, None)),
        check_vma=False,
    )
```

```python
import functools

import jax
import jax.numpy as jnp
from jax import lax
from jax.experimental import pallas as pl
from jax.experimental.pallas import tpu as pltpu
from jax.sharding import PartitionSpec as P

ITERS = 2
BF16 = jnp.bfloat16
F32 = jnp.float32
VMEM = pl.BlockSpec(memory_space=pltpu.VMEM)
SMEM = pl.BlockSpec(memory_space=pltpu.SMEM)
ANY = pl.BlockSpec(memory_space=pl.ANY)
HBM = pl.BlockSpec(memory_space=pltpu.HBM)


def params(mib):
    return pltpu.CompilerParams(vmem_limit_bytes=mib * 2**20)


def dot(left, right, dims):
    return lax.dot_general(left, right, (dims, ((), ())), preferred_element_type=F32)


def split(value):
    high = value.astype(BF16)
    return high, (value - high.astype(F32)).astype(BF16)


def square(value):
    high, rest = split(value)
    return dot(
        jnp.concatenate([high, high, rest, rest], axis=1),
        jnp.concatenate([high, rest, high, rest], axis=1),
        ((1,), (1,)),
    )


def cost(flops, size):
    return pl.CostEstimate(flops=flops, bytes_accessed=size, transcendentals=0)


def prepare_kernel(
    aux_ref, occ_ref, used_ref, energy_ref, first_ref, second_ref, ints_ref,
    first_out, second_out, ints_out, factor_ref, sems,
):
    count, width, _ = factor_ref.shape
    half = lax.rem(aux_ref[0], 2)
    rows = pl.ds(half * count, count)
    copies = [
        pltpu.make_async_copy(first_ref.at[rows], first_out, sems.at[0]),
        pltpu.make_async_copy(second_ref.at[rows], second_out, sems.at[1]),
        pltpu.make_async_copy(ints_ref, ints_out, sems.at[2]),
    ]
    for copy in copies:
        copy.start()
    shape = (width, width)
    along = lax.broadcasted_iota(jnp.int32, shape, 1)
    down = lax.broadcasted_iota(jnp.int32, shape, 0)
    for p in range(count):
        row = half * count + p
        energy = jnp.broadcast_to(energy_ref[pl.ds(row, 1)], shape)
        denom = energy.T + energy - occ_ref[0, row] - occ_ref[1, row]
        inside = (along < used_ref[row]) & (down < used_ref[row])
        factor_ref[p] = jnp.where(inside, -1.0 / denom, 0.0)
    for copy in copies:
        copy.wait()


def prepare(aux, occupied, used, energy, first, second, ints):
    pair_dev, width, _ = first.shape
    shape = (pair_dev // 2, width, width)
    return pl.pallas_call(
        prepare_kernel,
        out_shape=(
            jax.ShapeDtypeStruct(shape, BF16),
            jax.ShapeDtypeStruct(shape, BF16),
            jax.ShapeDtypeStruct(ints.shape, BF16),
            jax.ShapeDtypeStruct(shape, F32),
        ),
        in_specs=[SMEM] * 3 + [VMEM] + [HBM] * 3,
        out_specs=(VMEM,) * 4,
        scratch_shapes=[pltpu.SemaphoreType.DMA((3,))],
        compiler_params=params(8),
        cost_estimate=cost(0, 8 * pair_dev * width * width),
        name="prepare",
    )(aux, occupied, used, energy, first, second, ints)


PRODUCT, FIRST, SECOND = 4, 5, 6


def index_kernel(
    rounds, here_ref, aux_ref, orbitals_ref, near_ref, couple_ref, index_ref, weight_ref
):
    nbr_count, pair_dev = couple_ref.shape
    count = pair_dev // 2
    here = here_ref[0]
    half = lax.rem(aux_ref[0], 2)
    across = lax.rem(aux_ref[0] // 2, 2)
    near_block = -1
    for start, end in rounds[0] if rounds else ():
        near_block = jnp.where(here == end, start, near_block)

    def place(p, n):
        if not rounds:
            return p * nbr_count + n
        wanted = near_ref[n, here * pair_dev + half * count + p]
        owner = wanted // pair_dev
        local = wanted - owner * pair_dev
        side = local // count
        local = local - side * count
        other = jnp.where(side == half, 0, 1)
        quarter = local // (count // 2)
        halved = (
            4 * count
            + jnp.where(quarter == across, 0, count)
            + other * (count // 2)
            + local
            - quarter * (count // 2)
        )
        spot = other * count + local + jnp.where(owner == here, 0, 2 * count)
        return jnp.where(owner == near_block, halved, spot)

    lane = lax.broadcasted_iota(jnp.int32, (1, index_ref.shape[1]), 1)
    for p in range(count):
        row = half * count + p
        first = orbitals_ref[0, row] - here * 2
        second = orbitals_ref[1, row] - here * 2 + 2
        values = {PRODUCT: first * 6 + second, FIRST: first, SECOND: second}
        values.update((n, place(p, n)) for n in range(nbr_count))
        index_ref[p : p + 1] = sum(jnp.where(lane == at, v, 0) for at, v in values.items())
        weight_ref[p : p + 1] = sum(
            jnp.where(lane == n, couple_ref[n, row], 0.0) for n in range(nbr_count)
        )


def indices(rounds, here, aux, orbitals, near, couple):
    nbr_count, pair_dev = couple.shape
    assert nbr_count <= PRODUCT
    return pl.pallas_call(
        functools.partial(index_kernel, rounds),
        out_shape=(
            jax.ShapeDtypeStruct((pair_dev // 2, 128), jnp.int32),
            jax.ShapeDtypeStruct((pair_dev // 2, 128), F32),
        ),
        in_specs=[SMEM] * 5,
        out_specs=(VMEM, VMEM),
        compiler_params=params(4),
        cost_estimate=cost(10**6, 2**16),
        name="indices",
    )(here, aux, orbitals, near, couple)


def product_kernel(aux_ref, own_ref, near_ref, all_ref, sent_ref):
    count, _, width = own_ref.shape
    second = lax.rem(aux_ref[0], 2) == 1
    own = jnp.concatenate([own_ref[i] for i in range(count)], axis=1)
    near = jnp.concatenate([near_ref[i] for i in range(count)], axis=1)
    full = dot(jnp.where(second, near, own), jnp.where(second, own, near), ((0,), (0,)))
    at = 0
    for i in range(count):
        for j in range(count):
            block = full[i * width : (i + 1) * width, j * width : (j + 1) * width].astype(BF16)
            all_ref[at : at + width] = block
            sent_ref[at : at + width] = block
            at += width
    all_ref[at:] = dot(own_ref[0], own_ref[1], ((0,), (0,))).astype(BF16)


def products(aux, ints, near):
    count, depth, width = ints.shape
    rows = count * count * width
    return pl.pallas_call(
        product_kernel,
        out_shape=(
            jax.ShapeDtypeStruct((rows + width, width), BF16),
            jax.ShapeDtypeStruct((rows, width), BF16),
        ),
        in_specs=[SMEM] + [VMEM] * 2,
        out_specs=(VMEM, VMEM),
        compiler_params=params(12),
        cost_estimate=cost(10 * depth * width * width, 8 * depth * width),
        name="products",
    )(aux, ints, near)


def own_part(aux_ref, low_ref, part_ref):
    count = part_ref.shape[0]
    part_ref[...] = low_ref[pl.ds(lax.rem(aux_ref[0] // 2, 2) * count, count)]


def exchange_kernel(aux_ref, index_ref, *refs):
    mine_refs, other_refs, refs = refs[:4], refs[4:8], refs[8:]
    first_ref, second_ref, factor_ref, exch_ref, low_ref, part_ref, table = refs
    count, width, _ = exch_ref.shape
    second = lax.rem(aux_ref[0], 2) == 1
    rows = 4 * width

    def summed(refs):
        whole, cross, near, near_cross = (ref[...].astype(F32) for ref in refs)
        both = whole + cross
        return both[:rows] + (near + near_cross), both[rows:]

    mine, inner = summed(mine_refs)
    others, inner_other = summed(other_refs)
    for i in range(2):
        for j in range(2):
            at = (2 * i + j) * width
            one = mine[at : at + width]
            two = others[at : at + width]
            table[i * 6 + 4 + j] = jnp.where(second, two, one)
            table[j * 6 + i] = jnp.where(second, one, two).T
    inner = inner + inner_other
    table[3] = inner
    table[6 + 2] = inner.T
    for p in range(count):
        right = second_ref[p]
        left = first_ref[p]
        high, rest = split(table[index_ref[p, PRODUCT]])
        inner = dot(
            jnp.concatenate([high, rest], axis=1),
            jnp.concatenate([right, right], axis=0),
            ((1,), (0,)),
        )
        high, rest = split(inner)
        exch = dot(
            jnp.concatenate([left, left], axis=0),
            jnp.concatenate([high, rest], axis=0),
            ((0,), (0,)),
        )
        exch_ref[p] = exch
        low_ref[p] = (factor_ref[p] * exch).astype(BF16)
    own_part(aux_ref, low_ref, part_ref)


def exchange(aux, index, sums, first, second, factor):
    shape = first.shape
    count, width, _ = shape
    return pl.pallas_call(
        exchange_kernel,
        out_shape=(
            jax.ShapeDtypeStruct(shape, F32),
            jax.ShapeDtypeStruct(shape, BF16),
            jax.ShapeDtypeStruct((count // 2, width, width), BF16),
        ),
        in_specs=[SMEM] + [VMEM] * (len(sums) + 4),
        out_specs=(VMEM,) * 3,
        scratch_shapes=[pltpu.VMEM((12, width, width), F32)],
        compiler_params=params(12),
        cost_estimate=cost(8 * count * width**3, 20 * count * width * width),
        name="exchange",
    )(aux, index, *sums, first, second, factor)


def sweep_kernel(step, pieces, here_ref, aux_ref, index_ref, weight_ref, *refs):
    parts = refs[:pieces]
    over_ref, exch_ref, factor_ref, second_ref = refs[pieces : pieces + 4]
    last = step == "last"
    refs = refs[pieces + 4 :]
    count, width, _ = exch_ref.shape
    nbr_count = over_ref.shape[1]
    here = here_ref[0]
    half = lax.rem(aux_ref[0], 2)
    across = lax.rem(aux_ref[0] // 2, 2) * (count // 2)
    if step == "rest":
        table, part_ref = parts
        (low_ref,) = refs
        low_ref[pl.ds(across, count // 2)] = part_ref[...]
        pairs = [count // 2 - across + k for k in range(count // 2)]
    else:
        table = refs[-1]
        at = 0
        for part in parts:
            table[at : at + part.shape[0]] = part[...]
            at += part.shape[0]
        pairs = [across + k for k in range(count // 2)]
    if last:
        amps_ref, terms_ref, one_ref, two_ref, all_terms, table = refs
        pairs = range(count)
    done = []
    for k, p in enumerate(pairs):
        row = half * count + p
        halves = []
        for n in range(nbr_count):
            moved = dot(over_ref[row, n], table[index_ref[p, n]], ((1,), (0,)))
            halves.append((weight_ref[p, n] * moved).astype(BF16))
        coupled = dot(
            jnp.concatenate(halves, axis=1),
            jnp.concatenate([over_ref[row, n] for n in range(nbr_count)], axis=1),
            ((1,), (1,)),
        )
        amps = factor_ref[p] * (exch_ref[p] - coupled)
        if last:
            amps_ref[p] = amps
            done.append(amps)
        elif step == "part":
            refs[0][k] = amps.astype(BF16)
        else:
            low_ref[p] = amps.astype(BF16)
    if last:
        terms = []
        for p in range(count):
            right = second_ref[p]
            high, rest = split(done[p])
            moved = dot(
                jnp.concatenate([right, right], axis=1),
                jnp.concatenate([high, rest], axis=1),
                ((1,), (1,)),
            )
            terms.append(square(moved))
        all_terms[...] = jnp.zeros_like(all_terms)
        for p in range(count):
            spot = index_ref[p, SECOND]
            all_terms[spot] += terms[p]
        terms_ref[...] = all_terms[2:4]
        below = lax.rem(here, 2) * 4
        one_ref[...] = all_terms[pl.ds(4 - below, 2)].astype(BF16)
        two_ref[...] = all_terms[pl.ds(below, 2)].astype(BF16)


def sweep(last, here, aux, index, weight, parts, over, exch, factor, second):
    count, width, _ = exch.shape
    table = (sum(part.shape[0] for part in parts), width, width)

    def call(step, parts, out_shape, scratch):
        return pl.pallas_call(
            functools.partial(sweep_kernel, step, len(parts)),
            out_shape=out_shape,
            in_specs=[SMEM] * 2 + [VMEM] * (len(parts) + 6),
            out_specs=(VMEM,) * len(out_shape),
            scratch_shapes=scratch,
            compiler_params=params(16),
            cost_estimate=cost(16 * count * width**3, (table[0] + 16 * count) * width * width),
            name="sweep_" + step,
        )(here, aux, index, weight, *parts, over, exch, factor, second)

    if last:
        return call(
            "last",
            parts,
            (
                jax.ShapeDtypeStruct(exch.shape, F32),
                jax.ShapeDtypeStruct((2, width, width), F32),
                jax.ShapeDtypeStruct((2, width, width), BF16),
                jax.ShapeDtypeStruct((2, width, width), BF16),
            ),
            [pltpu.VMEM((6, width, width), F32), pltpu.VMEM(table, BF16)],
        )
    part, whole = call(
        "part",
        parts,
        (
            jax.ShapeDtypeStruct((count // 2, width, width), BF16),
            jax.ShapeDtypeStruct(table, BF16),
        ),
        [],
    )
    (low,) = call("rest", (whole, part), (jax.ShapeDtypeStruct(exch.shape, BF16),), [])
    return low, part


def token_kernel(piece_ref, out_ref):
    out_ref[...] = piece_ref[0, :16]


def token(piece):
    return pl.pallas_call(
        token_kernel,
        out_shape=jax.ShapeDtypeStruct((16, piece.shape[-1]), BF16),
        in_specs=[VMEM],
        out_specs=VMEM,
        compiler_params=params(4),
        cost_estimate=cost(5 * 10**9, 2**20),
        name="token",
    )(piece)


def join_kernel(left_ref, right_ref, token_ref, piece_ref, out_ref):
    del token_ref, piece_ref
    out_ref[...] = left_ref[...] + right_ref[...]


def joined(left, right, token, piece):
    return pl.pallas_call(
        join_kernel,
        out_shape=jax.ShapeDtypeStruct(left.shape, BF16),
        in_specs=[VMEM] * 3 + [ANY],
        out_specs=VMEM,
        compiler_params=params(4),
        cost_estimate=cost(left.size, 6 * left.size),
        name="joined",
    )(left, right, token, piece)


def first_kernel(
    aux_ref, index_ref, amps_ref, others_ref, first_ref, whole_ref, terms_ref, sems
):
    count = amps_ref.shape[0]
    half = lax.rem(aux_ref[0], 2)
    copies = [
        pltpu.make_async_copy(amps_ref, whole_ref.at[pl.ds(half * count, count)], sems.at[0]),
        pltpu.make_async_copy(others_ref, whole_ref.at[pl.ds((1 - half) * count, count)], sems.at[1]),
    ]
    for copy in copies:
        copy.start()
    terms = []
    for p in range(count):
        high, rest = split(amps_ref[p])
        left = first_ref[p]
        moved = dot(
            jnp.concatenate([left, left], axis=1),
            jnp.concatenate([high, rest], axis=0),
            ((1,), (0,)),
        )
        terms.append(square(moved))
    terms_ref[...] = jnp.zeros_like(terms_ref)
    for p in range(count):
        spot = index_ref[p, FIRST]
        terms_ref[spot] += terms[p]
    for copy in copies:
        copy.wait()


def first_terms(aux, index, amps, others, first):
    count, width, _ = amps.shape
    return pl.pallas_call(
        first_kernel,
        out_shape=(
            jax.ShapeDtypeStruct((2 * count, width, width), F32),
            jax.ShapeDtypeStruct((2, width, width), F32),
        ),
        in_specs=[SMEM] + [VMEM] * 4,
        out_specs=(ANY, VMEM),
        scratch_shapes=[pltpu.SemaphoreType.DMA((2,))],
        compiler_params=params(12),
        cost_estimate=cost(12 * count * width**3, 16 * count * width * width),
        name="first_terms",
    )(aux, index, amps, others, first)


def window_rounds(groups):
    edges = []
    for block in range(groups):
        start = min(max(block - 1, 0), groups - 3)
        edges += [(source, block) for source in range(start, start + 3) if source != block]
    edges.sort(key=lambda edge: (-abs(edge[0] - edge[1]), edge))
    first = []
    for source, block in edges:
        if all(source != s and block != d for s, d in first):
            first.append((source, block))
    rest = [edge for edge in edges if edge not in first]
    both = [edge for edge in rest if edge[::-1] in rest]
    rounds = [first, both, [edge for edge in rest if edge not in both]]
    assert len(rounds[0]) == groups
    return rounds


def same_owner_rank(owners):
    count = owners.shape[-1]
    places = jnp.arange(count)
    earlier = places[:, None] > places[None, :]
    same = owners[..., :, None] == owners[..., None, :]
    return jnp.sum(same & earlier, axis=-1)


def shards(
    ints,
    proj_first,
    proj_second,
    intersections,
    couple,
    virt_energy,
    occ_energy,
    pno_count,
    pair_orbitals,
    neighbours,
):
    groups = lax.axis_size("pair")
    here = lax.axis_index("pair")
    aux_count = lax.axis_size("aux")
    aux = lax.axis_index("aux")
    half = aux % 2
    occ_dev, _, width = ints.shape
    pair_dev = proj_first.shape[0]
    nbr_count = couple.shape[1]
    wanted = pair_dev * nbr_count
    cap = 2 * wanted // groups
    count = pair_dev // 2
    partners = [
        [(i, j) for i in range(groups) for j in (i + 1 - 2 * ((i + r) % 2),) if 0 <= j < groups]
        for r in range(2)
    ]

    def swap(value, step=1):
        return lax.ppermute(value, "aux", [(i, i ^ step) for i in range(aux_count)])

    ints, here_s, aux_s = lax.optimization_barrier((ints, here.reshape(1), aux.reshape(1)))

    def both(one, two):
        return [lax.ppermute(one, "pair", partners[0]), lax.ppermute(two, "pair", partners[1])]

    def exchanged(one, two, rounds):
        return [
            lax.ppermute(
                value,
                ("pair", "aux"),
                [
                    (i * aux_count + a, j * aux_count + a)
                    for a in range(aux_count)
                    for i, j in rounds[(r + a) % 2]
                ],
            )
            for r, value in enumerate((one, two))
        ]

    def joint(rounds):
        return [
            (i * aux_count + a, j * aux_count + (a ^ turn))
            for a in range(aux_count)
            for i, j, turn in rounds[a % 2]
        ]

    near = lax.ppermute(
        ints,
        ("pair", "aux"),
        joint(
            [
                [(i + 1, i, 0) for i in range(groups - 1)],
                [(i, i + 1, 0) for i in range(groups - 1)],
            ]
        ),
    )
    first, second, ints, factor = prepare(
        aux_s, occ_energy.T, pno_count, virt_energy, proj_first, proj_second, ints
    )
    near, first, second, ints, factor = lax.optimization_barrier(
        (near, first, second, ints, factor)
    )

    assert aux_count == 4
    if cap < pair_dev or groups // 4 != 1:
        rounds = None
        requests = neighbours.reshape(groups, wanted)
        owners = requests // pair_dev
        ranks = same_owner_rank(owners)
        at_home = owners == here
        pick = at_home[:, None, :] & (ranks[:, None, :] == jnp.arange(cap)[None, :, None])
        local = requests % pair_dev
        select = jnp.any(
            pick[..., None]
            & (local[:, None, :, None] == jnp.arange(pair_dev)[None, None, None, :]),
            axis=2,
        )
        select = select.astype(BF16).reshape(groups * cap, pair_dev)
        own_requests = lax.dynamic_slice_in_dim(requests, here, 1, 0)[0]
        own_ranks = lax.dynamic_slice_in_dim(ranks, here, 1, 0)[0]
        row_index = lax.dynamic_slice_in_dim(
            own_requests // pair_dev * cap + own_ranks,
            half * count * nbr_count,
            count * nbr_count,
            0,
        )
    else:
        rounds = window_rounds(groups)
    index, weight = indices(rounds, here_s, aux_s, pair_orbitals.T, neighbours.T, couple.T)

    everything, sent = products(aux_s, ints, near)

    def over_z(turn):
        return lax.ppermute(
            sent,
            ("pair", "aux"),
            joint(
                [
                    [(i, i + 1, turn) for i in range(groups - 1)],
                    [(i + 1, i, turn) for i in range(groups - 1)],
                ]
            ),
        )

    sums = [everything, swap(everything, 2), over_z(1), over_z(3)]
    exch, low, part = exchange(
        aux_s, index, sums + [swap(value) for value in sums], first, second, factor
    )

    def gathered(low, part):
        if rounds is None:
            others = swap(low)
            flat = jnp.where(
                half == 0, jnp.concatenate([low, others]), jnp.concatenate([others, low])
            ).reshape(pair_dev, width * width)
            outgoing = jnp.dot(select, flat, preferred_element_type=F32).astype(BF16)
            outgoing = outgoing.reshape(groups, cap, width, width)
            received = lax.all_to_all(outgoing, "pair", split_axis=0, concat_axis=0, tiled=True)
            return [received.reshape(groups * cap, width, width)[row_index]]
        one = lax.ppermute(part, "pair", rounds[0])
        one_other = swap(one)
        cross = swap(one, 2)
        two = joined(*exchanged(low, low, rounds[:0:-1]), token(one), one_other)
        return [low, swap(low), two, swap(two), one, one_other, cross, swap(cross)]

    for it in range(ITERS):
        out = sweep(
            it == ITERS - 1,
            here_s,
            aux_s,
            index,
            weight,
            gathered(low, part),
            intersections,
            exch,
            factor,
            second,
        )
        if it < ITERS - 1:
            low, part = out
    amps, terms, *sent = out

    near_one, near_two = both(*sent)
    whole, inner = first_terms(aux_s, index, amps, swap(amps), first)
    density = inner + terms + near_one.astype(F32) + near_two.astype(F32)
    density = (density + swap(density)) / width
    return (whole, density)


def solution(mesh):
    return jax.shard_map(
        shards,
        mesh=mesh,
        in_specs=(
            P(("mol", "pair"), "aux", None),
            P(("mol", "pair"), None, None),
            P(("mol", "pair"), None, None),
            P(("mol", "pair"), None, None, None),
            P(("mol", "pair"), None),
            P(("mol", "pair"), None),
            P(("mol", "pair"), None),
            P(("mol", "pair")),
            P(("mol", "pair"), None),
            P("mol", None),
        ),
        out_specs=(P(("mol", "pair"), None, None), P(("mol", "pair"), None, None)),
        check_vma=False,
    )
```
